32 devices in a mesh: dp: 4 (over z), seq: 4 (over y, x), mp: 2 (over core).
Axes of the slice: x: 2, y: 2, z: 4, core: 2. Of those that a mesh axis runs over, the one named last changes fastest.
Arguments:
- tokens: bfloat16 [2, 4, 2048, 768], P(None, 'dp', 'seq'), may hold values from -6 to 6
- output_cotangent: bfloat16 [2, 4, 2048, 768], P(None, 'dp', 'seq'), may hold values from -6 to 6
- document_numbers: int32 [2, 4, 2048], P(None, 'dp'), may hold values from 0 to 3, as said below
- document_adapter: int32 [2, 4, 4], P(None, 'dp'), may hold values from 0 to 7
- input_norm_gain: bfloat16 [2, 768], replicated, may hold values from 0.5 to 1.5
- gate_head_projection: bfloat16 [2, 768, 2, 1536], P(None, 'dp', None, 'mp'), may hold values from -0.21875 to 0.21875
- map_projection: bfloat16 [2, 768, 256], P(None, 'dp'), may hold values from -0.21875 to 0.21875
- step_projection: bfloat16 [2, 768, 24], P(None, 'dp', 'mp'), may hold values from -0.21875 to 0.21875
- output_projection: bfloat16 [2, 1536, 768], P(None, 'mp', 'dp'), may hold values from -0.15625 to 0.15625
- head_conv_taps: bfloat16 [2, 5, 1536], P(None, None, 'mp'), may hold values from -0.5 to 0.5
- map_conv_taps: bfloat16 [2, 5, 256], replicated, may hold values from -0.5 to 0.5
- head_settings: float32 [2, 3, 24], P(None, None, 'mp'), as said below
- gated_norm_gain: bfloat16 [2, 1536], P(None, 'mp'), may hold values from 0.5 to 1.5
- adapter_broad: float32 [2, 8, 16, 3, 1536], P(None, 'dp', None, None, 'mp'), may hold values from -0.3125 to 0.3125
- adapter_step: float32 [2, 8, 16, 24], P(None, 'dp', None, 'mp'), may hold values from -0.3125 to 0.3125
- adapter_shared: float32 [2, 8, 16, 1792], P(None, 'dp'), may hold values from -0.3125 to 0.3125
- broad_first_moment: float32 [2, 8, 16, 3, 1536], P(None, 'dp', None, None, 'mp'), may hold values from -0.0048828125 to 0.0048828125
- step_first_moment: float32 [2, 8, 16, 24], P(None, 'dp', None, 'mp'), may hold values from -0.0048828125 to 0.0048828125
- shared_first_moment: float32 [2, 8, 16, 1792], P(None, 'dp'), may hold values from -0.0048828125 to 0.0048828125
- broad_second_moment: float32 [2, 8, 16, 3, 1536], P(None, 'dp', None, None, 'mp'), may hold values from 6.080713e-07 to 2.432285e-06
- step_second_moment: float32 [2, 8, 16, 24], P(None, 'dp', None, 'mp'), may hold values from 6.080713e-07 to 2.432285e-06
- shared_second_moment: float32 [2, 8, 16, 1792], P(None, 'dp'), may hold values from 6.080713e-07 to 2.432285e-06
Outputs:
- mixed_out: bfloat16 [2, 4, 2048, 768], P(None, 'dp', 'seq')
- grad_tokens: bfloat16 [2, 4, 2048, 768], P(None, 'dp', 'seq')
- grad_norm: float32 [], replicated
- revised_broad: float32 [2, 8, 16, 3, 1536], P(None, 'dp', None, None, 'mp')
- revised_step: float32 [2, 8, 16, 24], P(None, 'dp', None, 'mp')
- revised_shared: float32 [2, 8, 16, 1792], P(None, 'dp')
- fresh_first_broad: float32 [2, 8, 16, 3, 1536], P(None, 'dp', None, None, 'mp')
- fresh_first_step: float32 [2, 8, 16, 24], P(None, 'dp', None, 'mp')
- fresh_first_shared: float32 [2, 8, 16, 1792], P(None, 'dp')
- fresh_square_broad: float32 [2, 8, 16, 3, 1536], P(None, 'dp', None, None, 'mp')
- fresh_square_step: float32 [2, 8, 16, 24], P(None, 'dp', None, 'mp')
- fresh_square_shared: float32 [2, 8, 16, 1792], P(None, 'dp')
- copy_wide: bfloat16 [2, 8, 16, 3, 1536], P(None, 'dp', None, None, 'mp')
- copy_dt: bfloat16 [2, 8, 16, 24], P(None, 'dp', None, 'mp')
- copy_rep: bfloat16 [2, 8, 16, 1792], P(None, 'dp')
The draws below stay inside these ranges and needn't reach their ends.
Inputs may be any that keep to these rules, and one draw needn't show every extreme that they name: `document_numbers`: never falling along a pack and starting at 0. In each row one micro-batch, drawn from the seed, holds a single document; every other pack holds documents 0 to 3, the last of them at least half of the pack. `head_settings`: row 0 is the bias added before softplus, row 1 the logarithm of the decay coefficient, row 2 the skip factor.
All inputs are finite; a program needn't handle non-finite values.
Results may differ from the reference program's by a relative error of at most 0.025.
Values may be sent and summed in bfloat16 or wider, within the bound.
No kernel may reach another device: no remote copies, remote signals or barrier semaphores. Data moves between devices by JAX's collectives and lax.ppermute only.
A program may use at most 256 MiB of HBM per device.

```python
import math
import jax
import jax.numpy as jnp
from jax import lax

MODEL_DIM = 768
MIXER_HEADS = 24
HEAD_DIM = 64
SCAN_STATE = 128
CONV = 4
SPAN = 256
ADAPTER_RANK = 16
ADAPTER_COUNT = 8
DOCS = 4
LAYER_COUNT = 2
MB = 2
STEP = 10
INNER_WIDTH = 1536
PACK = 2048
ROWS = 4


def permute_cuts(one_key):
    return jax.random.permutation(one_key, PACK // 2 - 1)


def draw_document_numbers(key, part):
    key = jax.random.fold_in(key, 11)
    whole_key, cut_key = jax.random.split(key)
    whole_batch = jax.random.randint(whole_key, (ROWS,), 0, MB)
    pack_keys = jax.random.split(cut_key, MB * ROWS)
    shuffled = jax.vmap(permute_cuts)(pack_keys)
    cut_points = jnp.sort(shuffled[:, :DOCS - 1] + 1, axis=1)
    positions = jnp.arange(PACK)
    seg_all = jnp.sum((positions[None, :, None] >= cut_points[:, None, :]).astype(jnp.int32), axis=2)
    seg_all = seg_all.reshape(MB, ROWS, PACK)
    single = jnp.arange(MB)[:, None] == whole_batch[None, :]
    return jnp.where(single[:, :, None], 0, seg_all).astype(jnp.int32)


def draw_head_settings(key, part):
    key = jax.random.fold_in(key, 23)
    sub_keys = jax.random.split(key, 5)
    fast_share = 0.5
    fast_head = jax.random.uniform(sub_keys[0], (LAYER_COUNT, MIXER_HEADS)) < fast_share
    fast_rate = jnp.exp(jax.random.uniform(sub_keys[1], (LAYER_COUNT, MIXER_HEADS), minval=jnp.log(1.0 / 50.0), maxval=jnp.log(1.0 / 30.0)))
    slow_rate = jnp.exp(jax.random.uniform(sub_keys[2], (LAYER_COUNT, MIXER_HEADS), minval=jnp.log(0.2 / PACK), maxval=jnp.log(2.0 / PACK)))
    decay_rate = jnp.where(fast_head, fast_rate, slow_rate)
    step_base = jnp.exp(jax.random.uniform(sub_keys[3], (LAYER_COUNT, MIXER_HEADS), minval=jnp.log(0.02), maxval=jnp.log(0.08)))
    step_bias = jnp.log(jnp.expm1(step_base))
    decay_coef = jnp.log(decay_rate / step_base)
    skip_gain = jax.random.uniform(sub_keys[4], (LAYER_COUNT, MIXER_HEADS), minval=0.5, maxval=1.5)
    return jnp.stack([step_bias, decay_coef, skip_gain], axis=1).astype(jnp.float32)


def set_ends(entries, own_key, smallest, top_value):
    longest = entries.shape.index(max(entries.shape))
    spots = []
    for shift in (0, 1):
        where = [jax.random.randint(jax.random.fold_in(own_key, axis), (), 0, length) for axis, length in enumerate(entries.shape)]
        where[longest] = (where[longest] + shift) % entries.shape[longest]
        spots.append(tuple(where))
    return entries.at[spots[0]].set(smallest).at[spots[1]].set(top_value)


def block_levels(key, dims, shards, low, largest):
    factor_of = 1.0
    for dim, shards_of in shards:
        heights = jax.random.uniform(jax.random.fold_in(jax.random.fold_in(key, 6), dim), (shards_of,), jnp.float32, low / len(shards), largest / len(shards))
        factor_of = factor_of * jnp.repeat(jnp.exp(heights), dims[dim] // shards_of).reshape((-1,) + (1,) * (len(dims) - 1 - dim))
    return factor_of


def scatter_about(key, shape, width, limit, pieces=(), kind=jnp.bfloat16):
    drawn = jax.random.normal(key, shape, jnp.float32) * width
    if len(pieces) > 0:
        drawn = block_levels(key, shape, pieces, -0.22, 0.18) * drawn
    return jnp.clip(drawn, min=-limit, max=limit).astype(kind)


def setup_inputs(seed: int = 0) -> dict:
    streams_of = jax.random.split(jax.random.key(seed), 23)
    return {
        "tokens": scatter_about(streams_of[0], (MB, ROWS, PACK, MODEL_DIM), 1.0, 6.0, ((1, 4), (2, 4))),
        "output_cotangent": scatter_about(streams_of[1], (MB, ROWS, PACK, MODEL_DIM), 1.0, 6.0, ((1, 4), (2, 4))),
        "document_numbers": draw_document_numbers(jax.random.fold_in(streams_of[22], 71), 0),
        "document_adapter": set_ends(jax.random.randint(streams_of[3], (MB, ROWS, DOCS), 0, ADAPTER_COUNT), jax.random.fold_in(streams_of[3], 1), 0, ADAPTER_COUNT - 1).astype(jnp.int32),
        "input_norm_gain": jnp.clip(1.0 + 0.1 * jax.random.normal(streams_of[4], (LAYER_COUNT, MODEL_DIM), jnp.float32), 0.5, 1.5).astype(jnp.bfloat16),
        "gate_head_projection": scatter_about(streams_of[5], (LAYER_COUNT, MODEL_DIM, 2, INNER_WIDTH), MODEL_DIM ** -0.5, 0.21875, ((1, 4), (3, 2))),
        "map_projection": scatter_about(streams_of[6], (LAYER_COUNT, MODEL_DIM, 2 * SCAN_STATE), MODEL_DIM ** -0.5, 0.21875, ((1, 4),)),
        "step_projection": scatter_about(streams_of[7], (LAYER_COUNT, MODEL_DIM, MIXER_HEADS), MODEL_DIM ** -0.5, 0.21875, ((1, 4), (2, 2))),
        "output_projection": scatter_about(streams_of[8], (LAYER_COUNT, INNER_WIDTH, MODEL_DIM), INNER_WIDTH ** -0.5, 0.15625, ((1, 2), (2, 4))),
        "head_conv_taps": jnp.clip(jax.random.uniform(streams_of[9], (LAYER_COUNT, CONV + 1, INNER_WIDTH), jnp.float32, -0.5, 0.5) * block_levels(streams_of[9], (LAYER_COUNT, CONV + 1, INNER_WIDTH), ((2, 2),), -0.4, 0.0), -0.5, 0.5).astype(jnp.bfloat16),
        "map_conv_taps": jnp.clip(jax.random.uniform(streams_of[10], (LAYER_COUNT, CONV + 1, 2 * SCAN_STATE), jnp.float32, -0.5, 0.5), -0.5, 0.5).astype(jnp.bfloat16),
        "head_settings": draw_head_settings(jax.random.fold_in(streams_of[22], 71), 0),
        "gated_norm_gain": jnp.clip(1.0 + 0.1 * jax.random.normal(streams_of[12], (LAYER_COUNT, INNER_WIDTH), jnp.float32), 0.5, 1.5).astype(jnp.bfloat16),
        "adapter_broad": scatter_about(streams_of[13], (LAYER_COUNT, ADAPTER_COUNT, ADAPTER_RANK, 3, INNER_WIDTH), 0.05, 0.3125, ((1, 4), (4, 2)), jnp.float32),
        "adapter_step": scatter_about(streams_of[14], (LAYER_COUNT, ADAPTER_COUNT, ADAPTER_RANK, MIXER_HEADS), 0.05, 0.3125, ((1, 4), (3, 2)), jnp.float32),
        "adapter_shared": scatter_about(streams_of[15], (LAYER_COUNT, ADAPTER_COUNT, ADAPTER_RANK, 2 * MODEL_DIM + 2 * SCAN_STATE), 0.05, 0.3125, ((1, 4),), jnp.float32),
        "broad_first_moment": scatter_about(streams_of[16], (LAYER_COUNT, ADAPTER_COUNT, ADAPTER_RANK, 3, INNER_WIDTH), (1.0 / (LAYER_COUNT * ADAPTER_COUNT * ADAPTER_RANK * (3 * INNER_WIDTH + MIXER_HEADS + 2 * MODEL_DIM + 2 * SCAN_STATE)) ** 0.5), 0.0048828125, ((1, 4), (4, 2)), jnp.float32),
        "step_first_moment": scatter_about(streams_of[17], (LAYER_COUNT, ADAPTER_COUNT, ADAPTER_RANK, MIXER_HEADS), (1.0 / (LAYER_COUNT * ADAPTER_COUNT * ADAPTER_RANK * (3 * INNER_WIDTH + MIXER_HEADS + 2 * MODEL_DIM + 2 * SCAN_STATE)) ** 0.5), 0.0048828125, ((1, 4), (3, 2)), jnp.float32),
        "shared_first_moment": scatter_about(streams_of[18], (LAYER_COUNT, ADAPTER_COUNT, ADAPTER_RANK, 2 * MODEL_DIM + 2 * SCAN_STATE), (1.0 / (LAYER_COUNT * ADAPTER_COUNT * ADAPTER_RANK * (3 * INNER_WIDTH + MIXER_HEADS + 2 * MODEL_DIM + 2 * SCAN_STATE)) ** 0.5), 0.0048828125, ((1, 4),), jnp.float32),
        "broad_second_moment": jnp.clip(jnp.exp(math.log(2.4322851004399126e-06) - 1.3862944 * jax.random.uniform(streams_of[19], (LAYER_COUNT, ADAPTER_COUNT, ADAPTER_RANK, 3, INNER_WIDTH), jnp.float32) ** block_levels(streams_of[19], (LAYER_COUNT, ADAPTER_COUNT, ADAPTER_RANK, 3, INNER_WIDTH), ((1, 4), (4, 2)), -0.2, 0.2)), 6.080712751099782e-07, 2.4322851004399126e-06),
        "step_second_moment": jnp.clip(jnp.exp(math.log(2.4322851004399126e-06) - 1.3862944 * jax.random.uniform(streams_of[20], (LAYER_COUNT, ADAPTER_COUNT, ADAPTER_RANK, MIXER_HEADS), jnp.float32) ** block_levels(streams_of[20], (LAYER_COUNT, ADAPTER_COUNT, ADAPTER_RANK, MIXER_HEADS), ((1, 4), (3, 2)), -0.2, 0.2)), 6.080712751099782e-07, 2.4322851004399126e-06),
        "shared_second_moment": jnp.clip(jnp.exp(math.log(2.4322851004399126e-06) - 1.3862944 * jax.random.uniform(streams_of[21], (LAYER_COUNT, ADAPTER_COUNT, ADAPTER_RANK, 2 * MODEL_DIM + 2 * SCAN_STATE), jnp.float32) ** block_levels(streams_of[21], (LAYER_COUNT, ADAPTER_COUNT, ADAPTER_RANK, 2 * MODEL_DIM + 2 * SCAN_STATE), ((1, 4),), -0.2, 0.2)), 6.080712751099782e-07, 2.4322851004399126e-06),
    }


norm_eps = 1e-05
learn_rate = 0.04
beta_one = 0.5
beta_two = 0.5
weight_decay = 0.01
adam_eps = 1e-08
clip_max = 1.0
highest = lax.Precision.HIGHEST

@jax.custom_vjp
def low(v):
    return lax.optimization_barrier(v.astype(jnp.bfloat16)).astype(jnp.float32)

@jax.custom_vjp
def low_back(v):
    return v

def low_keep(v):
    return (low(v), None)

def low_pass(kept, grad):
    return (grad,)

def back_keep(v):
    return (v, None)

def back_low(kept, grad):
    return (low(grad),)
low.defvjp(low_keep, low_pass)
low_back.defvjp(back_keep, back_low)

def dense(left_side, right_side):
    return jnp.dot(left_side, right_side, precision=highest, preferred_element_type=jnp.float32)

def rms_scale(values):
    return lax.rsqrt(lax.optimization_barrier(jnp.mean(values * values, axis=-1, keepdims=True)) + norm_eps)

def select_rank(values, adapter_pick):
    length = values.shape[0]
    return lax.optimization_barrier(jnp.sum(values.reshape(length, adapter_pick.shape[1], -1) * adapter_pick[:, :, None], axis=1))

def spread_rank(values, adapter_pick):
    length = values.shape[0]
    return (adapter_pick[:, :, None] * values[:, None, :]).reshape(length, -1)

def conv_mix(mixer_rows, conv_taps, seg_row):
    summed = conv_taps[CONV][None, :] + conv_taps[0][None, :] * mixer_rows
    for offset in range(1, CONV):
        moved = jnp.concatenate([jnp.zeros((offset, mixer_rows.shape[1]), jnp.float32), mixer_rows[:-offset]], axis=0)
        before_seg = jnp.concatenate([jnp.full((offset,), -1, jnp.int32), seg_row[:-offset]], axis=0)
        same_doc = jnp.where(before_seg == seg_row, 1.0, 0.0).astype(jnp.float32)
        summed = summed + conv_taps[offset][None, :] * moved * same_doc[:, None]
    return summed

def ssd_block(carry, members):
    state_now, last_seg = carry
    x_block, b_block, c_block, dt_block, decay_block, seg_block = members
    cumulated = jnp.cumsum(decay_block, axis=0)
    positions = jnp.arange(SPAN)
    same_doc = (seg_block[:, None] == seg_block[None, :]) & (positions[:, None] >= positions[None, :])
    gaps_log = cumulated[:, None, :] - cumulated[None, :, :]
    mix_weight = jnp.where(same_doc[:, :, None], jnp.exp(jnp.where(same_doc[:, :, None], gaps_log, 0.0)), 0.0)
    scores = dense(c_block, b_block.T)
    mixing = scores[:, :, None] * mix_weight * dt_block[None, :, :]
    final_result = jnp.einsum('tsh,shp->thp', mixing, x_block, precision=highest)
    entry = jnp.where(seg_block == last_seg, 1.0, 0.0).astype(jnp.float32)[:, None] * jnp.exp(cumulated)
    final_result = final_result + entry[:, :, None] * jnp.einsum('tn,hpn->thp', c_block, state_now, precision=highest)
    tail_weight = jnp.where(seg_block == seg_block[SPAN - 1], 1.0, 0.0).astype(jnp.float32)[:, None] * jnp.exp(cumulated[SPAN - 1][None, :] - cumulated) * dt_block
    keep_block = jnp.where(seg_block[SPAN - 1] == last_seg, 1.0, 0.0).astype(jnp.float32) * jnp.exp(cumulated[SPAN - 1])
    added = jnp.einsum('shp,sn->hpn', tail_weight[:, :, None] * x_block, b_block, precision=highest)
    state_now = keep_block[:, None, None] * state_now + added
    return ((state_now, seg_block[SPAN - 1]), final_result)

def ssd_whole(x_heads, b_matrix, c_matrix, dt_value, decay_log, seg_row):
    length, head_count, head_width = x_heads.shape
    blocks = length // SPAN
    members = (x_heads.reshape(blocks, SPAN, head_count, head_width), b_matrix.reshape(blocks, SPAN, -1), c_matrix.reshape(blocks, SPAN, -1), dt_value.reshape(blocks, SPAN, head_count), decay_log.reshape(blocks, SPAN, head_count), seg_row.reshape(blocks, SPAN))
    initial = (jnp.zeros((head_count, head_width, b_matrix.shape[1]), jnp.float32), jnp.array(-1, jnp.int32))
    _, final_result = lax.scan(jax.checkpoint(ssd_block), initial, members)
    return final_result.reshape(length, head_count, head_width)

def mamba_layer(residual, frozen, adapter, seg_row, adapter_pick):
    gain_vec, gate_head_projection, map_projection, step_projection, output_projection, conv_taps, head_table, norm_vec = frozen
    wide_part, dt_part, rep_part = adapter
    length = residual.shape[0]
    normed = low(residual * rms_scale(residual) * gain_vec[None, :])
    a_in = jnp.transpose(rep_part[:, :, :MODEL_DIM], (2, 0, 1)).reshape(MODEL_DIM, ADAPTER_COUNT * ADAPTER_RANK)
    b_in = jnp.concatenate([wide_part[:, :, 0:2].reshape(ADAPTER_COUNT * ADAPTER_RANK, 2 * INNER_WIDTH), rep_part[:, :, MODEL_DIM:MODEL_DIM + 2 * SCAN_STATE].reshape(ADAPTER_COUNT * ADAPTER_RANK, 2 * SCAN_STATE), dt_part.reshape(ADAPTER_COUNT * ADAPTER_RANK, MIXER_HEADS)], axis=1)
    w_in = jnp.concatenate([gate_head_projection.reshape(MODEL_DIM, 2 * INNER_WIDTH), map_projection, step_projection], axis=1)
    lowrank = low_back(low(select_rank(dense(normed, a_in), adapter_pick)))
    proj = low_back(dense(normed, w_in) + dense(spread_rank(lowrank, adapter_pick), b_in))
    gate_raw = proj[:, :INNER_WIDTH]
    mixer_rows = low(proj[:, INNER_WIDTH:2 * INNER_WIDTH + 2 * SCAN_STATE])
    dt_raw = proj[:, 2 * INNER_WIDTH + 2 * SCAN_STATE:]
    activated = jax.nn.silu(conv_mix(mixer_rows, conv_taps, seg_row))
    x_heads = activated[:, :INNER_WIDTH].reshape(length, MIXER_HEADS, HEAD_DIM)
    b_matrix = activated[:, INNER_WIDTH:INNER_WIDTH + SCAN_STATE]
    c_matrix = activated[:, INNER_WIDTH + SCAN_STATE:]
    dt_value = jax.nn.softplus(dt_raw + head_table[0][None, :])
    decay_log = -jnp.exp(head_table[1])[None, :] * dt_value
    mixed = ssd_whole(x_heads, b_matrix, c_matrix, dt_value, decay_log, seg_row) + head_table[2][None, :, None] * x_heads
    gated = mixed.reshape(length, INNER_WIDTH) * jax.nn.silu(gate_raw)
    normal_out = low(gated * rms_scale(gated) * norm_vec[None, :])
    a_out = jnp.transpose(wide_part[:, :, 2], (2, 0, 1)).reshape(INNER_WIDTH, ADAPTER_COUNT * ADAPTER_RANK)
    b_out = rep_part[:, :, MODEL_DIM + 2 * SCAN_STATE:].reshape(ADAPTER_COUNT * ADAPTER_RANK, MODEL_DIM)
    second = low_back(low(select_rank(dense(normal_out, a_out), adapter_pick)))
    branch = low_back(dense(normal_out, output_projection) + dense(spread_rank(second, adapter_pick), b_out))
    return residual + branch

def adamw_update(param_now, gradient, moment_now, square_now, scale_factor):
    gradient = gradient * scale_factor
    first_mom = beta_one * moment_now + (1.0 - beta_one) * gradient
    second_mom = beta_two * square_now + (1.0 - beta_two) * gradient * gradient
    update = first_mom / (1.0 - beta_one ** STEP) / (jnp.sqrt(second_mom / (1.0 - beta_two ** STEP)) + adam_eps)
    param_new = param_now - learn_rate * (update + weight_decay * param_now)
    return (param_new, first_mom, second_mom)

def reference(tokens, output_cotangent, document_numbers, document_adapter, input_norm_gain, gate_head_projection, map_projection, step_projection, output_projection, head_conv_taps, map_conv_taps, head_settings, gated_norm_gain, adapter_broad, adapter_step, adapter_shared, broad_first_moment, step_first_moment, shared_first_moment, broad_second_moment, step_second_moment, shared_second_moment):
    frozen = []
    for layer_index in range(LAYER_COUNT):
        conv_taps = jnp.concatenate([head_conv_taps[layer_index], map_conv_taps[layer_index]], axis=1).astype(jnp.float32)
        frozen.append((input_norm_gain[layer_index].astype(jnp.float32), gate_head_projection[layer_index].astype(jnp.float32), map_projection[layer_index].astype(jnp.float32), step_projection[layer_index].astype(jnp.float32), output_projection[layer_index].astype(jnp.float32), conv_taps, head_settings[layer_index], gated_norm_gain[layer_index].astype(jnp.float32)))
    packs = MB * ROWS
    flat_tokens = tokens.reshape(packs, PACK, MODEL_DIM)
    flat_grads = output_cotangent.reshape(packs, PACK, MODEL_DIM)
    flat_segs = document_numbers.reshape(packs, PACK)
    flat_adapters = document_adapter.reshape(packs, DOCS)

    def one_pack(totals, items):
        packed_tokens, cotangent, seg_row, chosen = items
        doc_pick = jnp.where(seg_row[:, None] == jnp.arange(DOCS)[None, :], 1.0, 0.0).astype(jnp.float32)
        which_pick = jnp.where(chosen[:, None] == jnp.arange(ADAPTER_COUNT)[None, :], 1.0, 0.0).astype(jnp.float32)
        adapter_pick = dense(doc_pick, which_pick)

        def forward_pass(residual, wide_all, dt_all, rep_all):
            for layer_index in range(LAYER_COUNT):
                adapter = (low(wide_all[layer_index]), low(dt_all[layer_index]), low(rep_all[layer_index]))
                residual = mamba_layer(residual, frozen[layer_index], adapter, seg_row, adapter_pick)
            return residual
        final_result, backward_map = jax.vjp(forward_pass, packed_tokens.astype(jnp.float32), adapter_broad, adapter_step, adapter_shared)
        gradients = backward_map(cotangent.astype(jnp.float32))
        totals = (totals[0] + gradients[1], totals[1] + gradients[2], totals[2] + gradients[3])
        return (totals, (final_result.astype(jnp.bfloat16), gradients[0].astype(jnp.bfloat16)))
    begin_position = (jnp.zeros_like(adapter_broad), jnp.zeros_like(adapter_step), jnp.zeros_like(adapter_shared))
    totals, (outputs, input_grads) = lax.scan(one_pack, begin_position, (flat_tokens, flat_grads, flat_segs, flat_adapters))
    gradient_broad, gradient_step, gradient_shared = totals
    grad_norm = jnp.sqrt(jnp.sum(gradient_broad * gradient_broad) + jnp.sum(gradient_step * gradient_step) + jnp.sum(gradient_shared * gradient_shared))
    scale_factor = clip_max / jnp.maximum(grad_norm, clip_max)
    revised_broad, fresh_first_broad, fresh_square_broad = adamw_update(adapter_broad, gradient_broad, broad_first_moment, broad_second_moment, scale_factor)
    revised_step, fresh_first_step, fresh_square_step = adamw_update(adapter_step, gradient_step, step_first_moment, step_second_moment, scale_factor)
    revised_shared, fresh_first_shared, fresh_square_shared = adamw_update(adapter_shared, gradient_shared, shared_first_moment, shared_second_moment, scale_factor)
    return (outputs.reshape(MB, ROWS, PACK, MODEL_DIM), input_grads.reshape(MB, ROWS, PACK, MODEL_DIM), grad_norm, revised_broad, revised_step, revised_shared, fresh_first_broad, fresh_first_step, fresh_first_shared, fresh_square_broad, fresh_square_step, fresh_square_shared, revised_broad.astype(jnp.bfloat16), revised_step.astype(jnp.bfloat16), revised_shared.astype(jnp.bfloat16))
```

```python
import functools

import jax
import jax.numpy as jnp
from jax import lax
from jax.experimental import pallas as pl
from jax.experimental.pallas import tpu as pltpu
from jax.sharding import PartitionSpec as P

CONV = 4
STEP = 10
LANES = 128
SPAN = 128
PAD = 8
RESET = -128.0

norm_eps = 1e-05
learn_rate = 0.04
beta_one = 0.5
beta_two = 0.5
weight_decay = 0.01
adam_eps = 1e-08
clip_max = 1.0
low = jnp.bfloat16
full = jnp.float32


def nn(a, b):
    return lax.dot_general(a, b, (((1,), (0,)), ((), ())), preferred_element_type=full)


def nt(a, b):
    return lax.dot_general(a, b, (((1,), (1,)), ((), ())), preferred_element_type=full)


def tn(a, b):
    return lax.dot_general(a, b, (((0,), (0,)), ((), ())), preferred_element_type=full)


def two_parts(values, axis):
    high = values.astype(low)
    rest = (values - high.astype(full)).astype(low)
    return jnp.concatenate([high, rest], axis=axis)


def three_parts(values, axis):
    high = values.astype(low)
    rest = values - high.astype(full)
    middle = rest.astype(low)
    last = (rest - middle.astype(full)).astype(low)
    return jnp.concatenate([high, middle, last], axis=axis)


def widen(values, spread_two):
    return nn(two_parts(values, 1), spread_two)


def per_head(values, spread_two):
    heads = spread_two[:LANES]
    high = values.astype(low)
    rest = (values - high.astype(full)).astype(low)
    return nt(high, heads) + nt(rest, heads)


def triangle(kind):
    rows = lax.broadcasted_iota(jnp.int32, (SPAN, SPAN), 0)
    columns = lax.broadcasted_iota(jnp.int32, (SPAN, SPAN), 1)
    return rows >= columns if kind == "lower" else rows <= columns


def cumulate(values, kind):
    keep = triangle(kind).astype(full).astype(low)
    return nn(jnp.concatenate([keep, keep, keep], axis=1), three_parts(values, 0))


def sigmoid(values):
    return 1.0 / (1.0 + jnp.exp(-values))


def kernel_call(body, outs, ins, scratch=(), flops=0, name=None, limit=48):
    moved = sum(a.size * a.dtype.itemsize for a in list(ins) + list(outs))
    whole = pl.BlockSpec(memory_space=pltpu.VMEM)
    return pl.pallas_call(
        body,
        out_shape=tuple(outs),
        in_specs=[whole] * len(ins),
        out_specs=tuple([whole] * len(outs)),
        scratch_shapes=list(scratch),
        compiler_params=pltpu.CompilerParams(vmem_limit_bytes=limit * 2**20),
        cost_estimate=pl.CostEstimate(flops=flops, bytes_accessed=moved, transcendentals=0),
        name=name,
    )(*ins)


def shape(dims, kind):
    return jax.ShapeDtypeStruct(dims, kind)


def project_kernel(halves, half, h, gain, mask, w_in, adapt, normed_o, spread_o, gate_o, rows_o, dt_o):
    values = h[...].astype(full)
    width = values.shape[1]
    scale = lax.rsqrt(jnp.mean(values * values, axis=1, keepdims=True) + norm_eps)
    normed = (values * scale * gain[0:1]).astype(low)
    normed_o[...] = normed
    first = 3 * half + 2 * LANES
    part = width // halves
    down = jnp.concatenate([adapt[m, :, first : first + part] for m in range(halves)], axis=1)
    spread = nt(normed, down).astype(low) * mask[...]
    spread_o[...] = spread
    inner = halves * half
    for m in range(halves):
        for begin, end, target, place in (
            (0, half, gate_o, m * half),
            (half, 2 * half, rows_o, m * half),
            (2 * half, 2 * half + LANES, rows_o, inner + m * LANES),
        ):
            made = nn(normed, w_in[m, :, begin:end]) + nn(spread, adapt[m, :, begin:end])
            target[:, place : place + end - begin] = made.astype(target.dtype)
    begin = 2 * half + LANES
    w_dt = sum(w_in[m, :, begin : begin + LANES].astype(full) for m in range(halves)).astype(low)
    b_dt = sum(adapt[m, :, begin : begin + LANES].astype(full) for m in range(halves)).astype(low)
    dt_o[...] = nn(normed, w_dt) + nn(spread, b_dt)


def conv_chunk(ext, lags, taps, begin, columns):
    window = ext[pl.ds(begin, SPAN + PAD), columns]
    summed = taps[CONV : CONV + 1, columns] + taps[0:1, columns] * window[PAD:]
    for lag in range(1, CONV):
        same = lags[pl.ds(begin, SPAN), (lag - 1) * LANES : lag * LANES]
        summed = summed + taps[lag : lag + 1, columns] * window[PAD - lag : PAD - lag + SPAN] * same
    return summed


def fill_extended(ext, halo, rows):
    ext[0:PAD, :] = halo[...].astype(full)
    ext[PAD : PAD + rows.shape[0], :] = rows[...].astype(full)


def states_kernel(
    inner, rows, halo, taps, lags, dt_raw, table, jump, spread_two,
    act_o, xdt_o, dt_o, cum_o, flat_o, begin_o, end_o, total_o, ext, state,
):
    length = rows.shape[0]
    channels = rows.shape[1]
    fill_extended(ext, halo, rows)
    state[...] = jnp.zeros_like(state)

    def block(k, so_far):
        begin = pl.multiple_of(k * SPAN, SPAN)
        span = pl.ds(begin, SPAN)
        for c in range(0, channels, LANES):
            columns = slice(c, c + LANES)
            summed = conv_chunk(ext, lags, taps, begin, columns)
            act_o[span, columns] = (summed * sigmoid(summed)).astype(low)
        raw = dt_raw[span, :] + table[0:1, :]
        dt = jnp.maximum(raw, 0.0) + jnp.log1p(jnp.exp(-jnp.abs(raw)))
        cum = cumulate(jump[span, :] - jnp.exp(table[1:2, :]) * dt, "lower")
        dt_o[span, :] = dt
        cum_o[span, :] = cum
        flat_o[:, span] = cum.T
        total = cum[SPAN - 1 : SPAN, :]
        xdt = (act_o[span, 0:inner].astype(full) * widen(dt, spread_two[...])).astype(low)
        xdt_o[span, :] = xdt
        tail = widen(jnp.exp(total - cum), spread_two[...])
        b_map = act_o[span, inner : inner + LANES]
        begin_o[k] = state[...].astype(low)
        keep = widen(jnp.broadcast_to(jnp.exp(total), (8, LANES)), spread_two[...])[0:1]
        state[...] = state[...] * keep + tn(b_map, (xdt.astype(full) * tail).astype(low))
        return so_far + total

    total = lax.fori_loop(0, length // SPAN, block, jnp.zeros((1, LANES), full))
    end_o[...] = state[...].astype(low)
    total_o[...] = jnp.broadcast_to(total, total_o.shape)


def intra_kernel(inner, head_width, act, xdt, cum, flat, begin_state, skip, spread_two, y_o):
    length = act.shape[0]
    keep = triangle("lower")
    left = lax.broadcasted_iota(jnp.int32, (SPAN, LANES), 1) < head_width

    def block(k, carry):
        begin = pl.multiple_of(k * SPAN, SPAN)
        span = pl.ds(begin, SPAN)
        b_map = act[span, inner : inner + LANES]
        c_map = act[span, inner + LANES : inner + 2 * LANES]
        scores = nt(c_map, b_map)
        cum_now = cum[span, :]
        entry = widen(jnp.exp(cum_now), spread_two[...])
        before = nn(c_map, begin_state[k])
        for pair in range(inner // LANES):
            columns = slice(pair * LANES, (pair + 1) * LANES)
            mixing = []
            for head in (2 * pair, 2 * pair + 1):
                gap = cum_now[:, head : head + 1] - flat[head : head + 1, span]
                mixing.append((scores * jnp.exp(jnp.where(keep, gap, -1e30))).astype(low))
            x_pair = xdt[span, columns]
            nothing = jnp.zeros_like(x_pair)
            x_two = jnp.concatenate([jnp.where(left, x_pair, nothing), jnp.where(left, nothing, x_pair)], axis=0)
            intra = nn(jnp.concatenate(mixing, axis=1), x_two)
            y_o[span, columns] = (
                intra
                + entry[:, columns] * before[:, columns]
                + skip[0:1, columns] * act[span, columns].astype(full)
            ).astype(low)
        return carry

    lax.fori_loop(0, length // SPAN, block, 0)


def combine(parts, weights_log, spread_two):
    weights = widen(jnp.exp(weights_log), spread_two)
    total = parts[0].astype(full) * weights[0:1]
    for i in range(1, len(parts)):
        total = total + parts[i].astype(full) * weights[i : i + 1]
    return total


def output_kernel(
    halves, half, count, last, h, y_local, gate, act, cum, carry_log, gain, mask, w_out, adapt, spread_two, *rest
):
    parts, rest = rest[:count], rest[count:]
    h_o, y_o, normal_o, spread_o, coming_o, gated_s = rest
    length = h.shape[0]
    inner = halves * half
    coming = combine([p[...] for p in parts], carry_log[...], spread_two[...]).astype(low)
    coming_o[...] = coming
    before = jnp.zeros((1, LANES), full)
    for k in range(length // SPAN):
        span = slice(k * SPAN, (k + 1) * SPAN)
        cum_now = cum[span, :]
        carry = widen(jnp.exp(cum_now + before), spread_two[...])
        before = before + cum_now[SPAN - 1 : SPAN, :]
        c_map = act[span, inner + LANES : inner + 2 * LANES]
        y = y_local[span, :].astype(full) + carry * nn(c_map, coming)
        y_o[span, :] = y.astype(low)
        z = gate[span, :].astype(full)
        gated = y * z * sigmoid(z)
        scale = lax.rsqrt(jnp.mean(gated * gated, axis=1, keepdims=True) + norm_eps)
        normal_o[span, :] = (gated * scale * gain[0:1]).astype(low)
    place = 2 * half + 2 * LANES
    second = jnp.zeros((length, LANES), full)
    for m in range(halves):
        second = second + nt(normal_o[:, m * half : (m + 1) * half], adapt[m, :, place : place + half])
    spread = second.astype(low) * mask[...]
    spread_o[...] = spread
    width = h.shape[1]
    part = width // halves
    first = 3 * half + 2 * LANES + part
    up = jnp.concatenate([adapt[m, :, first : first + part] for m in range(halves)], axis=1)
    branch = nn(spread, up)
    for m in range(halves):
        branch = branch + nt(normal_o[:, m * half : (m + 1) * half], w_out[m])
    h_o[...] = (h[...].astype(full) + branch).astype(h_o.dtype)


def output_back_kernel(
    halves, half, upstream, y, gate, normal, spread_out, act, cum, gain, mask, w_out, adapt, spread_two,
    dgate_o, dy_o, own_o, down_o, up_o, seconds,
):
    length = y.shape[0]
    inner = halves * half
    width = upstream.shape[1]
    part = width // halves
    up_low = upstream[...].astype(low)
    place = 2 * half + 2 * LANES
    first = 3 * half + 2 * LANES + part
    up = jnp.concatenate([adapt[m, :, first : first + part] for m in range(halves)], axis=1)
    second = nt(up_low, up).astype(low) * mask[...]
    seconds[...] = second
    up_grad = tn(spread_out[...], up_low)
    for m in range(halves):
        up_o[m] = up_grad[:, m * part : (m + 1) * part].astype(up_o.dtype)
        down_o[m] = tn(second, normal[:, m * half : (m + 1) * half]).astype(down_o.dtype)
    own = jnp.zeros((LANES, inner), full)
    before = jnp.zeros((1, LANES), full)
    for k in range(length // SPAN):
        span = slice(k * SPAN, (k + 1) * SPAN)
        up_now = up_low[span]
        grads = []
        for m in range(halves):
            grads.append(nn(up_now, w_out[m]) + nn(seconds[span, :], adapt[m, :, place : place + half]))
        weighted = jnp.concatenate(grads, axis=1) * gain[0:1]
        y_now = y[span, :].astype(full)
        z = gate[span, :].astype(full)
        sig = sigmoid(z)
        silu = z * sig
        gated = y_now * silu
        scale = lax.rsqrt(jnp.mean(gated * gated, axis=1, keepdims=True) + norm_eps)
        mean_in = jnp.mean(weighted * gated, axis=1, keepdims=True)
        grad_gated = scale * weighted - gated * (scale * scale * scale * mean_in)
        dgate_o[span, :] = (grad_gated * y_now * sig * (1.0 + z * (1.0 - sig))).astype(low)
        dy = grad_gated * silu
        dy_o[span, :] = dy.astype(low)
        cum_now = cum[span, :]
        carry = widen(jnp.exp(cum_now + before), spread_two[...])
        before = before + cum_now[SPAN - 1 : SPAN, :]
        own = own + tn(act[span, inner + LANES : inner + 2 * LANES], (carry * dy).astype(low))
    own_o[...] = own.astype(low)


def intra_back_kernel(inner, head_width, act, xdt, dy, cum, flat, u_o, db_o, dc_o):
    length = act.shape[0]
    keep = triangle("upper")
    left = lax.broadcasted_iota(jnp.int32, (SPAN, LANES), 1) < head_width

    def block(k, carry):
        begin = pl.multiple_of(k * SPAN, SPAN)
        span = pl.ds(begin, SPAN)
        b_map = act[span, inner : inner + LANES]
        c_map = act[span, inner + LANES : inner + 2 * LANES]
        scores = nt(b_map, c_map)
        cum_now = cum[span, :]
        dscores = jnp.zeros((SPAN, SPAN), full)
        for pair in range(inner // LANES):
            columns = slice(pair * LANES, (pair + 1) * LANES)
            dy_pair = dy[span, columns]
            nothing = jnp.zeros_like(dy_pair)
            dy_two = jnp.concatenate([jnp.where(left, dy_pair, nothing), jnp.where(left, nothing, dy_pair)], axis=0)
            products = nt(xdt[span, columns], dy_two)
            mixing = []
            for i, head in enumerate((2 * pair, 2 * pair + 1)):
                gap = flat[head : head + 1, span] - cum_now[:, head : head + 1]
                decay = jnp.exp(jnp.where(keep, gap, -1e30))
                mixing.append((scores * decay).astype(low))
                dscores = dscores + products[:, i * SPAN : (i + 1) * SPAN] * decay
            u_o[span, columns] = nn(jnp.concatenate(mixing, axis=1), dy_two).astype(low)
        dlow = dscores.astype(low)
        db_o[span, :] = nn(dlow, c_map)
        dc_o[span, :] = tn(dlow, b_map)
        return carry

    lax.fori_loop(0, length // SPAN, block, 0)


def scan_back_kernel(
    inner, count, rows, halo, taps, lags, act, xdt, dy, y, u, db_in, dc_in, dt, cum, dt_raw, table, skip,
    begin_state, coming, carry_log, spread_two, *rest,
):
    parts, rest = rest[:count], rest[count:]
    dconv_o, ddt_o, ext, grad, dact = rest
    length = act.shape[0]
    channels = rows.shape[1]
    blocks = length // SPAN
    fill_extended(ext, halo, rows)
    grad[...] = combine([p[...] for p in parts], carry_log[...], spread_two[...])
    ends = [cum[(k + 1) * SPAN - 1 : (k + 1) * SPAN, :] for k in range(blocks)]
    for k in reversed(range(blocks)):
        span = slice(k * SPAN, (k + 1) * SPAN)
        cum_now = cum[span, :]
        total = ends[k]
        before = sum(ends[:k], jnp.zeros((1, LANES), full))
        b_map = act[span, inner : inner + LANES]
        c_map = act[span, inner + LANES : inner + 2 * LANES]
        grad_low = grad[...].astype(low)
        tail = widen(jnp.exp(total - cum_now), spread_two[...])
        entry = widen(jnp.exp(cum_now), spread_two[...])
        rows_wide = widen(jnp.exp(jnp.concatenate([total, before] * 4, axis=0)), spread_two[...])
        keep, carry = rows_wide[0:1], rows_wide[1:2]
        x = act[span, 0:inner].astype(full)
        x_dt = xdt[span, :].astype(full)
        from_later = tail * nn(b_map, grad_low)
        v = u[span, :].astype(full) + from_later
        state = begin_state[k].astype(full) + carry * coming[...].astype(full)
        dy_now = dy[span, :].astype(full)
        db = db_in[span, :] + nt((x_dt * tail).astype(low), grad_low)
        entry_dy = (entry * dy_now).astype(low)
        dc = dc_in[span, :] + nt(entry_dy, state.astype(low))
        kept = keep * grad[...]
        end_rows = jnp.sum(x_dt * from_later, axis=0, keepdims=True) + jnp.sum(kept * state, axis=0, keepdims=True)
        grad[...] = kept + tn(c_map, entry_dy)
        y_scan = y[span, :].astype(full) - skip[0:1, :] * x
        dcum = per_head(dy_now * y_scan - x_dt * v, spread_two[...])
        at_end = per_head(jnp.broadcast_to(end_rows, (8, inner)), spread_two[...])[0:1]
        ddecay = cumulate(dcum, "upper") + at_end
        raw = dt_raw[span, :] + table[0:1, :]
        ddt = per_head(x * v, spread_two[...]) - ddecay * jnp.exp(table[1:2, :])
        ddt_o[span, :] = (ddt * sigmoid(raw)).astype(low)
        dact[span, 0:inner] = widen(dt[span, :], spread_two[...]) * v + skip[0:1, :] * dy_now
        dact[span, inner : inner + LANES] = db
        dact[span, inner + LANES : inner + 2 * LANES] = dc
        for c in range(0, channels, LANES):
            columns = slice(c, c + LANES)
            summed = conv_chunk(ext, lags, taps, k * SPAN, columns)
            sig = sigmoid(summed)
            dconv_o[span, columns] = (dact[span, columns] * sig * (1.0 + summed * (1.0 - sig))).astype(low)


def gate_back_kernel(halves, half, dgate, spread, w_in, adapt, dn_o, dl_o, grad_o):
    dn = dl = 0.0
    for m in range(halves):
        piece = dgate[:, m * half : (m + 1) * half]
        dn = dn + nt(piece, w_in[m, :, 0:half])
        dl = dl + nt(piece, adapt[m, :, 0:half])
        grad_o[m] = tn(spread[...], piece).astype(grad_o.dtype)
    dn_o[...] = dn
    dl_o[...] = dl


def project_back_kernel(
    halves, half, upstream, h, gain, mask, dconv, after, taps, lags, ddt, dn_in, dl_in, spread, normed, w_in, adapt,
    dh_o, grad_o, down_o, ext, drows,
):
    length = h.shape[0]
    channels = dconv.shape[1]
    inner = halves * half
    ext[0:length, :] = dconv[...].astype(full)
    ext[length : length + PAD, :] = after[...].astype(full)

    def block(k, carry):
        begin = pl.multiple_of(k * SPAN, SPAN)
        span = pl.ds(begin, SPAN)
        for c in range(0, channels, LANES):
            columns = slice(c, c + LANES)
            window = ext[pl.ds(begin, SPAN + PAD), columns]
            total = taps[0:1, columns] * window[:SPAN]
            for lag in range(1, CONV):
                same = lags[span, (lag - 1) * LANES : lag * LANES]
                total = total + taps[lag : lag + 1, columns] * window[lag : lag + SPAN] * same
            drows[span, columns] = total.astype(low)
        return carry

    lax.fori_loop(0, length // SPAN, block, 0)
    dn, dl = dn_in[...], dl_in[...]
    begin = 2 * half + LANES
    step = ddt[...]
    w_dt = sum(w_in[m, :, begin : begin + LANES].astype(full) for m in range(halves)).astype(low)
    b_dt = sum(adapt[m, :, begin : begin + LANES].astype(full) for m in range(halves)).astype(low)
    dn = dn + nt(step, w_dt)
    dl = dl + nt(step, b_dt)
    step_grad = tn(spread[...], step).astype(grad_o.dtype)
    for m in range(halves):
        for first, last, place in (
            (half, 2 * half, m * half),
            (2 * half, 2 * half + LANES, inner + m * LANES),
        ):
            piece = drows[:, place : place + last - first]
            dn = dn + nt(piece, w_in[m, :, first:last])
            dl = dl + nt(piece, adapt[m, :, first:last])
            grad_o[m, :, first - half : last - half] = tn(spread[...], piece).astype(grad_o.dtype)
        grad_o[m, :, half + LANES : half + 2 * LANES] = step_grad
    back = dl.astype(low) * mask[...]
    width = h.shape[1]
    part = width // halves
    place = 3 * half + 2 * LANES
    for m in range(halves):
        down_o[m] = tn(back, normed[:, m * part : (m + 1) * part]).astype(down_o.dtype)
    down = jnp.concatenate([adapt[m, :, place : place + part] for m in range(halves)], axis=1)
    dn = dn + nn(back, down)
    values = h[...].astype(full)
    scale = lax.rsqrt(jnp.mean(values * values, axis=1, keepdims=True) + norm_eps)
    weighted = dn * gain[0:1]
    mean_in = jnp.mean(weighted * values, axis=1, keepdims=True)
    dh = upstream[...].astype(full) + scale * weighted - values * (scale * scale * scale * mean_in)
    dh_o[...] = dh.astype(dh_o.dtype)


def moved(block, axis, distance, wrap=False):
    count = lax.axis_size(axis)
    route = [(i, (i + distance) % count) for i in range(count) if wrap or 0 <= i + distance < count]
    return lax.ppermute(block, axis, route)


def swapped(block):
    count = lax.axis_size("mp")
    return lax.ppermute(block, "mp", [(i, count - 1 - i) for i in range(count)])


def summed_shares(parts, axis):
    count = lax.axis_size(axis)
    place = lax.axis_index(axis)
    total = lax.dynamic_index_in_dim(parts, place, 0, False).astype(full)
    for distance in range(1, count):
        piece = lax.dynamic_index_in_dim(parts, (place + distance) % count, 0, False)
        total = total + moved(piece, axis, distance, True).astype(full)
    return total


def reduced(gradient):
    mine = lax.axis_index("mp")
    keep = lax.dynamic_index_in_dim(gradient, mine, 0, False)
    give = lax.dynamic_index_in_dim(gradient, 1 - mine, 0, False)
    both = (keep.astype(full) + swapped(give).astype(full)).astype(low)
    owners, pieces = lax.axis_size("dp"), lax.axis_size("seq")
    ranks, columns = both.shape
    shares = both.reshape(owners, pieces, ranks // (owners * pieces), columns)
    over_seq = summed_shares(jnp.moveaxis(shares, 1, 0), "seq").astype(low)
    return summed_shares(over_seq, "dp")


def adamw_update(param_now, gradient, moment_now, square_now, scale_factor):
    gradient = gradient * scale_factor
    first_mom = beta_one * moment_now + (1.0 - beta_one) * gradient
    second_mom = beta_two * square_now + (1.0 - beta_two) * gradient * gradient
    update = (
        first_mom
        / (1.0 - beta_one**STEP)
        / (jnp.sqrt(second_mom / (1.0 - beta_two**STEP)) + adam_eps)
    )
    param_new = param_now - learn_rate * (update + weight_decay * param_now)
    return (param_new, first_mom, second_mom)


def lanes_of(values, place):
    room = jnp.zeros(values.shape[:-1] + (LANES,), values.dtype)
    return lax.dynamic_update_slice_in_dim(room, values, place, values.ndim - 1)


def rows_of(values, count=PAD):
    return jnp.concatenate([values, jnp.zeros((count - values.shape[0],) + values.shape[1:], values.dtype)], axis=0)


def per_device(
    tokens,
    output_cotangent,
    document_numbers,
    document_adapter,
    input_norm_gain,
    gate_head_projection,
    map_projection,
    step_projection,
    output_projection,
    head_conv_taps,
    map_conv_taps,
    head_settings,
    gated_norm_gain,
    adapter_broad,
    adapter_step,
    adapter_shared,
    broad_first_moment,
    step_first_moment,
    shared_first_moment,
    broad_second_moment,
    step_second_moment,
    shared_second_moment,
):
    halves = lax.axis_size("mp")
    pieces = lax.axis_size("seq")
    owners = lax.axis_size("dp")
    core = lax.axis_index("mp")
    place = lax.axis_index("seq")
    length, width = tokens.shape[2:]
    layers, _, _, half = gate_head_projection.shape
    inner = halves * half
    heads_local = head_settings.shape[2]
    heads = halves * heads_local
    head_width = inner // heads
    own_adapters, rank = adapter_broad.shape[1:3]
    own_rows = own_adapters * rank
    adapters = own_adapters * owners
    ranks = adapters * rank
    part = width // halves
    states = map_projection.shape[2] // 2
    channels = inner + 2 * states

    def mine(values):
        return lax.dynamic_index_in_dim(values, core, 0, False)

    h_first = mine(tokens)[0]
    cotangent = mine(output_cotangent)[0]
    documents = mine(document_numbers)[0]
    chosen = mine(document_adapter)[0]

    def gathered(block):
        got = lax.all_gather(block, ("mp", "dp"), axis=0, tiled=True)
        return got.reshape(halves, -1, block.shape[1])

    low_broad = adapter_broad.astype(low)
    low_step = adapter_step.astype(low)
    low_shared = adapter_shared.astype(low)
    weights = []
    for layer in range(layers):
        zx = gate_head_projection[layer]
        maps = lax.dynamic_slice_in_dim(map_projection[layer], core * states, states, 1)
        steps = lanes_of(step_projection[layer], core * heads_local)
        w_in = gathered(jnp.concatenate([zx[:, 0], zx[:, 1], maps, steps], axis=1))
        broad = low_broad[layer].reshape(own_rows, 3, half)
        shared = low_shared[layer].reshape(own_rows, -1)
        adapt = gathered(
            jnp.concatenate(
                [
                    broad[:, 0],
                    broad[:, 1],
                    lax.dynamic_slice_in_dim(shared, width + core * states, states, 1),
                    lanes_of(low_step[layer].reshape(own_rows, heads_local), core * heads_local),
                    broad[:, 2],
                    lax.dynamic_slice_in_dim(shared, core * part, part, 1),
                    lax.dynamic_slice_in_dim(shared, width + 2 * states + core * part, part, 1),
                ],
                axis=1,
            )
        )
        w_out = gathered(output_projection[layer].T)
        weights.append((w_in, adapt, w_out))

    def over_cores(values):
        return lax.all_gather(values, "mp", axis=values.ndim - 1, tiled=True)

    taps_all = jnp.concatenate([over_cores(head_conv_taps), map_conv_taps], axis=2).astype(full)
    gains_two = over_cores(gated_norm_gain).astype(full)
    tables = over_cores(head_settings)
    head_of = jnp.arange(inner)[None, :] // head_width
    spread_one = (jnp.arange(LANES)[:, None] == head_of).astype(low)
    spread_two = jnp.concatenate([spread_one, spread_one], axis=0)

    begin = place * length
    ends = jnp.concatenate([jnp.full((PAD,), -1, jnp.int32), documents, jnp.full((PAD,), -2, jnp.int32)])
    near = lax.dynamic_slice_in_dim(ends, begin, length + 2 * PAD)
    own = near[PAD : PAD + length]
    jump = jnp.where(own != near[PAD - 1 : PAD - 1 + length], RESET, 0.0).astype(full)
    jump = jnp.broadcast_to(jump[:, None], (length, LANES))

    def same_as(lag):
        same = (own == near[PAD + lag : PAD + lag + length]).astype(full)
        return jnp.broadcast_to(same[:, None], (length, LANES))

    lags = jnp.concatenate([same_as(-lag) for lag in range(1, CONV)], axis=1)
    leads = jnp.concatenate([same_as(lag) for lag in range(1, CONV)], axis=1)
    which = jnp.arange(ranks)[None, :] // rank
    mask = jnp.zeros((length, ranks), jnp.bool_)
    for document in range(chosen.shape[0]):
        mask = mask | ((own == document)[:, None] & (which == chosen[document]))
    mask = mask.astype(low)

    places = jnp.arange(pieces)
    distances = rows_of(jnp.arange(1, pieces), max(PAD, pieces))[:, None]
    earlier = ((places[None] < place) & (places[None] > place - distances)).astype(full)
    later = ((places[None] > place) & (places[None] < place + distances)).astype(full)

    def weigh(chooser, totals):
        return jnp.sum(chooser[:, :, None] * totals[None], axis=1)

    flops_in = 2 * length * width * (2 * inner + 3 * LANES)
    flops_out = 2 * length * width * inner
    flops_scan = 4 * length * SPAN * inner

    h = h_first
    kept = []
    for layer in range(layers):
        w_in, adapt, w_out = weights[layer]
        gain = rows_of(input_norm_gain[layer].astype(full)[None])
        taps = rows_of(taps_all[layer])
        gain_two = rows_of(gains_two[layer][None])
        table = rows_of(jnp.pad(tables[layer], ((0, 0), (0, LANES - heads))))
        skip = rows_of(jnp.repeat(tables[layer][2], head_width)[None])
        normed, spread, gate, rows, dt_raw = kernel_call(
            functools.partial(project_kernel, halves, half),
            [
                shape((length, width), low),
                shape((length, ranks), low),
                shape((length, inner), full),
                shape((length, channels), low),
                shape((length, LANES), full),
            ],
            [h, gain, mask, w_in, adapt],
            flops=flops_in,
            name="project",
        )
        halo = moved(rows[length - PAD :], "seq", 1)
        act, xdt, dt, cum, flat, begin_state, end_state, total = kernel_call(
            functools.partial(states_kernel, inner),
            [
                shape((length, channels), low),
                shape((length, inner), low),
                shape((length, LANES), full),
                shape((length, LANES), full),
                shape((LANES, length), full),
                shape((length // SPAN, states, inner), low),
                shape((states, inner), low),
                shape((PAD, LANES), full),
            ],
            [rows, halo, taps, lags, dt_raw, table, jump, spread_two],
            scratch=[pltpu.VMEM((length + PAD, channels), full), pltpu.VMEM((states, inner), full)],
            flops=flops_scan,
            name="states",
        )
        totals = lax.all_gather(total[0:1], "seq", axis=0, tiled=True)
        arrived = [moved(end_state, "seq", d) for d in range(1, pieces)]
        y_local = kernel_call(
            functools.partial(intra_kernel, inner, head_width),
            [shape((length, inner), low)],
            [act, xdt, cum, flat, begin_state, skip, spread_two],
            flops=flops_scan,
            name="intra",
        )[0]
        last = layer == layers - 1
        h_next, y, normal, spread_out, coming = kernel_call(
            functools.partial(output_kernel, halves, half, len(arrived), last),
            [
                shape((length, width), low if last else full),
                shape((length, inner), low),
                shape((length, inner), low),
                shape((length, ranks), low),
                shape((states, inner), low),
            ],
            [h, y_local, gate, act, cum, weigh(earlier, totals), gain_two, mask, w_out, adapt, spread_two, *arrived],
            scratch=[pltpu.VMEM((8, LANES), full)],
            flops=flops_out,
            name="output",
        )
        kept.append(
            (h, gain, taps, gain_two, table, skip, normed, spread, gate, rows, halo, dt_raw, act, xdt, dt, cum, flat,
             begin_state, totals, y, normal, spread_out, coming)
        )
        h = h_next
    mixed_own = h

    upstream = cotangent
    shares = [None] * layers
    for layer in reversed(range(layers)):
        w_in, adapt, w_out = weights[layer]
        (h, gain, taps, gain_two, table, skip, normed, spread, gate, rows, halo, dt_raw, act, xdt, dt, cum, flat,
         begin_state, totals, y, normal, spread_out, coming) = kept[layer]
        dgate, dy, own_grad, g_down_out, g_up_out = kernel_call(
            functools.partial(output_back_kernel, halves, half),
            [
                shape((length, inner), low),
                shape((length, inner), low),
                shape((states, inner), low),
                shape((halves, ranks, half), low),
                shape((halves, ranks, part), low),
            ],
            [upstream, y, gate, normal, spread_out, act, cum, gain_two, mask, w_out, adapt, spread_two],
            scratch=[pltpu.VMEM((length, ranks), low)],
            flops=flops_out,
            name="output_back",
        )
        arrived = [moved(own_grad, "seq", -d) for d in range(1, pieces)]
        early = jnp.concatenate([g_down_out, g_up_out], axis=2)
        u, db, dc = kernel_call(
            functools.partial(intra_back_kernel, inner, head_width),
            [shape((length, inner), low), shape((length, LANES), full), shape((length, LANES), full)],
            [act, xdt, dy, cum, flat],
            flops=2 * flops_scan,
            name="intra_back",
        )
        dn, dl, g_gate = kernel_call(
            functools.partial(gate_back_kernel, halves, half),
            [shape((length, width), full), shape((length, ranks), full), shape((halves, ranks, half), low)],
            [dgate, spread, w_in, adapt],
            flops=flops_in // 2,
            name="gate_back",
        )
        dconv, ddt = kernel_call(
            functools.partial(scan_back_kernel, inner, len(arrived)),
            [shape((length, channels), low), shape((length, LANES), low)],
            [rows, halo, taps, lags, act, xdt, dy, y, u, db, dc, dt, cum, dt_raw, table, skip, begin_state, coming,
             weigh(later, totals), spread_two, *arrived],
            scratch=[
                pltpu.VMEM((length + PAD, channels), full),
                pltpu.VMEM((states, inner), full),
                pltpu.VMEM((length, channels), full),
            ],
            flops=2 * flops_scan,
            name="scan_back",
        )
        after = moved(dconv[:PAD], "seq", -1)
        dh, g_rest, g_down_in = kernel_call(
            functools.partial(project_back_kernel, halves, half),
            [
                shape((length, width), full if layer > 0 else low),
                shape((halves, ranks, half + 2 * LANES), low),
                shape((halves, ranks, part), low),
            ],
            [upstream, h, gain, mask, dconv, after, taps, leads, ddt, dn, dl, spread, normed, w_in, adapt],
            scratch=[pltpu.VMEM((length + PAD, channels), full), pltpu.VMEM((length, channels), low)],
            flops=flops_in // 2,
            name="project_back",
        )
        upstream = dh
        rest = jnp.concatenate([g_gate, g_rest, g_down_in], axis=2)
        shares[layer] = jnp.concatenate([reduced(rest), reduced(early)], axis=1)

    whole = lax.all_gather(jnp.stack(shares), "seq", axis=1, tiled=True)
    zx, maps, steps, down_in, down_out, up_out = jnp.split(
        whole,
        [2 * half, 2 * half + LANES, 2 * half + 2 * LANES, 2 * half + 2 * LANES + part, 3 * half + 2 * LANES + part],
        axis=2,
    )
    own_shared = jnp.concatenate([maps, down_in, up_out], axis=2)
    other_shared = swapped(own_shared)
    in_order = [jnp.where(core == m, own_shared, other_shared) for m in range(halves)]
    maps, down_in, up_out = (
        [entry[:, :, first:last] for entry in in_order]
        for first, last in ((0, LANES), (LANES, LANES + part), (LANES + part, LANES + 2 * part))
    )
    shared_gradient = jnp.concatenate([*down_in, *maps, *up_out], axis=2).reshape(adapter_shared.shape)
    broad_gradient = jnp.concatenate([zx, down_out], axis=2).reshape(adapter_broad.shape)
    step_gradient = lax.dynamic_slice_in_dim(steps, core * heads_local, heads_local, 2).reshape(adapter_step.shape)
    local_sq = (
        jnp.sum(broad_gradient * broad_gradient)
        + jnp.sum(step_gradient * step_gradient)
        + jnp.sum(own_shared * own_shared)
    )
    squares = jnp.broadcast_to(local_sq, (8, LANES))
    squares = squares + swapped(squares)
    total_sq = squares
    for distance in range(1, owners):
        total_sq = total_sq + moved(squares, "dp", distance, True)
    grad_norm = jnp.sqrt(total_sq[0, 0])
    scale_factor = clip_max / jnp.maximum(grad_norm, clip_max)
    revised_broad, fresh_first_broad, fresh_square_broad = adamw_update(
        adapter_broad, broad_gradient, broad_first_moment, broad_second_moment, scale_factor
    )
    revised_step, fresh_first_step, fresh_square_step = adamw_update(
        adapter_step, step_gradient, step_first_moment, step_second_moment, scale_factor
    )
    revised_shared, fresh_first_shared, fresh_square_shared = adamw_update(
        adapter_shared, shared_gradient, shared_first_moment, shared_second_moment, scale_factor
    )

    def both(values):
        other = swapped(values)
        return jnp.stack([jnp.where(core == m, values, other) for m in range(halves)])[:, None]

    return (
        both(mixed_own),
        both(upstream),
        grad_norm,
        revised_broad,
        revised_step,
        revised_shared,
        fresh_first_broad,
        fresh_first_step,
        fresh_first_shared,
        fresh_square_broad,
        fresh_square_step,
        fresh_square_shared,
        revised_broad.astype(low),
        revised_step.astype(low),
        revised_shared.astype(low),
    )


def solution(mesh):
    placed = (
        P(None, "dp", "seq", None),
        P(None, "dp", "seq", None),
        P(None, "dp", None),
        P(None, "dp", None),
        P(),
        P(None, "dp", None, "mp"),
        P(None, "dp", None),
        P(None, "dp", "mp"),
        P(None, "mp", "dp"),
        P(None, None, "mp"),
        P(),
        P(None, None, "mp"),
        P(None, "mp"),
        P(None, "dp", None, None, "mp"),
        P(None, "dp", None, "mp"),
        P(None, "dp", None, None),
        P(None, "dp", None, None, "mp"),
        P(None, "dp", None, "mp"),
        P(None, "dp", None, None),
        P(None, "dp", None, None, "mp"),
        P(None, "dp", None, "mp"),
        P(None, "dp", None, None),
    )
    return jax.shard_map(
        per_device,
        mesh=mesh,
        in_specs=placed,
        out_specs=(
            P(None, "dp", "seq", None),
            P(None, "dp", "seq", None),
            P(),
            P(None, "dp", None, None, "mp"),
            P(None, "dp", None, "mp"),
            P(None, "dp", None, None),
            P(None, "dp", None, None, "mp"),
            P(None, "dp", None, "mp"),
            P(None, "dp", None, None),
            P(None, "dp", None, None, "mp"),
            P(None, "dp", None, "mp"),
            P(None, "dp", None, None),
            P(None, "dp", None, None, "mp"),
            P(None, "dp", None, "mp"),
            P(None, "dp", None, None),
        ),
        check_vma=False,
    )
```

```python
import functools

import jax
import jax.numpy as jnp
from jax import lax
from jax.experimental import pallas as pl
from jax.experimental.pallas import tpu as pltpu
from jax.sharding import PartitionSpec as P

CONV = 4
STEP = 10
LANES = 128
SPAN = 128
PAD = 8
RESET = -128.0

norm_eps = 1e-05
learn_rate = 0.04
beta_one = 0.5
beta_two = 0.5
weight_decay = 0.01
adam_eps = 1e-08
clip_max = 1.0
low = jnp.bfloat16
full = jnp.float32


def nn(a, b):
    return lax.dot_general(a, b, (((1,), (0,)), ((), ())), preferred_element_type=full)


def nt(a, b):
    return lax.dot_general(a, b, (((1,), (1,)), ((), ())), preferred_element_type=full)


def tn(a, b):
    return lax.dot_general(a, b, (((0,), (0,)), ((), ())), preferred_element_type=full)


def two_parts(values, axis):
    high = values.astype(low)
    rest = (values - high.astype(full)).astype(low)
    return jnp.concatenate([high, rest], axis=axis)


def three_parts(values, axis):
    high = values.astype(low)
    rest = values - high.astype(full)
    middle = rest.astype(low)
    last = (rest - middle.astype(full)).astype(low)
    return jnp.concatenate([high, middle, last], axis=axis)


def widen(values, spread_two):
    return nn(two_parts(values, 1), spread_two)


def per_head(values, spread_two):
    heads = spread_two[:LANES]
    high = values.astype(low)
    rest = (values - high.astype(full)).astype(low)
    return nt(high, heads) + nt(rest, heads)


def triangle(kind):
    rows = lax.broadcasted_iota(jnp.int32, (SPAN, SPAN), 0)
    columns = lax.broadcasted_iota(jnp.int32, (SPAN, SPAN), 1)
    return rows >= columns if kind == "lower" else rows <= columns


def cumulate(values, kind):
    keep = triangle(kind).astype(full).astype(low)
    return nn(jnp.concatenate([keep, keep, keep], axis=1), three_parts(values, 0))


def sigmoid(values):
    return 1.0 / (1.0 + jnp.exp(-values))


def kernel_call(body, outs, ins, scratch=(), flops=0, name=None, limit=20, scalars=0):
    moved = sum(a.size * a.dtype.itemsize for a in list(ins) + list(outs))
    whole = pl.BlockSpec(memory_space=pltpu.VMEM)
    return pl.pallas_call(
        body,
        out_shape=tuple(outs),
        in_specs=[pl.BlockSpec(memory_space=pltpu.SMEM)] * scalars + [whole] * (len(ins) - scalars),
        out_specs=tuple([whole] * len(outs)),
        scratch_shapes=list(scratch),
        compiler_params=pltpu.CompilerParams(vmem_limit_bytes=limit * 2**20),
        cost_estimate=pl.CostEstimate(flops=flops, bytes_accessed=moved, transcendentals=0),
        name=name,
    )(*ins)


def shape(dims, kind):
    return jax.ShapeDtypeStruct(dims, kind)


def assemble_kernel(owners, pieces, place, pack, *rest):
    near, far, out = rest[: owners - 1], rest[owners - 1 : -1], rest[-1]
    quarter = pack.shape[0] // pieces
    owner, piece = place[0], place[1]
    out[owner] = pack[...]
    for i in range(owners - 1):
        source = lax.rem(owner + (owners - 1 - i), owners)
        if not far:
            out[source] = near[i][...]
            continue
        out[source, pl.ds(pl.multiple_of(piece * quarter, 16), quarter)] = near[i][...]
        for j in range(pieces - 1):
            sender = lax.rem(piece + (pieces - 1 - j), pieces)
            out[source, pl.ds(pl.multiple_of(sender * quarter, 16), quarter)] = far[j][i]


def sections(ref, first, last, columns=slice(None), core=None):
    if core is not None:
        return jnp.concatenate([ref[core, d, first:last, columns] for d in range(ref.shape[1])], axis=0)
    return jnp.concatenate([ref[d, first:last, columns] for d in range(ref.shape[0])], axis=0)


def core_sections(ref, core, first, last):
    return sections(ref, first, last, slice(None), core)


class Packs:
    def __init__(self, rows, adapter_rows, half, part):
        self.width, self.adapt = (0, rows), (rows, rows + adapter_rows)
        self.ends = (rows + adapter_rows, rows + 2 * adapter_rows)
        self.x, self.maps = slice(0, half), slice(half, half + LANES)
        self.steps = slice(half + LANES, half + 2 * LANES)
        self.mixed = slice(0, half + LANES)
        self.down, self.up = slice(0, part), slice(part, 2 * part)
        base = rows + adapter_rows
        self.out, self.out_down = (base, base + rows), (base + rows, base + rows + adapter_rows)
        self.half, self.part, self.rows = half, part, rows


def step_weights(own, other, first, last, columns, local):
    lane = lax.broadcasted_iota(jnp.int32, (1, LANES), 1)
    mine = sections(own, first, last, columns).astype(full)
    theirs = sections(other, first, last, columns).astype(full)
    return jnp.where(lane < local, mine, jnp.where(lane < 2 * local, theirs, 0.0)).astype(low)


def project_rows_kernel(packs, local, core, h, gain, mask, own, other, normed_o, spread_o, rows_o, dt_o):
    values = h[...].astype(full)
    half, part = packs.half, packs.part
    scale = lax.rsqrt(jnp.mean(values * values, axis=1, keepdims=True) + norm_eps)
    normed_o[...] = (values * scale * gain[0:1]).astype(low)
    normed = normed_o[...]
    places = ((own, core[0], 0), (other, 1 - core[0], half))
    down = jnp.zeros((h.shape[0], mask.shape[1]), full)
    for ref, index, _ in places:
        columns = pl.ds(pl.multiple_of(index * part, LANES), part)
        down = down + nt(normed_o[:, columns], sections(ref, *packs.ends, packs.down))
    spread = down.astype(low) * mask[...]
    spread_o[...] = spread
    for ref, index, place in places:
        made = nn(normed, sections(ref, *packs.width, packs.mixed)) + nn(spread, sections(ref, *packs.adapt, packs.mixed))
        rows_o[:, place : place + half] = made[:, :half].astype(low)
        rows_o[:, pl.ds(pl.multiple_of(2 * half + index * LANES, LANES), LANES)] = made[:, half:].astype(low)
    w_dt = step_weights(own, other, *packs.width, packs.steps, local)
    b_dt = step_weights(own, other, *packs.adapt, packs.steps, local)
    dt_o[...] = nn(normed, w_dt) + nn(spread, b_dt)


def project_gate_kernel(packs, core, normed, spread, wide, gate_o):
    half = packs.half
    for index, place in ((core[0], 0), (1 - core[0], half)):
        gate_o[:, place : place + half] = nn(normed[...], core_sections(wide, index, *packs.width)) + nn(
            spread[...], core_sections(wide, index, *packs.adapt)
        )


def conv_chunk(ext, lags, taps, begin, columns):
    window = ext[pl.ds(begin, SPAN + PAD), columns]
    summed = taps[CONV : CONV + 1, columns] + taps[0:1, columns] * window[PAD:]
    for lag in range(1, CONV):
        same = lags[pl.ds(begin, SPAN), (lag - 1) * LANES : lag * LANES]
        summed = summed + taps[lag : lag + 1, columns] * window[PAD - lag : PAD - lag + SPAN] * same
    return summed


def fill_extended(ext, halo, rows):
    ext[0:PAD, :] = halo[...].astype(full)
    ext[PAD : PAD + rows.shape[0], :] = rows[...].astype(full)


def states_kernel(
    inner, rows, halo, taps, lags, dt_raw, table, jump, spread_two,
    act_o, xdt_o, dt_o, cum_o, flat_o, begin_o, end_o, ext, state,
):
    length = rows.shape[0]
    channels = rows.shape[1]
    fill_extended(ext, halo, rows)
    state[...] = jnp.zeros_like(state)

    def block(k, so_far):
        begin = pl.multiple_of(k * SPAN, SPAN)
        span = pl.ds(begin, SPAN)
        for c in range(0, channels, LANES):
            columns = slice(c, c + LANES)
            summed = conv_chunk(ext, lags, taps, begin, columns)
            act_o[span, columns] = (summed * sigmoid(summed)).astype(low)
        raw = dt_raw[span, :] + table[0:1, :]
        dt = jnp.maximum(raw, 0.0) + jnp.log1p(jnp.exp(-jnp.abs(raw)))
        cum = cumulate(jump[span, :] - jnp.exp(table[1:2, :]) * dt, "lower")
        dt_o[span, :] = dt
        cum_o[span, :] = cum
        flat_o[:, span] = cum.T
        total = cum[SPAN - 1 : SPAN, :]
        xdt = (act_o[span, 0:inner].astype(full) * widen(dt, spread_two[...])).astype(low)
        xdt_o[span, :] = xdt
        tail = widen(jnp.exp(total - cum), spread_two[...])
        b_map = act_o[span, inner : inner + LANES]
        begin_o[k] = state[...].astype(low)
        keep = widen(jnp.broadcast_to(jnp.exp(total), (8, LANES)), spread_two[...])[0:1]
        state[...] = state[...] * keep + tn(b_map, (xdt.astype(full) * tail).astype(low))
        return so_far + total

    total = lax.fori_loop(0, length // SPAN, block, jnp.zeros((1, LANES), full))
    put_message(end_o, state[...], total, spread_two[...])


def intra_kernel(inner, head_width, act, xdt, cum, flat, begin_state, skip, spread_two, y_o):
    length = act.shape[0]
    keep = triangle("lower")
    left = lax.broadcasted_iota(jnp.int32, (SPAN, LANES), 1) < head_width

    def block(k, carry):
        begin = pl.multiple_of(k * SPAN, SPAN)
        span = pl.ds(begin, SPAN)
        b_map = act[span, inner : inner + LANES]
        c_map = act[span, inner + LANES : inner + 2 * LANES]
        scores = nt(c_map, b_map)
        cum_now = cum[span, :]
        entry = widen(jnp.exp(cum_now), spread_two[...])
        before = nn(c_map, begin_state[k])
        for pair in range(inner // LANES):
            columns = slice(pair * LANES, (pair + 1) * LANES)
            mixing = []
            for head in (2 * pair, 2 * pair + 1):
                gap = cum_now[:, head : head + 1] - flat[head : head + 1, span]
                mixing.append((scores * jnp.exp(jnp.where(keep, gap, -1e30))).astype(low))
            x_pair = xdt[span, columns]
            nothing = jnp.zeros_like(x_pair)
            x_two = jnp.concatenate([jnp.where(left, x_pair, nothing), jnp.where(left, nothing, x_pair)], axis=0)
            intra = nn(jnp.concatenate(mixing, axis=1), x_two)
            y_o[span, columns] = (
                intra
                + entry[:, columns] * before[:, columns]
                + skip[0:1, columns] * act[span, columns].astype(full)
            ).astype(low)
        return carry

    lax.fori_loop(0, length // SPAN, block, 0)


def put_message(out, values, total, spread_two):
    out[:LANES] = values.astype(low)
    high = total.astype(low).astype(full)
    middle = (total - high).astype(low).astype(full)
    parts = jnp.concatenate([high, middle, total - high - middle, jnp.zeros((13, LANES), full)], axis=0)
    out[LANES:] = nn(parts.astype(low), spread_two[:LANES]).astype(low)


def combine(messages):
    total = messages[0][:LANES].astype(full)
    decay = 0.0
    for i in range(1, len(messages)):
        decay = decay + jnp.sum(messages[i - 1][LANES : LANES + 16].astype(full), axis=0, keepdims=True)
        total = total + messages[i][:LANES].astype(full) * jnp.exp(decay)
    return total


def output_kernel(
    packs, count, core, h, y_local, gate, act, cum, gain, mask, first_own, first_other, wide, spread_two, *rest
):
    parts, rest = rest[:count], rest[count:]
    h_o, y_o, normal_o, spread_o, coming_o = rest
    length = h.shape[0]
    half, part = packs.half, packs.part
    inner = 2 * half
    coming = combine(parts).astype(low)
    coming_o[...] = coming
    before = jnp.zeros((1, LANES), full)
    for k in range(length // SPAN):
        span = slice(k * SPAN, (k + 1) * SPAN)
        cum_now = cum[span, :]
        carry = widen(jnp.exp(cum_now + before), spread_two[...])
        before = before + cum_now[SPAN - 1 : SPAN, :]
        c_map = act[span, inner + LANES : inner + 2 * LANES]
        y = y_local[span, :].astype(full) + carry * nn(c_map, coming)
        y_o[span, :] = y.astype(low)
        z = gate[span, :]
        gated = y * z * sigmoid(z)
        scale = lax.rsqrt(jnp.mean(gated * gated, axis=1, keepdims=True) + norm_eps)
        normal_o[span, :] = (gated * scale * gain[0:1]).astype(low)
    second = jnp.zeros((length, LANES), full)
    branch = h[...].astype(full)
    for index, place in ((core[0], 0), (1 - core[0], half)):
        normal = normal_o[:, place : place + half]
        second = second + nt(normal, core_sections(wide, index, *packs.out_down))
        branch = branch + nt(normal, core_sections(wide, index, *packs.out))
    h_o[...] = branch.astype(h_o.dtype)
    spread = second.astype(low) * mask[...]
    spread_o[...] = spread
    for ref, index in ((first_own, core[0]), (first_other, 1 - core[0])):
        columns = pl.ds(pl.multiple_of(index * part, LANES), part)
        h_o[:, columns] = (h_o[:, columns] + nn(spread, sections(ref, *packs.ends, packs.up))).astype(h_o.dtype)


def output_back_kernel(
    packs, core, upstream, y, gate, normal, spread_out, act, cum, gain, mask, first_own, first_other, wide, spread_two,
    *rest,
):
    found, rest = rest[:-7], rest[-7:]
    dgate_o, dy_o, own_o, *grads_o, seconds, lows = rest
    length = y.shape[0]
    half, part = packs.half, packs.part
    inner = 2 * half
    first = grads_o[0].shape[1] - half - part
    for i in range(len(found)):
        grads_o[i][:, :first] = found[i][...]
    lows[...] = upstream[...].astype(low)
    down = jnp.zeros(seconds.shape, full)
    for i, (ref, index) in enumerate(((first_own, core[0]), (first_other, 1 - core[0]))):
        now = lows[:, pl.ds(pl.multiple_of(index * part, LANES), part)]
        down = down + nt(now, sections(ref, *packs.ends, packs.up))
        grads_o[i][:, first + half :] = tn(spread_out[...], now).astype(low)
    second = down.astype(low) * mask[...]
    seconds[...] = second
    for i in range(2):
        grads_o[i][:, first : first + half] = tn(second, normal[:, i * half : (i + 1) * half]).astype(low)
    grad = jnp.zeros((LANES, inner), full)
    before = jnp.zeros((1, LANES), full)
    for k in range(length // SPAN):
        span = slice(k * SPAN, (k + 1) * SPAN)
        up_now = lows[span, :]
        grads = []
        for index in (core[0], 1 - core[0]):
            grads.append(
                nn(up_now, core_sections(wide, index, *packs.out))
                + nn(seconds[span, :], core_sections(wide, index, *packs.out_down))
            )
        weighted = jnp.concatenate(grads, axis=1) * gain[0:1]
        y_now = y[span, :].astype(full)
        z = gate[span, :]
        sig = sigmoid(z)
        silu = z * sig
        gated = y_now * silu
        scale = lax.rsqrt(jnp.mean(gated * gated, axis=1, keepdims=True) + norm_eps)
        mean_in = jnp.mean(weighted * gated, axis=1, keepdims=True)
        grad_gated = scale * weighted - gated * (scale * scale * scale * mean_in)
        dgate_o[span, :] = (grad_gated * y_now * sig * (1.0 + z * (1.0 - sig))).astype(low)
        dy = grad_gated * silu
        dy_o[span, :] = dy.astype(low)
        cum_now = cum[span, :]
        carry = widen(jnp.exp(cum_now + before), spread_two[...])
        before = before + cum_now[SPAN - 1 : SPAN, :]
        grad = grad + tn(act[span, inner + LANES : inner + 2 * LANES], (carry * dy).astype(low))
    put_message(own_o, grad, before, spread_two[...])


def intra_back_kernel(inner, head_width, act, xdt, dy, cum, flat, u_o, db_o, dc_o):
    length = act.shape[0]
    keep = triangle("upper")
    left = lax.broadcasted_iota(jnp.int32, (SPAN, LANES), 1) < head_width

    def block(k, carry):
        begin = pl.multiple_of(k * SPAN, SPAN)
        span = pl.ds(begin, SPAN)
        b_map = act[span, inner : inner + LANES]
        c_map = act[span, inner + LANES : inner + 2 * LANES]
        scores = nt(b_map, c_map)
        cum_now = cum[span, :]
        dscores = jnp.zeros((SPAN, SPAN), full)
        for pair in range(inner // LANES):
            columns = slice(pair * LANES, (pair + 1) * LANES)
            dy_pair = dy[span, columns]
            nothing = jnp.zeros_like(dy_pair)
            dy_two = jnp.concatenate([jnp.where(left, dy_pair, nothing), jnp.where(left, nothing, dy_pair)], axis=0)
            products = nt(xdt[span, columns], dy_two)
            mixing = []
            for i, head in enumerate((2 * pair, 2 * pair + 1)):
                gap = flat[head : head + 1, span] - cum_now[:, head : head + 1]
                decay = jnp.exp(jnp.where(keep, gap, -1e30))
                mixing.append((scores * decay).astype(low))
                dscores = dscores + products[:, i * SPAN : (i + 1) * SPAN] * decay
            u_o[span, columns] = nn(jnp.concatenate(mixing, axis=1), dy_two).astype(low)
        dlow = dscores.astype(low)
        db_o[span, :] = nn(dlow, c_map)
        dc_o[span, :] = tn(dlow, b_map)
        return carry

    lax.fori_loop(0, length // SPAN, block, 0)


def scan_back_kernel(
    inner, count, rows, halo, taps, lags, act, xdt, dy, y, u, db_in, dc_in, dt, cum, dt_raw, table, skip,
    begin_state, coming, spread_two, *rest,
):
    parts, rest = rest[:count], rest[count:]
    dconv_o, ddt_o, ext, grad, dact = rest
    length = act.shape[0]
    channels = rows.shape[1]
    blocks = length // SPAN
    fill_extended(ext, halo, rows)
    grad[...] = combine(parts)
    ends = [cum[(k + 1) * SPAN - 1 : (k + 1) * SPAN, :] for k in range(blocks)]
    for k in reversed(range(blocks)):
        span = slice(k * SPAN, (k + 1) * SPAN)
        cum_now = cum[span, :]
        total = ends[k]
        before = sum(ends[:k], jnp.zeros((1, LANES), full))
        b_map = act[span, inner : inner + LANES]
        c_map = act[span, inner + LANES : inner + 2 * LANES]
        grad_low = grad[...].astype(low)
        tail = widen(jnp.exp(total - cum_now), spread_two[...])
        entry = widen(jnp.exp(cum_now), spread_two[...])
        rows_wide = widen(jnp.exp(jnp.concatenate([total, before] * 4, axis=0)), spread_two[...])
        keep, carry = rows_wide[0:1], rows_wide[1:2]
        x = act[span, 0:inner].astype(full)
        x_dt = xdt[span, :].astype(full)
        from_later = tail * nn(b_map, grad_low)
        v = u[span, :].astype(full) + from_later
        state = begin_state[k].astype(full) + carry * coming[...].astype(full)
        dy_now = dy[span, :].astype(full)
        db = db_in[span, :] + nt((x_dt * tail).astype(low), grad_low)
        entry_dy = (entry * dy_now).astype(low)
        dc = dc_in[span, :] + nt(entry_dy, state.astype(low))
        kept = keep * grad[...]
        end_rows = jnp.sum(x_dt * from_later, axis=0, keepdims=True) + jnp.sum(kept * state, axis=0, keepdims=True)
        grad[...] = kept + tn(c_map, entry_dy)
        y_scan = y[span, :].astype(full) - skip[0:1, :] * x
        dcum = per_head(dy_now * y_scan - x_dt * v, spread_two[...])
        at_end = per_head(jnp.broadcast_to(end_rows, (8, inner)), spread_two[...])[0:1]
        ddecay = cumulate(dcum, "upper") + at_end
        raw = dt_raw[span, :] + table[0:1, :]
        ddt = per_head(x * v, spread_two[...]) - ddecay * jnp.exp(table[1:2, :])
        ddt_o[span, :] = (ddt * sigmoid(raw)).astype(low)
        dact[span, 0:inner] = widen(dt[span, :], spread_two[...]) * v + skip[0:1, :] * dy_now
        dact[span, inner : inner + LANES] = db
        dact[span, inner + LANES : inner + 2 * LANES] = dc
        for c in range(0, channels, LANES):
            columns = slice(c, c + LANES)
            summed = conv_chunk(ext, lags, taps, k * SPAN, columns)
            sig = sigmoid(summed)
            dconv_o[span, columns] = (dact[span, columns] * sig * (1.0 + summed * (1.0 - sig))).astype(low)


def gate_back_kernel(packs, core, dgate, spread, wide, dn_o, dl_o, grad_o):
    half = packs.half
    dn = dl = 0.0
    for i, index in enumerate((core[0], 1 - core[0])):
        piece = dgate[:, i * half : (i + 1) * half]
        dn = dn + nt(piece, core_sections(wide, index, *packs.width))
        dl = dl + nt(piece, core_sections(wide, index, *packs.adapt))
        grad_o[i] = tn(spread[...], piece).astype(grad_o.dtype)
    dn_o[...] = dn
    dl_o[...] = dl


def project_back_kernel(
    packs, local, core, upstream, h, gain, mask, dconv, after, taps, leads, ddt, dn_in, dl_in, spread, normed, own, other,
    *rest,
):
    found, rest = rest[:-6], rest[-6:]
    dh_o, *grads_o, ext, drows, dn_s = rest
    gate_grad, found = found[0], found[1:]
    length = h.shape[0]
    channels = dconv.shape[1]
    half, part = packs.half, packs.part
    ext[0:length, :] = dconv[...].astype(full)
    ext[length : length + PAD, :] = after[...].astype(full)

    def block(k, carry):
        begin = pl.multiple_of(k * SPAN, SPAN)
        span = pl.ds(begin, SPAN)
        for c in range(0, channels, LANES):
            columns = slice(c, c + LANES)
            window = ext[pl.ds(begin, SPAN + PAD), columns]
            total = taps[0:1, columns] * window[:SPAN]
            for lag in range(1, CONV):
                same = leads[span, (lag - 1) * LANES : lag * LANES]
                total = total + taps[lag : lag + 1, columns] * window[lag : lag + SPAN] * same
            drows[span, columns] = total.astype(low)
        return carry

    lax.fori_loop(0, length // SPAN, block, 0)
    step = ddt[...]
    dn = dn_in[...] + nt(step, step_weights(own, other, *packs.width, packs.steps, local))
    dl = dl_in[...] + nt(step, step_weights(own, other, *packs.adapt, packs.steps, local))
    step_grad = tn(spread[...], step)
    places = ((own, core[0]), (other, 1 - core[0]))
    for i, (ref, index) in enumerate(places):
        maps = drows[:, pl.ds(pl.multiple_of(2 * half + index * LANES, LANES), LANES)]
        piece = jnp.concatenate([drows[:, i * half : (i + 1) * half], maps], axis=1)
        dn = dn + nt(piece, sections(ref, *packs.width, packs.mixed))
        dl = dl + nt(piece, sections(ref, *packs.adapt, packs.mixed))
        grad_o = grads_o[i]
        grad_o[:, :half] = gate_grad[i]
        grad_o[:, half : 2 * half + LANES] = tn(spread[...], piece).astype(low)
        turned = step_grad if i == 0 else pltpu.roll(step_grad, LANES - local, 1)
        grad_o[:, 2 * half + LANES : 2 * half + 2 * LANES] = turned.astype(low)
    back = dl.astype(low) * mask[...]
    dn_s[...] = dn
    for i, (ref, index) in enumerate(places):
        columns = pl.ds(pl.multiple_of(index * part, LANES), part)
        begin = 2 * half + 2 * LANES
        grads_o[i][:, begin : begin + part] = tn(back, normed[:, columns]).astype(low)
        if found:
            grads_o[i][:, begin + part :] = found[i][...]
        dn_s[:, columns] = dn_s[:, columns] + nn(back, sections(ref, *packs.ends, packs.down))
    dn = dn_s[...]
    values = h[...].astype(full)
    scale = lax.rsqrt(jnp.mean(values * values, axis=1, keepdims=True) + norm_eps)
    weighted = dn * gain[0:1]
    mean_in = jnp.mean(weighted * values, axis=1, keepdims=True)
    dh = upstream[...].astype(full) + scale * weighted - values * (scale * scale * scale * mean_in)
    dh_o[...] = dh.astype(dh_o.dtype)


def moved(block, axis, distance, wrap=False):
    count = lax.axis_size(axis)
    route = [(i, (i + distance) % count) for i in range(count) if wrap or 0 <= i + distance < count]
    return lax.ppermute(block, axis, route)


def swapped(block):
    count = lax.axis_size("mp")
    return lax.ppermute(block, "mp", [(i, count - 1 - i) for i in range(count)])


def over_mp(own, other):
    return (own.astype(full) + swapped(other).astype(full)).astype(low)


def over_dp(both):
    owners, place = lax.axis_size("dp"), lax.axis_index("dp")
    count = both.shape[0] // owners
    total = lax.dynamic_slice_in_dim(both, place * count, count, 0).astype(full)
    for distance in range(1, owners):
        share = lax.dynamic_slice_in_dim(both, (place + distance) % owners * count, count, 0)
        total = total + moved(share, "dp", distance, True).astype(full)
    return total.astype(low)


def over_seq(total):
    result = total.astype(full)
    for distance in range(1, lax.axis_size("seq")):
        result = result + moved(total, "seq", distance, True).astype(full)
    return result


def adamw_update(param_now, gradient, moment_now, square_now, scale_factor):
    gradient = gradient * scale_factor
    first_mom = beta_one * moment_now + (1.0 - beta_one) * gradient
    second_mom = beta_two * square_now + (1.0 - beta_two) * gradient * gradient
    update = (
        first_mom
        / (1.0 - beta_one**STEP)
        / (jnp.sqrt(second_mom / (1.0 - beta_two**STEP)) + adam_eps)
    )
    param_new = param_now - learn_rate * (update + weight_decay * param_now)
    return (param_new, first_mom, second_mom)


def rows_of(values, count=PAD):
    return jnp.concatenate([values, jnp.zeros((count - values.shape[0],) + values.shape[1:], values.dtype)], axis=0)


def per_device(
    tokens,
    output_cotangent,
    document_numbers,
    document_adapter,
    input_norm_gain,
    gate_head_projection,
    map_projection,
    step_projection,
    output_projection,
    head_conv_taps,
    map_conv_taps,
    head_settings,
    gated_norm_gain,
    adapter_broad,
    adapter_step,
    adapter_shared,
    broad_first_moment,
    step_first_moment,
    shared_first_moment,
    broad_second_moment,
    step_second_moment,
    shared_second_moment,
):
    halves = lax.axis_size("mp")
    pieces = lax.axis_size("seq")
    owners = lax.axis_size("dp")
    core = lax.axis_index("mp")
    place = lax.axis_index("seq")
    length, width = tokens.shape[2:]
    layers, _, _, half = gate_head_projection.shape
    inner = halves * half
    heads_local = head_settings.shape[2]
    heads = halves * heads_local
    head_width = inner // heads
    own_adapters, rank = adapter_broad.shape[1:3]
    own_rows = own_adapters * rank
    adapters = own_adapters * owners
    ranks = adapters * rank
    part = width // halves
    states = map_projection.shape[2] // 2
    channels = inner + 2 * states

    def mine(values):
        return lax.dynamic_index_in_dim(values, core, 0, False)

    h_first = mine(tokens)[0]
    cotangent = mine(output_cotangent)[0]
    documents = mine(document_numbers)[0]
    chosen = mine(document_adapter)[0]

    low_broad = adapter_broad.astype(low)
    low_step = adapter_step.astype(low)
    low_shared = adapter_shared.astype(low)
    rows_own = gate_head_projection.shape[1]
    packs = Packs(rows_own, own_rows, half, part)
    spots = jnp.stack([lax.axis_index("dp"), place]).astype(jnp.int32)
    core_in = jnp.full((1,), core, jnp.int32)

    def twice(values):
        room = jnp.zeros(values.shape[:-1] + (LANES - 2 * values.shape[-1],), values.dtype)
        return jnp.concatenate([values, values, room], axis=-1)

    def packed(layer):
        zx = gate_head_projection[layer]
        broad = low_broad[layer].reshape(own_rows, 3, half)
        shared = low_shared[layer].reshape(own_rows, -1)
        maps = lax.dynamic_slice_in_dim(map_projection[layer], core * states, states, 1)
        maps_up = lax.dynamic_slice_in_dim(shared, width + core * states, states, 1)
        down = lax.dynamic_slice_in_dim(shared, core * part, part, 1)
        up = lax.dynamic_slice_in_dim(shared, width + 2 * states + core * part, part, 1)
        first = jnp.concatenate(
            [
                jnp.concatenate([zx[:, 1], maps, twice(step_projection[layer])], axis=1),
                jnp.concatenate([broad[:, 1], maps_up, twice(low_step[layer].reshape(own_rows, heads_local))], axis=1),
                jnp.concatenate([down, up, jnp.zeros((own_rows, half + 2 * LANES - 2 * part), low)], axis=1),
            ],
            axis=0,
        )
        second = jnp.concatenate([zx[:, 0], broad[:, 0], output_projection[layer].T, broad[:, 2]], axis=0)
        return first, second

    def ordered(values, after):
        return values if after is None else lax.optimization_barrier((values, after))[0]

    def sent(pack, quartered, after):
        quarter = pack.shape[0] // pieces
        if quarter % 16 or pack.shape[0] % pieces or owners == 1 or pieces == 1:
            return ordered(pack, after), None
        if quartered:
            mine_now = lax.dynamic_slice_in_dim(pack, place * quarter, quarter, 0)
        else:
            mine_now = pack
        mine_now = ordered(mine_now, after)
        return pack, [moved(mine_now, "dp", d, True) for d in range(1, owners)]

    def passed_on(near, after):
        if near is None:
            return []
        stack = ordered(jnp.stack(near), after)
        return [moved(stack, "seq", d, True) for d in range(1, pieces)]

    def gathered(pack, near, far, after):
        if near is None:
            own = lax.all_gather(ordered(pack, after), "dp", tiled=False)
        else:
            own = kernel_call(
                functools.partial(assemble_kernel, owners, pieces),
                [shape((owners,) + pack.shape, low)],
                [spots, pack, *ordered(near, after), *far],
                scalars=1,
                name="assemble",
                limit=20,
            )[0]
        return own, swapped(own)

    def last_of(messages, instead):
        return messages[-1] if messages else instead

    def over_cores(values):
        return jnp.concatenate([values, swapped(values)], axis=values.ndim - 1)

    widths = over_cores(jnp.concatenate([head_conv_taps, gated_norm_gain[:, None]], axis=1))
    taps_all = jnp.concatenate([widths[:, : CONV + 1], map_conv_taps], axis=2).astype(full)
    gains_two = widths[:, CONV + 1].astype(full)
    tables = over_cores(head_settings)
    head_of = jnp.arange(inner)[None, :] // head_width
    spread_one = (jnp.arange(LANES)[:, None] == head_of).astype(low)
    spread_two = jnp.concatenate([spread_one, spread_one], axis=0)

    begin = place * length
    ends = jnp.concatenate([jnp.full((PAD,), -1, jnp.int32), documents, jnp.full((PAD,), -2, jnp.int32)])
    near = lax.dynamic_slice_in_dim(ends, begin, length + 2 * PAD)
    own = near[PAD : PAD + length]
    jump = jnp.where(own != near[PAD - 1 : PAD - 1 + length], RESET, 0.0).astype(full)
    jump = jnp.broadcast_to(jump[:, None], (length, LANES))

    def same_as(lag):
        same = (own == near[PAD + lag : PAD + lag + length]).astype(full)
        return jnp.broadcast_to(same[:, None], (length, LANES))

    lags = jnp.concatenate([same_as(-lag) for lag in range(1, CONV)], axis=1)
    leads = jnp.concatenate([same_as(lag) for lag in range(1, CONV)], axis=1)
    which = jnp.arange(ranks)[None, :] // rank
    mask = jnp.zeros((length, ranks), jnp.bool_)
    for document in range(chosen.shape[0]):
        mask = mask | ((own == document)[:, None] & (which == chosen[document]))
    mask = mask.astype(low)

    tables_of = []
    for layer in range(layers):
        tables_of.append(
            (
                rows_of(input_norm_gain[layer].astype(full)[None]),
                rows_of(taps_all[layer]),
                rows_of(gains_two[layer][None]),
                rows_of(jnp.pad(tables[layer], ((0, 0), (0, LANES - heads)))),
                rows_of(jnp.repeat(tables[layer][2], head_width)[None]),
            )
        )
    prepared = (tables_of, spread_two, lags, leads, jump, mask, h_first, cotangent)

    packs_of = [packed(layer) for layer in range(layers)]
    flights = {0: sent(packs_of[0][0], True, None)}
    before = flights[0][1]
    for layer in range(1, layers):
        flights[2 * layer] = sent(packs_of[layer][0], True, before)
        before = flights[2 * layer][1]
    weights = {0: gathered(*flights[0], passed_on(flights[0][1], None), (before, prepared))}

    def gathered_both(pack, after):
        return lax.all_gather(ordered(pack, after), ("mp", "dp")).reshape((halves, owners) + pack.shape)

    weights[1] = gathered_both(packs_of[0][1], flights[0][1])

    flops_in = 2 * length * width * (2 * inner + 3 * LANES)
    flops_out = 2 * length * width * inner
    flops_scan = 4 * length * SPAN * inner

    h = h_first
    kept = []
    for layer in range(layers):
        first_own, first_other = weights[2 * layer]
        gain, taps, gain_two, table, skip = tables_of[layer]
        normed, spread, rows, dt_raw = kernel_call(
            functools.partial(project_rows_kernel, packs, heads_local),
            [
                shape((length, width), low),
                shape((length, ranks), low),
                shape((length, channels), low),
                shape((length, LANES), full),
            ],
            [core_in, h, gain, mask, first_own, first_other],
            scalars=1,
            flops=flops_in // 2,
            name="project_rows",
        )
        halo = moved(rows[length - PAD :], "seq", 1)
        act, xdt, dt, cum, flat, begin_state, end_state = kernel_call(
            functools.partial(states_kernel, inner),
            [
                shape((length, channels), low),
                shape((length, inner), low),
                shape((length, LANES), full),
                shape((length, LANES), full),
                shape((LANES, length), full),
                shape((length // SPAN, states, inner), low),
                shape((states + 16, inner), low),
            ],
            [rows, halo, taps, lags, dt_raw, table, jump, spread_two],
            scratch=[pltpu.VMEM((length + PAD, channels), full), pltpu.VMEM((states, inner), full)],
            flops=flops_scan,
            name="states",
        )
        arrived = [moved(end_state, "seq", d) for d in range(1, pieces)]
        y_local = kernel_call(
            functools.partial(intra_kernel, inner, head_width),
            [shape((length, inner), low)],
            [act, xdt, cum, flat, begin_state, skip, spread_two],
            flops=flops_scan,
            name="intra",
        )[0]
        wide = weights[2 * layer + 1]
        if layer + 1 < layers:
            weights[2 * layer + 3] = gathered_both(packs_of[layer + 1][1], act)
            next_far = passed_on(flights[2 * layer + 2][1], last_of(arrived, y_local))
        gate = kernel_call(
            functools.partial(project_gate_kernel, packs),
            [shape((length, inner), full)],
            [core_in, normed, spread, wide],
            scalars=1,
            flops=flops_in // 2,
            name="project_gate",
        )[0]
        h_next, y, normal, spread_out, coming = kernel_call(
            functools.partial(output_kernel, packs, len(arrived)),
            [
                shape((length, width), full),
                shape((length, inner), low),
                shape((length, inner), low),
                shape((length, ranks), low),
                shape((states, inner), low),
            ],
            [core_in, h, y_local, gate, act, cum, gain_two, mask, first_own, first_other, wide, spread_two, *arrived],
            scalars=1,
            flops=flops_out,
            name="output",
        )
        kept.append(
            (h, gain, taps, gain_two, table, skip, normed, spread, gate, rows, halo, dt_raw, act, xdt, dt, cum, flat,
             begin_state, y, normal, spread_out, coming)
        )
        h = h_next
        if layer + 1 < layers:
            weights[2 * layer + 2] = gathered(*flights[2 * layer + 2], next_far, h)
    mixed_own = h.astype(low)

    upstream = cotangent
    found = []
    for layer in reversed(range(layers)):
        first_own, first_other = weights[2 * layer]
        wide = weights[2 * layer + 1]
        (h, gain, taps, gain_two, table, skip, normed, spread, gate, rows, halo, dt_raw, act, xdt, dt, cum, flat,
         begin_state, y, normal, spread_out, coming) = kept[layer]
        dgate, dy, own_grad, *early = kernel_call(
            functools.partial(output_back_kernel, packs),
            [
                shape((length, inner), low),
                shape((length, inner), low),
                shape((states + 16, inner), low),
                *[shape((ranks, half + part + sum(f.shape[1] for f in found[::2])), low)] * 2,
            ],
            [core_in, upstream, y, gate, normal, spread_out, act, cum, gain_two, mask, first_own, first_other, wide,
             spread_two, *found],
            scratch=[pltpu.VMEM((length, ranks), low), pltpu.VMEM((length, width), low)],
            scalars=1,
            flops=flops_out,
            name="output_back",
        )
        arrived = [moved(own_grad, "seq", -d) for d in range(1, pieces)]
        if layer == 0:
            before_last = over_mp(*early)
            early = []
        u, db, dc = kernel_call(
            functools.partial(intra_back_kernel, inner, head_width),
            [shape((length, inner), low), shape((length, LANES), full), shape((length, LANES), full)],
            [act, xdt, dy, cum, flat],
            flops=2 * flops_scan,
            name="intra_back",
        )
        dn, dl, g_gate = kernel_call(
            functools.partial(gate_back_kernel, packs),
            [shape((length, width), full), shape((length, ranks), full), shape((halves, ranks, half), low)],
            [core_in, dgate, spread, wide],
            scalars=1,
            flops=flops_in // 2,
            name="gate_back",
        )
        if layer == 0:
            before_last, arrived, u = lax.optimization_barrier((before_last, arrived, u))
        dconv, ddt = kernel_call(
            functools.partial(scan_back_kernel, inner, len(arrived)),
            [shape((length, channels), low), shape((length, LANES), low)],
            [rows, halo, taps, lags, act, xdt, dy, y, u, db, dc, dt, cum, dt_raw, table, skip, begin_state, coming,
             spread_two, *arrived],
            scratch=[
                pltpu.VMEM((length + PAD, channels), full),
                pltpu.VMEM((states, inner), full),
                pltpu.VMEM((length, channels), full),
            ],
            flops=2 * flops_scan,
            name="scan_back",
        )
        after = moved(dconv[:PAD], "seq", -1)
        if layer == 0:
            before_last = over_dp(before_last)
            dconv = ordered(dconv, before_last)
            before_last = over_seq(ordered(before_last, after))
        dh, *found = kernel_call(
            functools.partial(project_back_kernel, packs, heads_local),
            [
                shape((length, width), full if layer > 0 else low),
                *[shape((ranks, 2 * half + 2 * LANES + part + sum(e.shape[1] for e in early[:1])), low)] * 2,
            ],
            [core_in, upstream, h, gain, mask, dconv, after, taps, leads, ddt, dn, dl, spread, normed, first_own,
             first_other, g_gate, *early],
            scratch=[
                pltpu.VMEM((length + PAD, channels), full),
                pltpu.VMEM((length, channels), low),
                pltpu.VMEM((length, width), full),
            ],
            scalars=1,
            flops=flops_in // 2,
            name="project_back",
        )
        upstream = dh

    last = over_seq(over_dp(over_mp(*ordered(found, before_last))))
    columns = 3 * half + 2 * LANES + 2 * part
    every = jnp.concatenate([last, before_last[:, (layers - 1) * columns :], before_last[:, : (layers - 1) * columns]], axis=1)
    whole = jnp.stack([every[:, i * columns : (i + 1) * columns] for i in range(layers)])
    zx, maps, steps, down_in, down_out, up_out = jnp.split(
        whole,
        [2 * half, 2 * half + LANES, 2 * half + 2 * LANES, 2 * half + 2 * LANES + part, 3 * half + 2 * LANES + part],
        axis=2,
    )
    own_shared = jnp.concatenate([maps, down_in, up_out], axis=2)
    other_shared = swapped(own_shared)
    in_order = [jnp.where(core == m, own_shared, other_shared) for m in range(halves)]
    maps, down_in, up_out = (
        [entry[:, :, first:last] for entry in in_order]
        for first, last in ((0, LANES), (LANES, LANES + part), (LANES + part, LANES + 2 * part))
    )
    shared_gradient = jnp.concatenate([*down_in, *maps, *up_out], axis=2).reshape(adapter_shared.shape)
    broad_gradient = jnp.concatenate([zx, down_out], axis=2).reshape(adapter_broad.shape)
    step_gradient = steps[:, :, :heads_local].reshape(adapter_step.shape)
    local_sq = (
        jnp.sum(broad_gradient * broad_gradient)
        + jnp.sum(step_gradient * step_gradient)
        + jnp.sum(own_shared * own_shared)
    )
    squares = jnp.broadcast_to(local_sq, (8, LANES))
    squares = squares + swapped(squares)
    total_sq = squares
    for distance in range(1, owners):
        total_sq = total_sq + moved(squares, "dp", distance, True)
    grad_norm = jnp.sqrt(total_sq[0, 0])
    scale_factor = clip_max / jnp.maximum(grad_norm, clip_max)
    revised_broad, fresh_first_broad, fresh_square_broad = adamw_update(
        adapter_broad, broad_gradient, broad_first_moment, broad_second_moment, scale_factor
    )
    revised_step, fresh_first_step, fresh_square_step = adamw_update(
        adapter_step, step_gradient, step_first_moment, step_second_moment, scale_factor
    )
    revised_shared, fresh_first_shared, fresh_square_shared = adamw_update(
        adapter_shared, shared_gradient, shared_first_moment, shared_second_moment, scale_factor
    )

    def both(values):
        other = swapped(values)
        return jnp.stack([jnp.where(core == m, values, other) for m in range(halves)])[:, None]

    return (
        both(mixed_own),
        both(upstream),
        grad_norm,
        revised_broad,
        revised_step,
        revised_shared,
        fresh_first_broad,
        fresh_first_step,
        fresh_first_shared,
        fresh_square_broad,
        fresh_square_step,
        fresh_square_shared,
        revised_broad.astype(low),
        revised_step.astype(low),
        revised_shared.astype(low),
    )


def solution(mesh):
    placed = (
        P(None, "dp", "seq", None),
        P(None, "dp", "seq", None),
        P(None, "dp", None),
        P(None, "dp", None),
        P(),
        P(None, "dp", None, "mp"),
        P(None, "dp", None),
        P(None, "dp", "mp"),
        P(None, "mp", "dp"),
        P(None, None, "mp"),
        P(),
        P(None, None, "mp"),
        P(None, "mp"),
        P(None, "dp", None, None, "mp"),
        P(None, "dp", None, "mp"),
        P(None, "dp", None, None),
        P(None, "dp", None, None, "mp"),
        P(None, "dp", None, "mp"),
        P(None, "dp", None, None),
        P(None, "dp", None, None, "mp"),
        P(None, "dp", None, "mp"),
        P(None, "dp", None, None),
    )
    return jax.shard_map(
        per_device,
        mesh=mesh,
        in_specs=placed,
        out_specs=(
            P(None, "dp", "seq", None),
            P(None, "dp", "seq", None),
            P(),
            P(None, "dp", None, None, "mp"),
            P(None, "dp", None, "mp"),
            P(None, "dp", None, None),
            P(None, "dp", None, None, "mp"),
            P(None, "dp", None, "mp"),
            P(None, "dp", None, None),
            P(None, "dp", None, None, "mp"),
            P(None, "dp", None, "mp"),
            P(None, "dp", None, None),
            P(None, "dp", None, None, "mp"),
            P(None, "dp", None, "mp"),
            P(None, "dp", None, None),
        ),
        check_vma=False,
    )
```

```python
import functools

import jax
import jax.numpy as jnp
import numpy as np
from jax import lax
from jax.experimental import pallas as pl
from jax.experimental.pallas import tpu as pltpu
from jax.sharding import PartitionSpec as P

CONV = 4
STEP = 10
LANES = 128
SPAN = 128
PAD = 8
RESET = -128.0
GAIN_TWO, SKIP, GAIN, STEP_BIAS, DECAY, TABLE_ROWS = 5, 6, 7, 8, 9, 16

norm_eps = 1e-05
learn_rate = 0.04
beta_one = 0.5
beta_two = 0.5
weight_decay = 0.01
adam_eps = 1e-08
clip_max = 1.0
low = jnp.bfloat16
full = jnp.float32


def nn(a, b):
    return lax.dot_general(a, b, (((1,), (0,)), ((), ())), preferred_element_type=full)


def nt(a, b):
    return lax.dot_general(a, b, (((1,), (1,)), ((), ())), preferred_element_type=full)


def tn(a, b):
    return lax.dot_general(a, b, (((0,), (0,)), ((), ())), preferred_element_type=full)


def two_parts(values, axis):
    high = values.astype(low)
    rest = (values - high.astype(full)).astype(low)
    return jnp.concatenate([high, rest], axis=axis)


def three_parts(values, axis):
    high = values.astype(low)
    rest = values - high.astype(full)
    middle = rest.astype(low)
    last = (rest - middle.astype(full)).astype(low)
    return jnp.concatenate([high, middle, last], axis=axis)


def widen(values, spread_two):
    return nn(two_parts(values, 1), spread_two)


def per_head(values, spread_two):
    heads = spread_two[:LANES]
    high = values.astype(low)
    rest = (values - high.astype(full)).astype(low)
    return nt(high, heads) + nt(rest, heads)


def triangle(kind):
    rows = lax.broadcasted_iota(jnp.int32, (SPAN, SPAN), 0)
    columns = lax.broadcasted_iota(jnp.int32, (SPAN, SPAN), 1)
    return rows >= columns if kind == "lower" else rows <= columns


def cumulate(values, kind):
    keep = triangle(kind).astype(full).astype(low)
    return nn(jnp.concatenate([keep, keep, keep], axis=1), three_parts(values, 0))


def sigmoid(values):
    return 1.0 / (1.0 + jnp.exp(-values))


def kernel_call(body, outs, ins, scratch=(), flops=0, name=None, limit=20, scalars=0):
    moved = sum(a.size * a.dtype.itemsize for a in list(ins) + list(outs))
    whole = pl.BlockSpec(memory_space=pltpu.VMEM)
    return pl.pallas_call(
        body,
        out_shape=tuple(outs),
        in_specs=[pl.BlockSpec(memory_space=pltpu.SMEM)] * scalars + [whole] * (len(ins) - scalars),
        out_specs=tuple([whole] * len(outs)),
        scratch_shapes=list(scratch),
        compiler_params=pltpu.CompilerParams(vmem_limit_bytes=limit * 2**20),
        cost_estimate=pl.CostEstimate(flops=flops, bytes_accessed=moved, transcendentals=0),
        name=name,
    )(*ins)


def shape(dims, kind):
    return jax.ShapeDtypeStruct(dims, kind)


def assemble_kernel(owners, pieces, place, pack, *rest):
    near, far, out = rest[: owners - 1], rest[owners - 1 : -1], rest[-1]
    quarter = pack.shape[0] // pieces
    owner, piece = place[0], place[1]
    out[owner] = pack[...]
    for i in range(owners - 1):
        source = lax.rem(owner + (owners - 1 - i), owners)
        if not far:
            out[source] = near[i][...]
            continue
        out[source, pl.ds(pl.multiple_of(piece * quarter, 16), quarter)] = near[i][...]
        for j in range(pieces - 1):
            sender = lax.rem(piece + (pieces - 1 - j), pieces)
            out[source, pl.ds(pl.multiple_of(sender * quarter, 16), quarter)] = far[j][i]


def sections(ref, first, last, columns=slice(None), core=None):
    if core is not None:
        return jnp.concatenate([ref[core, d, first:last, columns] for d in range(ref.shape[1])], axis=0)
    return jnp.concatenate([ref[d, first:last, columns] for d in range(ref.shape[0])], axis=0)


def core_sections(ref, core, first, last):
    return sections(ref, first, last, slice(None), core)


class Packs:
    def __init__(self, rows, adapter_rows, half, part):
        self.width, self.adapt = (0, rows), (rows, rows + adapter_rows)
        self.ends = (rows + adapter_rows, rows + 2 * adapter_rows)
        self.x, self.maps = slice(0, half), slice(half, half + LANES)
        self.steps = slice(half + LANES, half + 2 * LANES)
        self.mixed = slice(0, half + LANES)
        self.down, self.up = slice(0, part), slice(part, 2 * part)
        base = rows + adapter_rows
        self.out, self.out_down = (base, base + rows), (base + rows, base + rows + adapter_rows)
        self.half, self.part, self.rows = half, part, rows


def step_weights(own, other, first, last, columns, local):
    lane = lax.broadcasted_iota(jnp.int32, (1, LANES), 1)
    mine = sections(own, first, last, columns).astype(full)
    theirs = sections(other, first, last, columns).astype(full)
    return jnp.where(lane < local, mine, jnp.where(lane < 2 * local, theirs, 0.0)).astype(low)


def project_rows_kernel(packs, local, layer, core, h, tables, mask, own, other, normed_o, spread_o, rows_o, dt_o):
    values = h[...].astype(full)
    half, part = packs.half, packs.part
    scale = lax.rsqrt(jnp.mean(values * values, axis=1, keepdims=True) + norm_eps)
    normed_o[...] = (values * scale * tables[layer, GAIN : GAIN + 1, : h.shape[1]]).astype(low)
    normed = normed_o[...]
    places = ((own, core[0], 0), (other, 1 - core[0], half))
    down = jnp.zeros((h.shape[0], mask.shape[1]), full)
    for ref, index, _ in places:
        columns = pl.ds(pl.multiple_of(index * part, LANES), part)
        down = down + nt(normed_o[:, columns], sections(ref, *packs.ends, packs.down))
    spread = down.astype(low) * mask[...]
    spread_o[...] = spread
    for ref, index, place in places:
        made = nn(normed, sections(ref, *packs.width, packs.mixed)) + nn(spread, sections(ref, *packs.adapt, packs.mixed))
        rows_o[:, place : place + half] = made[:, :half].astype(low)
        rows_o[:, pl.ds(pl.multiple_of(2 * half + index * LANES, LANES), LANES)] = made[:, half:].astype(low)
    w_dt = step_weights(own, other, *packs.width, packs.steps, local)
    b_dt = step_weights(own, other, *packs.adapt, packs.steps, local)
    dt_o[...] = nn(normed, w_dt) + nn(spread, b_dt)


def project_gate_kernel(packs, core, normed, spread, wide, gate_o):
    half = packs.half
    for index, place in ((core[0], 0), (1 - core[0], half)):
        gate_o[:, place : place + half] = nn(normed[...], core_sections(wide, index, *packs.width)) + nn(
            spread[...], core_sections(wide, index, *packs.adapt)
        )


def conv_chunk(ext, same, taps, begin, columns):
    window = ext[pl.ds(begin, SPAN + PAD), columns]
    summed = taps[CONV : CONV + 1, columns] + taps[0:1, columns] * window[PAD:]
    for lag in range(1, CONV):
        summed = summed + taps[lag : lag + 1, columns] * window[PAD - lag : PAD - lag + SPAN] * same[lag - 1]
    return summed


def same_documents(front, span):
    return [front[span, i * LANES : (i + 1) * LANES].astype(full) for i in range(CONV - 1)]


def fill_extended(ext, halo, rows):
    ext[0:PAD, :] = halo[...].astype(full)
    ext[PAD : PAD + rows.shape[0], :] = rows[...].astype(full)


def states_kernel(
    inner, layer, rows, halo, tables, front, dt_raw, spread_two,
    act_o, xdt_o, dt_o, cum_o, flat_o, begin_o, end_o, ext, state,
):
    length = rows.shape[0]
    channels = rows.shape[1]
    table = tables.at[layer]
    fill_extended(ext, halo, rows)
    state[...] = jnp.zeros_like(state)

    def block(k, so_far):
        begin = pl.multiple_of(k * SPAN, SPAN)
        span = pl.ds(begin, SPAN)
        same = same_documents(front, span)
        for c in range(0, channels, LANES):
            columns = slice(c, c + LANES)
            summed = conv_chunk(ext, same, table, begin, columns)
            act_o[span, columns] = (summed * sigmoid(summed)).astype(low)
        raw = dt_raw[span, :] + table[STEP_BIAS : STEP_BIAS + 1, :LANES]
        dt = jnp.maximum(raw, 0.0) + jnp.log1p(jnp.exp(-jnp.abs(raw)))
        jump = front[span, (CONV - 1) * LANES :].astype(full)
        cum = cumulate(jump - jnp.exp(table[DECAY : DECAY + 1, :LANES]) * dt, "lower")
        dt_o[span, :] = dt
        cum_o[span, :] = cum
        flat_o[:, span] = cum.T
        total = cum[SPAN - 1 : SPAN, :]
        xdt = (act_o[span, 0:inner].astype(full) * widen(dt, spread_two[...])).astype(low)
        xdt_o[span, :] = xdt
        tail = widen(jnp.exp(total - cum), spread_two[...])
        b_map = act_o[span, inner : inner + LANES]
        begin_o[k] = state[...].astype(low)
        keep = widen(jnp.broadcast_to(jnp.exp(total), (8, LANES)), spread_two[...])[0:1]
        state[...] = state[...] * keep + tn(b_map, (xdt.astype(full) * tail).astype(low))
        return so_far + total

    total = lax.fori_loop(0, length // SPAN, block, jnp.zeros((1, LANES), full))
    put_message(end_o, state[...], total, spread_two[...])


def intra_kernel(inner, head_width, layer, act, xdt, cum, flat, begin_state, tables, spread_two, y_o):
    length = act.shape[0]
    keep = triangle("lower")
    left = lax.broadcasted_iota(jnp.int32, (SPAN, LANES), 1) < head_width

    def block(k, carry):
        begin = pl.multiple_of(k * SPAN, SPAN)
        span = pl.ds(begin, SPAN)
        b_map = act[span, inner : inner + LANES]
        c_map = act[span, inner + LANES : inner + 2 * LANES]
        scores = nt(c_map, b_map)
        cum_now = cum[span, :]
        entry = widen(jnp.exp(cum_now), spread_two[...])
        before = nn(c_map, begin_state[k])
        for pair in range(inner // LANES):
            columns = slice(pair * LANES, (pair + 1) * LANES)
            mixing = []
            for head in (2 * pair, 2 * pair + 1):
                gap = cum_now[:, head : head + 1] - flat[head : head + 1, span]
                mixing.append((scores * jnp.exp(jnp.where(keep, gap, -1e30))).astype(low))
            x_pair = xdt[span, columns]
            nothing = jnp.zeros_like(x_pair)
            x_two = jnp.concatenate([jnp.where(left, x_pair, nothing), jnp.where(left, nothing, x_pair)], axis=0)
            intra = nn(jnp.concatenate(mixing, axis=1), x_two)
            y_o[span, columns] = (
                intra
                + entry[:, columns] * before[:, columns]
                + tables[layer, SKIP : SKIP + 1, columns] * act[span, columns].astype(full)
            ).astype(low)
        return carry

    lax.fori_loop(0, length // SPAN, block, 0)


def put_message(out, values, total, spread_two):
    out[:LANES] = values.astype(low)
    high = total.astype(low).astype(full)
    middle = (total - high).astype(low).astype(full)
    parts = jnp.concatenate([high, middle, total - high - middle, jnp.zeros((13, LANES), full)], axis=0)
    out[LANES:] = nn(parts.astype(low), spread_two[:LANES]).astype(low)


def combine(messages):
    total = messages[0][:LANES].astype(full)
    decay = 0.0
    for i in range(1, len(messages)):
        decay = decay + jnp.sum(messages[i - 1][LANES : LANES + 16].astype(full), axis=0, keepdims=True)
        total = total + messages[i][:LANES].astype(full) * jnp.exp(decay)
    return total


def output_kernel(
    packs, count, layer, core, h, y_local, gate, act, cum, tables, mask, first_own, first_other, wide, spread_two, *rest
):
    parts, rest = rest[:count], rest[count:]
    h_o, y_o, normal_o, spread_o, coming_o = rest
    length = h.shape[0]
    half, part = packs.half, packs.part
    inner = 2 * half
    coming = combine(parts).astype(low)
    coming_o[...] = coming
    before = jnp.zeros((1, LANES), full)
    for k in range(length // SPAN):
        span = slice(k * SPAN, (k + 1) * SPAN)
        cum_now = cum[span, :]
        carry = widen(jnp.exp(cum_now + before), spread_two[...])
        before = before + cum_now[SPAN - 1 : SPAN, :]
        c_map = act[span, inner + LANES : inner + 2 * LANES]
        y = y_local[span, :].astype(full) + carry * nn(c_map, coming)
        y_o[span, :] = y.astype(low)
        z = gate[span, :]
        gated = y * z * sigmoid(z)
        scale = lax.rsqrt(jnp.mean(gated * gated, axis=1, keepdims=True) + norm_eps)
        normal_o[span, :] = (gated * scale * tables[layer, GAIN_TWO : GAIN_TWO + 1, :inner]).astype(low)
    second = jnp.zeros((length, LANES), full)
    branch = h[...].astype(full)
    for index, place in ((core[0], 0), (1 - core[0], half)):
        normal = normal_o[:, place : place + half]
        second = second + nt(normal, core_sections(wide, index, *packs.out_down))
        branch = branch + nt(normal, core_sections(wide, index, *packs.out))
    h_o[...] = branch.astype(h_o.dtype)
    spread = second.astype(low) * mask[...]
    spread_o[...] = spread
    for ref, index in ((first_own, core[0]), (first_other, 1 - core[0])):
        columns = pl.ds(pl.multiple_of(index * part, LANES), part)
        h_o[:, columns] = (h_o[:, columns] + nn(spread, sections(ref, *packs.ends, packs.up))).astype(h_o.dtype)


def output_back_kernel(
    packs, layer, core, upstream, y, gate, normal, spread_out, act, cum, tables, mask, first_own, first_other, wide, spread_two,
    *rest,
):
    found, rest = rest[:-7], rest[-7:]
    dgate_o, dy_o, own_o, *grads_o, seconds, lows = rest
    length = y.shape[0]
    half, part = packs.half, packs.part
    inner = 2 * half
    first = grads_o[0].shape[1] - half - part
    for i in range(len(found)):
        grads_o[i][:, :first] = found[i][...]
    lows[...] = upstream[...].astype(low)
    down = jnp.zeros(seconds.shape, full)
    for i, (ref, index) in enumerate(((first_own, core[0]), (first_other, 1 - core[0]))):
        now = lows[:, pl.ds(pl.multiple_of(index * part, LANES), part)]
        down = down + nt(now, sections(ref, *packs.ends, packs.up))
        grads_o[i][:, first + half :] = tn(spread_out[...], now).astype(low)
    second = down.astype(low) * mask[...]
    seconds[...] = second
    for i in range(2):
        grads_o[i][:, first : first + half] = tn(second, normal[:, i * half : (i + 1) * half]).astype(low)
    grad = jnp.zeros((LANES, inner), full)
    before = jnp.zeros((1, LANES), full)
    for k in range(length // SPAN):
        span = slice(k * SPAN, (k + 1) * SPAN)
        up_now = lows[span, :]
        grads = []
        for index in (core[0], 1 - core[0]):
            grads.append(
                nn(up_now, core_sections(wide, index, *packs.out))
                + nn(seconds[span, :], core_sections(wide, index, *packs.out_down))
            )
        weighted = jnp.concatenate(grads, axis=1) * tables[layer, GAIN_TWO : GAIN_TWO + 1, :inner]
        y_now = y[span, :].astype(full)
        z = gate[span, :]
        sig = sigmoid(z)
        silu = z * sig
        gated = y_now * silu
        scale = lax.rsqrt(jnp.mean(gated * gated, axis=1, keepdims=True) + norm_eps)
        mean_in = jnp.mean(weighted * gated, axis=1, keepdims=True)
        grad_gated = scale * weighted - gated * (scale * scale * scale * mean_in)
        dgate_o[span, :] = (grad_gated * y_now * sig * (1.0 + z * (1.0 - sig))).astype(low)
        dy = grad_gated * silu
        dy_o[span, :] = dy.astype(low)
        cum_now = cum[span, :]
        carry = widen(jnp.exp(cum_now + before), spread_two[...])
        before = before + cum_now[SPAN - 1 : SPAN, :]
        grad = grad + tn(act[span, inner + LANES : inner + 2 * LANES], (carry * dy).astype(low))
    put_message(own_o, grad, before, spread_two[...])


def intra_back_kernel(inner, head_width, act, xdt, dy, cum, flat, u_o, db_o, dc_o):
    length = act.shape[0]
    keep = triangle("upper")
    left = lax.broadcasted_iota(jnp.int32, (SPAN, LANES), 1) < head_width

    def block(k, carry):
        begin = pl.multiple_of(k * SPAN, SPAN)
        span = pl.ds(begin, SPAN)
        b_map = act[span, inner : inner + LANES]
        c_map = act[span, inner + LANES : inner + 2 * LANES]
        scores = nt(b_map, c_map)
        cum_now = cum[span, :]
        dscores = jnp.zeros((SPAN, SPAN), full)
        for pair in range(inner // LANES):
            columns = slice(pair * LANES, (pair + 1) * LANES)
            dy_pair = dy[span, columns]
            nothing = jnp.zeros_like(dy_pair)
            dy_two = jnp.concatenate([jnp.where(left, dy_pair, nothing), jnp.where(left, nothing, dy_pair)], axis=0)
            products = nt(xdt[span, columns], dy_two)
            mixing = []
            for i, head in enumerate((2 * pair, 2 * pair + 1)):
                gap = flat[head : head + 1, span] - cum_now[:, head : head + 1]
                decay = jnp.exp(jnp.where(keep, gap, -1e30))
                mixing.append((scores * decay).astype(low))
                dscores = dscores + products[:, i * SPAN : (i + 1) * SPAN] * decay
            u_o[span, columns] = nn(jnp.concatenate(mixing, axis=1), dy_two).astype(low)
        dlow = dscores.astype(low)
        db_o[span, :] = nn(dlow, c_map)
        dc_o[span, :] = tn(dlow, b_map)
        return carry

    lax.fori_loop(0, length // SPAN, block, 0)


def scan_back_kernel(
    inner, count, layer, rows, halo, tables, front, act, xdt, dy, y, u, db_in, dc_in, dt, cum, dt_raw,
    begin_state, coming, spread_two, *rest,
):
    parts = rest[:count]
    dconv_o, ddt_o, ext, grad, dact = rest[-5:]
    length = act.shape[0]
    channels = rows.shape[1]
    blocks = length // SPAN
    table = tables.at[layer]
    skip = table[SKIP : SKIP + 1, :inner]
    fill_extended(ext, halo, rows)
    grad[...] = combine(parts)
    ends = [cum[(k + 1) * SPAN - 1 : (k + 1) * SPAN, :] for k in range(blocks)]
    for k in reversed(range(blocks)):
        span = slice(k * SPAN, (k + 1) * SPAN)
        cum_now = cum[span, :]
        total = ends[k]
        before = sum(ends[:k], jnp.zeros((1, LANES), full))
        b_map = act[span, inner : inner + LANES]
        c_map = act[span, inner + LANES : inner + 2 * LANES]
        grad_low = grad[...].astype(low)
        tail = widen(jnp.exp(total - cum_now), spread_two[...])
        entry = widen(jnp.exp(cum_now), spread_two[...])
        rows_wide = widen(jnp.exp(jnp.concatenate([total, before] * 4, axis=0)), spread_two[...])
        keep, carry = rows_wide[0:1], rows_wide[1:2]
        x = act[span, 0:inner].astype(full)
        x_dt = xdt[span, :].astype(full)
        from_later = tail * nn(b_map, grad_low)
        v = u[span, :].astype(full) + from_later
        state = begin_state[k].astype(full) + carry * coming[...].astype(full)
        dy_now = dy[span, :].astype(full)
        db = db_in[span, :] + nt((x_dt * tail).astype(low), grad_low)
        entry_dy = (entry * dy_now).astype(low)
        dc = dc_in[span, :] + nt(entry_dy, state.astype(low))
        kept = keep * grad[...]
        end_rows = jnp.sum(x_dt * from_later, axis=0, keepdims=True) + jnp.sum(kept * state, axis=0, keepdims=True)
        grad[...] = kept + tn(c_map, entry_dy)
        y_scan = y[span, :].astype(full) - skip * x
        dcum = per_head(dy_now * y_scan - x_dt * v, spread_two[...])
        at_end = per_head(jnp.broadcast_to(end_rows, (8, inner)), spread_two[...])[0:1]
        ddecay = cumulate(dcum, "upper") + at_end
        raw = dt_raw[span, :] + table[STEP_BIAS : STEP_BIAS + 1, :LANES]
        ddt = per_head(x * v, spread_two[...]) - ddecay * jnp.exp(table[DECAY : DECAY + 1, :LANES])
        ddt_o[span, :] = (ddt * sigmoid(raw)).astype(low)
        dact[span, 0:inner] = widen(dt[span, :], spread_two[...]) * v + skip * dy_now
        dact[span, inner : inner + LANES] = db
        dact[span, inner + LANES : inner + 2 * LANES] = dc
        same = same_documents(front, span)
        for c in range(0, channels, LANES):
            columns = slice(c, c + LANES)
            summed = conv_chunk(ext, same, table, k * SPAN, columns)
            sig = sigmoid(summed)
            dconv_o[span, columns] = (dact[span, columns] * sig * (1.0 + summed * (1.0 - sig))).astype(low)


def gate_back_kernel(packs, core, dgate, spread, wide, dn_o, dl_o, grad_o):
    half = packs.half
    dn = dl = 0.0
    for i, index in enumerate((core[0], 1 - core[0])):
        piece = dgate[:, i * half : (i + 1) * half]
        dn = dn + nt(piece, core_sections(wide, index, *packs.width))
        dl = dl + nt(piece, core_sections(wide, index, *packs.adapt))
        grad_o[i] = tn(spread[...], piece).astype(grad_o.dtype)
    dn_o[...] = dn
    dl_o[...] = dl


def project_back_kernel(
    packs, local, layer, core, upstream, h, tables, mask, dconv, after, leads, ddt, dn_in, dl_in, spread, normed, own, other,
    *rest,
):
    found, rest = rest[:-6], rest[-6:]
    dh_o, *grads_o, ext, drows, dn_s = rest
    gate_grad, found = found[0], found[1:3]
    length = h.shape[0]
    channels = dconv.shape[1]
    half, part = packs.half, packs.part
    ext[0:length, :] = dconv[...].astype(full)
    ext[length : length + PAD, :] = after[...].astype(full)

    def block(k, carry):
        begin = pl.multiple_of(k * SPAN, SPAN)
        span = pl.ds(begin, SPAN)
        same = same_documents(leads, span)
        for c in range(0, channels, LANES):
            columns = slice(c, c + LANES)
            window = ext[pl.ds(begin, SPAN + PAD), columns]
            total = tables[layer, 0:1, columns] * window[:SPAN]
            for lag in range(1, CONV):
                total = total + tables[layer, lag : lag + 1, columns] * window[lag : lag + SPAN] * same[lag - 1]
            drows[span, columns] = total.astype(low)
        return carry

    lax.fori_loop(0, length // SPAN, block, 0)
    step = ddt[...]
    dn = dn_in[...] + nt(step, step_weights(own, other, *packs.width, packs.steps, local))
    dl = dl_in[...] + nt(step, step_weights(own, other, *packs.adapt, packs.steps, local))
    step_grad = tn(spread[...], step)
    places = ((own, core[0]), (other, 1 - core[0]))
    for i, (ref, index) in enumerate(places):
        maps = drows[:, pl.ds(pl.multiple_of(2 * half + index * LANES, LANES), LANES)]
        piece = jnp.concatenate([drows[:, i * half : (i + 1) * half], maps], axis=1)
        dn = dn + nt(piece, sections(ref, *packs.width, packs.mixed))
        dl = dl + nt(piece, sections(ref, *packs.adapt, packs.mixed))
        grad_o = grads_o[i]
        grad_o[:, :half] = gate_grad[i]
        grad_o[:, half : 2 * half + LANES] = tn(spread[...], piece).astype(low)
        turned = step_grad if i == 0 else pltpu.roll(step_grad, LANES - local, 1)
        grad_o[:, 2 * half + LANES : 2 * half + 2 * LANES] = turned.astype(low)
    back = dl.astype(low) * mask[...]
    dn_s[...] = dn
    for i, (ref, index) in enumerate(places):
        columns = pl.ds(pl.multiple_of(index * part, LANES), part)
        begin = 2 * half + 2 * LANES
        grads_o[i][:, begin : begin + part] = tn(back, normed[:, columns]).astype(low)
        if found:
            grads_o[i][:, begin + part :] = found[i][...]
        dn_s[:, columns] = dn_s[:, columns] + nn(back, sections(ref, *packs.ends, packs.down))
    dn = dn_s[...]
    values = h[...].astype(full)
    scale = lax.rsqrt(jnp.mean(values * values, axis=1, keepdims=True) + norm_eps)
    weighted = dn * tables[layer, GAIN : GAIN + 1, : h.shape[1]]
    mean_in = jnp.mean(weighted * values, axis=1, keepdims=True)
    dh = upstream[...].astype(full) + scale * weighted - values * (scale * scale * scale * mean_in)
    dh_o[...] = dh.astype(dh_o.dtype)


def moved(block, axis, distance, wrap=False):
    count = lax.axis_size(axis)
    route = [(i, (i + distance) % count) for i in range(count) if wrap or 0 <= i + distance < count]
    return lax.ppermute(block, axis, route)


def swapped(block):
    count = lax.axis_size("mp")
    return lax.ppermute(block, "mp", [(i, count - 1 - i) for i in range(count)])


def over_mp(own, other):
    return (own.astype(full) + swapped(other).astype(full)).astype(low)


def over_dp(both):
    owners, place = lax.axis_size("dp"), lax.axis_index("dp")
    count = both.shape[0] // owners
    total = lax.dynamic_slice_in_dim(both, place * count, count, 0).astype(full)
    for distance in range(1, owners):
        share = lax.dynamic_slice_in_dim(both, (place + distance) % owners * count, count, 0)
        total = total + moved(share, "dp", distance, True).astype(full)
    return total.astype(low)


def over_seq(total):
    result = total.astype(full)
    for distance in range(1, lax.axis_size("seq")):
        result = result + moved(total, "seq", distance, True).astype(full)
    return result


def adamw_update(param_now, gradient, moment_now, square_now, scale_factor):
    gradient = gradient * scale_factor
    first_mom = beta_one * moment_now + (1.0 - beta_one) * gradient
    second_mom = beta_two * square_now + (1.0 - beta_two) * gradient * gradient
    update = (
        first_mom
        / (1.0 - beta_one**STEP)
        / (jnp.sqrt(second_mom / (1.0 - beta_two**STEP)) + adam_eps)
    )
    param_new = param_now - learn_rate * (update + weight_decay * param_now)
    return (param_new, first_mom, second_mom)


def rows_of(values, count=PAD):
    return jnp.concatenate([values, jnp.zeros((count - values.shape[0],) + values.shape[1:], values.dtype)], axis=0)


def per_device(
    tokens,
    output_cotangent,
    document_numbers,
    document_adapter,
    input_norm_gain,
    gate_head_projection,
    map_projection,
    step_projection,
    output_projection,
    head_conv_taps,
    map_conv_taps,
    head_settings,
    gated_norm_gain,
    adapter_broad,
    adapter_step,
    adapter_shared,
    broad_first_moment,
    step_first_moment,
    shared_first_moment,
    broad_second_moment,
    step_second_moment,
    shared_second_moment,
):
    halves = lax.axis_size("mp")
    pieces = lax.axis_size("seq")
    owners = lax.axis_size("dp")
    core = lax.axis_index("mp")
    place = lax.axis_index("seq")
    length, width = tokens.shape[2:]
    layers, _, _, half = gate_head_projection.shape
    inner = halves * half
    heads_local = head_settings.shape[2]
    heads = halves * heads_local
    head_width = inner // heads
    own_adapters, rank = adapter_broad.shape[1:3]
    own_rows = own_adapters * rank
    adapters = own_adapters * owners
    ranks = adapters * rank
    part = width // halves
    states = map_projection.shape[2] // 2
    channels = inner + 2 * states

    def mine(values):
        return lax.dynamic_index_in_dim(values, core, 0, False)

    h_first = mine(tokens)[0]
    cotangent = mine(output_cotangent)[0]
    documents = mine(document_numbers)[0]
    chosen = mine(document_adapter)[0]

    low_broad = adapter_broad.astype(low)
    low_step = adapter_step.astype(low)
    low_shared = adapter_shared.astype(low)
    rows_own = gate_head_projection.shape[1]
    packs = Packs(rows_own, own_rows, half, part)
    spots = jnp.stack([lax.axis_index("dp"), place]).astype(jnp.int32)
    core_in = jnp.full((1,), core, jnp.int32)

    def twice(values):
        room = jnp.zeros(values.shape[:-1] + (LANES - 2 * values.shape[-1],), values.dtype)
        return jnp.concatenate([values, values, room], axis=-1)

    def packed(layer):
        zx = gate_head_projection[layer]
        broad = low_broad[layer].reshape(own_rows, 3, half)
        shared = low_shared[layer].reshape(own_rows, -1)
        maps = lax.dynamic_slice_in_dim(map_projection[layer], core * states, states, 1)
        maps_up = lax.dynamic_slice_in_dim(shared, width + core * states, states, 1)
        down = lax.dynamic_slice_in_dim(shared, core * part, part, 1)
        up = lax.dynamic_slice_in_dim(shared, width + 2 * states + core * part, part, 1)
        first = jnp.concatenate(
            [
                jnp.concatenate([zx[:, 1], maps, twice(step_projection[layer])], axis=1),
                jnp.concatenate([broad[:, 1], maps_up, twice(low_step[layer].reshape(own_rows, heads_local))], axis=1),
                jnp.concatenate([down, up, jnp.zeros((own_rows, half + 2 * LANES - 2 * part), low)], axis=1),
            ],
            axis=0,
        )
        second = jnp.concatenate([zx[:, 0], broad[:, 0], output_projection[layer].T, broad[:, 2]], axis=0)
        return first, second

    def ordered(values, after):
        return values if after is None else lax.optimization_barrier((values, after))[0]

    def sent(pack, quartered, after):
        quarter = pack.shape[0] // pieces
        if quarter % 16 or pack.shape[0] % pieces or owners == 1 or pieces == 1:
            return ordered(pack, after), None
        if quartered:
            mine_now = lax.dynamic_slice_in_dim(pack, place * quarter, quarter, 0)
        else:
            mine_now = pack
        mine_now = ordered(mine_now, after)
        return pack, [moved(mine_now, "dp", d, True) for d in range(1, owners)]

    def passed_on(near, after):
        if near is None:
            return []
        stack = ordered(jnp.stack(near), after)
        return [moved(stack, "seq", d, True) for d in range(1, pieces)]

    def gathered(pack, near, far, after):
        if near is None:
            own = lax.all_gather(ordered(pack, after), "dp", tiled=False)
        else:
            own = kernel_call(
                functools.partial(assemble_kernel, owners, pieces),
                [shape((owners,) + pack.shape, low)],
                [spots, pack, *ordered(near, after), *far],
                scalars=1,
                name="assemble",
                limit=20,
            )[0]
        return own, swapped(own)

    def last_of(messages, instead):
        return messages[-1] if messages else instead

    def over_cores(values):
        return jnp.concatenate([values, swapped(values)], axis=values.ndim - 1)

    widths = over_cores(jnp.concatenate([head_conv_taps, gated_norm_gain[:, None]], axis=1)).astype(full)
    settings = over_cores(head_settings)
    maps_taps = jnp.pad(map_conv_taps.astype(full), ((0, 0), (0, 1), (0, 0)))
    skips = jnp.broadcast_to(settings[:, 2:3, :, None], (layers, 1, heads, head_width)).reshape(layers, 1, inner)

    def wide_rows(values):
        return jnp.pad(values, ((0, 0), (0, 0), (0, channels - values.shape[2])))

    tables = jnp.concatenate(
        [
            jnp.concatenate([widths, maps_taps], axis=2),
            wide_rows(skips),
            wide_rows(input_norm_gain.astype(full)[:, None]),
            wide_rows(settings[:, :2]),
            jnp.zeros((layers, TABLE_ROWS - DECAY - 1, channels), full),
        ],
        axis=1,
    )
    head_of = np.arange(inner)[None, :] // head_width
    spread_one = (np.arange(LANES)[:, None] == head_of).astype(np.float32)
    spread_two = jnp.asarray(np.concatenate([spread_one, spread_one], axis=0), low)

    begin = place * length
    ends = jnp.concatenate([jnp.full((PAD,), -1, jnp.int32), documents, jnp.full((PAD,), -2, jnp.int32)])
    near = lax.dynamic_slice_in_dim(ends, begin, length + 2 * PAD)
    own = near[PAD : PAD + length]
    lane = jnp.arange(CONV * LANES)[None, :] // LANES

    def same_as(lag):
        return (own == near[PAD + lag : PAD + lag + length])[:, None]

    front = jnp.where(same_as(-1), 0.0, RESET)
    leads = same_as(CONV - 1)
    for lag in range(1, CONV):
        front = jnp.where(lane == lag - 1, jnp.where(same_as(-lag), 1.0, 0.0), front)
    for lag in range(1, CONV - 1):
        leads = jnp.where(lane[:, : -LANES] == lag - 1, same_as(lag), leads)
    front, leads = front.astype(low), leads.astype(low)
    which = jnp.arange(ranks)[None, :] // rank
    mask = jnp.zeros((length, ranks), jnp.bool_)
    for document in range(chosen.shape[0]):
        mask = mask | ((own == document)[:, None] & (which == chosen[document]))
    mask = mask.astype(low)

    prepared = (tables, front, leads, mask, h_first, cotangent)

    packs_of = [packed(layer) for layer in range(layers)]
    flights = {0: sent(packs_of[0][0], True, None)}
    before = flights[0][1]
    for layer in range(1, layers):
        flights[2 * layer] = sent(packs_of[layer][0], True, before)
        before = flights[2 * layer][1]
    first_far = passed_on(flights[0][1], prepared)
    weights = {0: gathered(*flights[0], first_far, before)}
    for layer in range(1, layers):
        next_far = passed_on(flights[2 * layer][1], first_far)
        weights[2 * layer] = gathered(*flights[2 * layer], next_far, weights[0][0])

    def gathered_both(pack, after):
        return lax.all_gather(ordered(pack, after), ("mp", "dp")).reshape((halves, owners) + pack.shape)

    weights[1] = gathered_both(packs_of[0][1], flights[0][1])

    flops_in = 2 * length * width * (2 * inner + 3 * LANES)
    flops_out = 2 * length * width * inner
    flops_scan = 4 * length * SPAN * inner

    h = h_first
    kept = []
    for layer in range(layers):
        first_own, first_other = weights[2 * layer]
        normed, spread, rows, dt_raw = kernel_call(
            functools.partial(project_rows_kernel, packs, heads_local, layer),
            [
                shape((length, width), low),
                shape((length, ranks), low),
                shape((length, channels), low),
                shape((length, LANES), full),
            ],
            [core_in, h, tables, mask, first_own, first_other],
            scalars=1,
            flops=flops_in // 2,
            name="project_rows",
        )
        halo = moved(rows[length - PAD :], "seq", 1)
        if layer + 1 < layers:
            halo = ordered(halo, weights[2 * layer + 2][0])
        act, xdt, dt, cum, flat, begin_state, end_state = kernel_call(
            functools.partial(states_kernel, inner, layer),
            [
                shape((length, channels), low),
                shape((length, inner), low),
                shape((length, LANES), full),
                shape((length, LANES), full),
                shape((LANES, length), full),
                shape((length // SPAN, states, inner), low),
                shape((states + 16, inner), low),
            ],
            [rows, halo, tables, front, dt_raw, spread_two],
            scratch=[pltpu.VMEM((length + PAD, channels), full), pltpu.VMEM((states, inner), full)],
            flops=flops_scan,
            name="states",
        )
        arrived = [moved(end_state, "seq", d) for d in range(1, pieces)]
        y_local = kernel_call(
            functools.partial(intra_kernel, inner, head_width, layer),
            [shape((length, inner), low)],
            [act, xdt, cum, flat, begin_state, tables, spread_two],
            flops=flops_scan,
            name="intra",
        )[0]
        wide = weights[2 * layer + 1]
        if layer + 1 < layers:
            weights[2 * layer + 3] = gathered_both(packs_of[layer + 1][1], act)
        gate = kernel_call(
            functools.partial(project_gate_kernel, packs),
            [shape((length, inner), full)],
            [core_in, normed, spread, wide],
            scalars=1,
            flops=flops_in // 2,
            name="project_gate",
        )[0]
        h_next, y, normal, spread_out, coming = kernel_call(
            functools.partial(output_kernel, packs, len(arrived), layer),
            [
                shape((length, width), full),
                shape((length, inner), low),
                shape((length, inner), low),
                shape((length, ranks), low),
                shape((states, inner), low),
            ],
            [core_in, h, y_local, gate, act, cum, tables, mask, first_own, first_other, wide, spread_two, *arrived],
            scalars=1,
            flops=flops_out,
            name="output",
        )
        kept.append(
            (h, normed, spread, gate, rows, halo, dt_raw, act, xdt, dt, cum, flat,
             begin_state, y, normal, spread_out, coming)
        )
        h = h_next
    mixed_own = h.astype(low)

    upstream = cotangent
    shares = []
    for layer in reversed(range(layers)):
        first_own, first_other = weights[2 * layer]
        wide = weights[2 * layer + 1]
        (h, normed, spread, gate, rows, halo, dt_raw, act, xdt, dt, cum, flat,
         begin_state, y, normal, spread_out, coming) = kept[layer]
        dgate, dy, own_grad, *early = kernel_call(
            functools.partial(output_back_kernel, packs, layer),
            [
                shape((length, inner), low),
                shape((length, inner), low),
                shape((states + 16, inner), low),
                *[shape((ranks, half + part), low)] * 2,
            ],
            [core_in, upstream, y, gate, normal, spread_out, act, cum, tables, mask, first_own, first_other, wide,
             spread_two],
            scratch=[pltpu.VMEM((length, ranks), low), pltpu.VMEM((length, width), low)],
            scalars=1,
            flops=flops_out,
            name="output_back",
        )
        arrived = [moved(own_grad, "seq", -d) for d in range(1, pieces)]
        u, db, dc = kernel_call(
            functools.partial(intra_back_kernel, inner, head_width),
            [shape((length, inner), low), shape((length, LANES), full), shape((length, LANES), full)],
            [act, xdt, dy, cum, flat],
            flops=2 * flops_scan,
            name="intra_back",
        )
        dn, dl, g_gate = kernel_call(
            functools.partial(gate_back_kernel, packs),
            [shape((length, width), full), shape((length, ranks), full), shape((halves, ranks, half), low)],
            [core_in, dgate, spread, wide],
            scalars=1,
            flops=flops_in // 2,
            name="gate_back",
        )
        reached = [share[:PAD, :LANES] for share in shares]
        dconv, ddt = kernel_call(
            functools.partial(scan_back_kernel, inner, len(arrived), layer),
            [shape((length, channels), low), shape((length, LANES), low)],
            [rows, halo, tables, front, act, xdt, dy, y, u, db, dc, dt, cum, dt_raw, begin_state, coming,
             spread_two, *arrived, *reached],
            scratch=[
                pltpu.VMEM((length + PAD, channels), full),
                pltpu.VMEM((states, inner), full),
                pltpu.VMEM((length, channels), full),
            ],
            flops=2 * flops_scan,
            name="scan_back",
        )
        after = moved(dconv[:PAD], "seq", -1)
        shares = [over_dp(share) for share in shares]
        reached = [share[:PAD, :LANES] for share in shares]
        dh, *grads = kernel_call(
            functools.partial(project_back_kernel, packs, heads_local, layer),
            [
                shape((length, width), full if layer > 0 else low),
                *[shape((ranks, 2 * half + 2 * LANES + part + sum(e.shape[1] for e in early[:1])), low)] * 2,
            ],
            [core_in, upstream, h, tables, mask, dconv, after, leads, ddt, dn, dl, spread, normed, first_own,
             first_other, g_gate, *early, *reached],
            scratch=[
                pltpu.VMEM((length + PAD, channels), full),
                pltpu.VMEM((length, channels), low),
                pltpu.VMEM((length, width), full),
            ],
            scalars=1,
            flops=flops_in // 2,
            name="project_back",
        )
        upstream = dh
        shares.append(over_mp(*grads))

    behind = [over_seq(share) for share in shares[:-1]]
    whole = jnp.stack([over_seq(ordered(over_dp(shares[-1]), behind)), *reversed(behind)])
    zx, maps, steps, down_in, down_out, up_out = jnp.split(
        whole,
        [2 * half, 2 * half + LANES, 2 * half + 2 * LANES, 2 * half + 2 * LANES + part, 3 * half + 2 * LANES + part],
        axis=2,
    )
    own_shared = jnp.concatenate([maps, down_in, up_out], axis=2)
    other_shared = swapped(own_shared)
    in_order = [jnp.where(core == m, own_shared, other_shared) for m in range(halves)]
    maps, down_in, up_out = (
        [entry[:, :, first:last] for entry in in_order]
        for first, last in ((0, LANES), (LANES, LANES + part), (LANES + part, LANES + 2 * part))
    )
    shared_gradient = jnp.concatenate([*down_in, *maps, *up_out], axis=2).reshape(adapter_shared.shape)
    broad_gradient = jnp.concatenate([zx, down_out], axis=2).reshape(adapter_broad.shape)
    step_gradient = steps[:, :, :heads_local].reshape(adapter_step.shape)
    local_sq = (
        jnp.sum(broad_gradient * broad_gradient)
        + jnp.sum(step_gradient * step_gradient)
        + jnp.sum(own_shared * own_shared)
    )
    squares = jnp.broadcast_to(local_sq, (8, LANES))
    squares = squares + swapped(squares)
    total_sq = squares
    for distance in range(1, owners):
        total_sq = total_sq + moved(squares, "dp", distance, True)
    grad_norm = jnp.sqrt(total_sq[0, 0])
    scale_factor = clip_max / jnp.maximum(grad_norm, clip_max)
    revised_broad, fresh_first_broad, fresh_square_broad = adamw_update(
        adapter_broad, broad_gradient, broad_first_moment, broad_second_moment, scale_factor
    )
    revised_step, fresh_first_step, fresh_square_step = adamw_update(
        adapter_step, step_gradient, step_first_moment, step_second_moment, scale_factor
    )
    revised_shared, fresh_first_shared, fresh_square_shared = adamw_update(
        adapter_shared, shared_gradient, shared_first_moment, shared_second_moment, scale_factor
    )

    def both(values):
        other = swapped(values)
        return jnp.stack([jnp.where(core == m, values, other) for m in range(halves)])[:, None]

    return (
        both(mixed_own),
        both(upstream),
        grad_norm,
        revised_broad,
        revised_step,
        revised_shared,
        fresh_first_broad,
        fresh_first_step,
        fresh_first_shared,
        fresh_square_broad,
        fresh_square_step,
        fresh_square_shared,
        revised_broad.astype(low),
        revised_step.astype(low),
        revised_shared.astype(low),
    )


def solution(mesh):
    placed = (
        P(None, "dp", "seq", None),
        P(None, "dp", "seq", None),
        P(None, "dp", None),
        P(None, "dp", None),
        P(),
        P(None, "dp", None, "mp"),
        P(None, "dp", None),
        P(None, "dp", "mp"),
        P(None, "mp", "dp"),
        P(None, None, "mp"),
        P(),
        P(None, None, "mp"),
        P(None, "mp"),
        P(None, "dp", None, None, "mp"),
        P(None, "dp", None, "mp"),
        P(None, "dp", None, None),
        P(None, "dp", None, None, "mp"),
        P(None, "dp", None, "mp"),
        P(None, "dp", None, None),
        P(None, "dp", None, None, "mp"),
        P(None, "dp", None, "mp"),
        P(None, "dp", None, None),
    )
    return jax.shard_map(
        per_device,
        mesh=mesh,
        in_specs=placed,
        out_specs=(
            P(None, "dp", "seq", None),
            P(None, "dp", "seq", None),
            P(),
            P(None, "dp", None, None, "mp"),
            P(None, "dp", None, "mp"),
            P(None, "dp", None, None),
            P(None, "dp", None, None, "mp"),
            P(None, "dp", None, "mp"),
            P(None, "dp", None, None),
            P(None, "dp", None, None, "mp"),
            P(None, "dp", None, "mp"),
            P(None, "dp", None, None),
            P(None, "dp", None, None, "mp"),
            P(None, "dp", None, "mp"),
            P(None, "dp", None, None),
        ),
        check_vma=False,
    )
```

```python
import functools

import jax
import jax.numpy as jnp
import numpy as np
from jax import lax
from jax.experimental import pallas as pl
from jax.experimental.pallas import tpu as pltpu
from jax.sharding import PartitionSpec as P

CONV = 4
STEP = 10
LANES = 128
SPAN = 128
PAD = 8
RESET = -128.0
GAIN_TWO, SKIP, GAIN, STEP_BIAS, DECAY, TABLE_ROWS = 5, 6, 7, 8, 9, 16

norm_eps = 1e-05
learn_rate = 0.04
beta_one = 0.5
beta_two = 0.5
weight_decay = 0.01
adam_eps = 1e-08
clip_max = 1.0
low = jnp.bfloat16
full = jnp.float32


def nn(a, b):
    return lax.dot_general(a, b, (((1,), (0,)), ((), ())), preferred_element_type=full)


def nt(a, b):
    return lax.dot_general(a, b, (((1,), (1,)), ((), ())), preferred_element_type=full)


def tn(a, b):
    return lax.dot_general(a, b, (((0,), (0,)), ((), ())), preferred_element_type=full)


def two_parts(values, axis):
    high = values.astype(low)
    rest = (values - high.astype(full)).astype(low)
    return jnp.concatenate([high, rest], axis=axis)


def three_parts(values, axis):
    high = values.astype(low)
    rest = values - high.astype(full)
    middle = rest.astype(low)
    last = (rest - middle.astype(full)).astype(low)
    return jnp.concatenate([high, middle, last], axis=axis)


def widen(values, spread_two):
    return nn(two_parts(values, 1), spread_two)


def per_head(values, spread_two):
    heads = spread_two[:LANES]
    high = values.astype(low)
    rest = (values - high.astype(full)).astype(low)
    return nt(high, heads) + nt(rest, heads)


def triangle(kind):
    rows = lax.broadcasted_iota(jnp.int32, (SPAN, SPAN), 0)
    columns = lax.broadcasted_iota(jnp.int32, (SPAN, SPAN), 1)
    return rows >= columns if kind == "lower" else rows <= columns


def cumulate(values, kind):
    keep = triangle(kind).astype(full).astype(low)
    return nn(jnp.concatenate([keep, keep, keep], axis=1), three_parts(values, 0))


def sigmoid(values):
    return 1.0 / (1.0 + jnp.exp(-values))


def kernel_call(body, outs, ins, scratch=(), flops=0, name=None, limit=20, scalars=0):
    moved = sum(a.size * a.dtype.itemsize for a in list(ins) + list(outs))
    whole = pl.BlockSpec(memory_space=pltpu.VMEM)
    return pl.pallas_call(
        body,
        out_shape=tuple(outs),
        in_specs=[pl.BlockSpec(memory_space=pltpu.SMEM)] * scalars + [whole] * (len(ins) - scalars),
        out_specs=tuple([whole] * len(outs)),
        scratch_shapes=list(scratch),
        compiler_params=pltpu.CompilerParams(vmem_limit_bytes=limit * 2**20),
        cost_estimate=pl.CostEstimate(flops=flops, bytes_accessed=moved, transcendentals=0),
        name=name,
    )(*ins)


def shape(dims, kind):
    return jax.ShapeDtypeStruct(dims, kind)


def assemble_kernel(owners, pieces, place, pack, *rest):
    near, far, out = rest[: owners - 1], rest[owners - 1 : owners + pieces - 2], rest[-1]
    quarter = pack.shape[0] // pieces
    owner, piece = place[0], place[1]
    out[owner] = pack[...]
    for i in range(owners - 1):
        source = lax.rem(owner + (owners - 1 - i), owners)
        out[source, pl.ds(pl.multiple_of(piece * quarter, 16), quarter)] = near[i][...]
        for j in range(pieces - 1):
            sender = lax.rem(piece + (pieces - 1 - j), pieces)
            out[source, pl.ds(pl.multiple_of(sender * quarter, 16), quarter)] = far[j][i]


def sections(ref, first, last, columns=slice(None), core=None):
    if core is not None:
        return jnp.concatenate([ref[core, d, first:last, columns] for d in range(ref.shape[1])], axis=0)
    return jnp.concatenate([ref[d, first:last, columns] for d in range(ref.shape[0])], axis=0)


def core_sections(ref, core, first, last):
    return sections(ref, first, last, slice(None), core)


class Packs:
    def __init__(self, rows, adapter_rows, half, part):
        self.width, self.adapt = (0, rows), (rows, rows + adapter_rows)
        self.ends = (rows + adapter_rows, rows + 2 * adapter_rows)
        self.x, self.maps = slice(0, half), slice(half, half + LANES)
        self.steps = slice(half + LANES, half + 2 * LANES)
        self.mixed = slice(0, half + LANES)
        self.down, self.up = slice(0, part), slice(part, 2 * part)
        base = rows + adapter_rows
        self.out, self.out_down = (base, base + rows), (base + rows, base + rows + adapter_rows)
        self.half, self.part, self.rows = half, part, rows


def step_weights(own, other, first, last, columns, local):
    lane = lax.broadcasted_iota(jnp.int32, (1, LANES), 1)
    mine = sections(own, first, last, columns).astype(full)
    theirs = sections(other, first, last, columns).astype(full)
    return jnp.where(lane < local, mine, jnp.where(lane < 2 * local, theirs, 0.0)).astype(low)


def project_rows_kernel(packs, local, layer, core, h, tables, mask, own, other, normed_o, spread_o, rows_o, dt_o):
    values = h[...].astype(full)
    half, part = packs.half, packs.part
    scale = lax.rsqrt(jnp.mean(values * values, axis=1, keepdims=True) + norm_eps)
    normed_o[...] = (values * scale * tables[layer, GAIN : GAIN + 1, : h.shape[1]]).astype(low)
    normed = normed_o[...]
    places = ((own, core[0], 0), (other, 1 - core[0], half))
    down = jnp.zeros((h.shape[0], mask.shape[1]), full)
    for ref, index, _ in places:
        columns = pl.ds(pl.multiple_of(index * part, LANES), part)
        down = down + nt(normed_o[:, columns], sections(ref, *packs.ends, packs.down))
    spread = down.astype(low) * mask[...]
    spread_o[...] = spread
    for ref, index, place in places:
        made = nn(normed, sections(ref, *packs.width, packs.mixed)) + nn(spread, sections(ref, *packs.adapt, packs.mixed))
        rows_o[:, place : place + half] = made[:, :half].astype(low)
        rows_o[:, pl.ds(pl.multiple_of(2 * half + index * LANES, LANES), LANES)] = made[:, half:].astype(low)
    w_dt = step_weights(own, other, *packs.width, packs.steps, local)
    b_dt = step_weights(own, other, *packs.adapt, packs.steps, local)
    dt_o[...] = nn(normed, w_dt) + nn(spread, b_dt)


def project_gate_kernel(packs, core, normed, spread, wide, gate_o):
    half = packs.half
    for index, place in ((core[0], 0), (1 - core[0], half)):
        gate_o[:, place : place + half] = nn(normed[...], core_sections(wide, index, *packs.width)) + nn(
            spread[...], core_sections(wide, index, *packs.adapt)
        )


def conv_chunk(ext, same, taps, begin, columns):
    window = ext[pl.ds(begin, SPAN + PAD), columns]
    summed = taps[CONV : CONV + 1, columns] + taps[0:1, columns] * window[PAD:]
    for lag in range(1, CONV):
        summed = summed + taps[lag : lag + 1, columns] * window[PAD - lag : PAD - lag + SPAN] * same[lag - 1]
    return summed


def same_documents(front, span):
    return [front[span, i * LANES : (i + 1) * LANES].astype(full) for i in range(CONV - 1)]


def fill_extended(ext, halo, rows):
    ext[0:PAD, :] = halo[...].astype(full)
    ext[PAD : PAD + rows.shape[0], :] = rows[...].astype(full)


def states_kernel(
    inner, layer, rows, halo, tables, front, dt_raw, spread_two, *rest,
):
    act_o, xdt_o, dt_o, cum_o, flat_o, begin_o, end_o, ext, state = rest[-9:]
    length = rows.shape[0]
    channels = rows.shape[1]
    table = tables.at[layer]
    fill_extended(ext, halo, rows)
    state[...] = jnp.zeros_like(state)

    def block(k, so_far):
        begin = pl.multiple_of(k * SPAN, SPAN)
        span = pl.ds(begin, SPAN)
        same = same_documents(front, span)
        for c in range(0, channels, LANES):
            columns = slice(c, c + LANES)
            summed = conv_chunk(ext, same, table, begin, columns)
            act_o[span, columns] = (summed * sigmoid(summed)).astype(low)
        raw = dt_raw[span, :] + table[STEP_BIAS : STEP_BIAS + 1, :LANES]
        dt = jnp.maximum(raw, 0.0) + jnp.log1p(jnp.exp(-jnp.abs(raw)))
        jump = front[span, (CONV - 1) * LANES :].astype(full)
        cum = cumulate(jump - jnp.exp(table[DECAY : DECAY + 1, :LANES]) * dt, "lower")
        dt_o[span, :] = dt
        cum_o[span, :] = cum
        flat_o[:, span] = cum.T
        total = cum[SPAN - 1 : SPAN, :]
        xdt = (act_o[span, 0:inner].astype(full) * widen(dt, spread_two[...])).astype(low)
        xdt_o[span, :] = xdt
        tail = widen(jnp.exp(total - cum), spread_two[...])
        b_map = act_o[span, inner : inner + LANES]
        begin_o[k] = state[...].astype(low)
        keep = widen(jnp.broadcast_to(jnp.exp(total), (8, LANES)), spread_two[...])[0:1]
        state[...] = state[...] * keep + tn(b_map, (xdt.astype(full) * tail).astype(low))
        return so_far + total

    total = lax.fori_loop(0, length // SPAN, block, jnp.zeros((1, LANES), full))
    put_message(end_o, state[...], total, spread_two[...])


def intra_kernel(inner, head_width, layer, act, xdt, cum, flat, begin_state, tables, spread_two, y_o):
    length = act.shape[0]
    keep = triangle("lower")
    left = lax.broadcasted_iota(jnp.int32, (SPAN, LANES), 1) < head_width

    def block(k, carry):
        begin = pl.multiple_of(k * SPAN, SPAN)
        span = pl.ds(begin, SPAN)
        b_map = act[span, inner : inner + LANES]
        c_map = act[span, inner + LANES : inner + 2 * LANES]
        scores = nt(c_map, b_map)
        cum_now = cum[span, :]
        entry = widen(jnp.exp(cum_now), spread_two[...])
        before = nn(c_map, begin_state[k])
        for pair in range(inner // LANES):
            columns = slice(pair * LANES, (pair + 1) * LANES)
            mixing = []
            for head in (2 * pair, 2 * pair + 1):
                gap = cum_now[:, head : head + 1] - flat[head : head + 1, span]
                mixing.append((scores * jnp.exp(jnp.where(keep, gap, -1e30))).astype(low))
            x_pair = xdt[span, columns]
            nothing = jnp.zeros_like(x_pair)
            x_two = jnp.concatenate([jnp.where(left, x_pair, nothing), jnp.where(left, nothing, x_pair)], axis=0)
            intra = nn(jnp.concatenate(mixing, axis=1), x_two)
            y_o[span, columns] = (
                intra
                + entry[:, columns] * before[:, columns]
                + tables[layer, SKIP : SKIP + 1, columns] * act[span, columns].astype(full)
            ).astype(low)
        return carry

    lax.fori_loop(0, length // SPAN, block, 0)


def put_message(out, values, total, spread_two):
    out[:LANES] = values.astype(low)
    high = total.astype(low).astype(full)
    middle = (total - high).astype(low).astype(full)
    parts = jnp.concatenate([high, middle, total - high - middle, jnp.zeros((13, LANES), full)], axis=0)
    out[LANES:] = nn(parts.astype(low), spread_two[:LANES]).astype(low)


def combine(messages):
    total = messages[0][:LANES].astype(full)
    decay = 0.0
    for i in range(1, len(messages)):
        decay = decay + jnp.sum(messages[i - 1][LANES : LANES + 16].astype(full), axis=0, keepdims=True)
        total = total + messages[i][:LANES].astype(full) * jnp.exp(decay)
    return total


def output_kernel(
    packs, count, layer, core, h, y_local, gate, act, cum, tables, mask, first_own, first_other, wide, spread_two, *rest
):
    parts, rest = rest[:count], rest[count:]
    h_o, y_o, normal_o, spread_o, coming_o = rest
    length = h.shape[0]
    half, part = packs.half, packs.part
    inner = 2 * half
    coming = combine(parts).astype(low)
    coming_o[...] = coming
    before = jnp.zeros((1, LANES), full)
    for k in range(length // SPAN):
        span = slice(k * SPAN, (k + 1) * SPAN)
        cum_now = cum[span, :]
        carry = widen(jnp.exp(cum_now + before), spread_two[...])
        before = before + cum_now[SPAN - 1 : SPAN, :]
        c_map = act[span, inner + LANES : inner + 2 * LANES]
        y = y_local[span, :].astype(full) + carry * nn(c_map, coming)
        y_o[span, :] = y.astype(low)
        z = gate[span, :]
        gated = y * z * sigmoid(z)
        scale = lax.rsqrt(jnp.mean(gated * gated, axis=1, keepdims=True) + norm_eps)
        normal_o[span, :] = (gated * scale * tables[layer, GAIN_TWO : GAIN_TWO + 1, :inner]).astype(low)
    second = jnp.zeros((length, LANES), full)
    branch = h[...].astype(full)
    for index, place in ((core[0], 0), (1 - core[0], half)):
        normal = normal_o[:, place : place + half]
        second = second + nt(normal, core_sections(wide, index, *packs.out_down))
        branch = branch + nt(normal, core_sections(wide, index, *packs.out))
    h_o[...] = branch.astype(h_o.dtype)
    spread = second.astype(low) * mask[...]
    spread_o[...] = spread
    for ref, index in ((first_own, core[0]), (first_other, 1 - core[0])):
        columns = pl.ds(pl.multiple_of(index * part, LANES), part)
        h_o[:, columns] = (h_o[:, columns] + nn(spread, sections(ref, *packs.ends, packs.up))).astype(h_o.dtype)


def output_back_kernel(
    packs, layer, core, upstream, y, gate, normal, spread_out, act, cum, tables, mask, first_own, first_other, wide, spread_two,
    *rest,
):
    found, rest = rest[:-7], rest[-7:]
    dgate_o, dy_o, own_o, *grads_o, seconds, lows = rest
    length = y.shape[0]
    half, part = packs.half, packs.part
    inner = 2 * half
    first = grads_o[0].shape[1] - half - part
    for i in range(len(found)):
        grads_o[i][:, :first] = found[i][...]
    lows[...] = upstream[...].astype(low)
    down = jnp.zeros(seconds.shape, full)
    for i, (ref, index) in enumerate(((first_own, core[0]), (first_other, 1 - core[0]))):
        now = lows[:, pl.ds(pl.multiple_of(index * part, LANES), part)]
        down = down + nt(now, sections(ref, *packs.ends, packs.up))
        grads_o[i][:, first + half :] = tn(spread_out[...], now).astype(low)
    second = down.astype(low) * mask[...]
    seconds[...] = second
    for i in range(2):
        grads_o[i][:, first : first + half] = tn(second, normal[:, i * half : (i + 1) * half]).astype(low)
    grad = jnp.zeros((LANES, inner), full)
    before = jnp.zeros((1, LANES), full)
    for k in range(length // SPAN):
        span = slice(k * SPAN, (k + 1) * SPAN)
        up_now = lows[span, :]
        grads = []
        for index in (core[0], 1 - core[0]):
            grads.append(
                nn(up_now, core_sections(wide, index, *packs.out))
                + nn(seconds[span, :], core_sections(wide, index, *packs.out_down))
            )
        weighted = jnp.concatenate(grads, axis=1) * tables[layer, GAIN_TWO : GAIN_TWO + 1, :inner]
        y_now = y[span, :].astype(full)
        z = gate[span, :]
        sig = sigmoid(z)
        silu = z * sig
        gated = y_now * silu
        scale = lax.rsqrt(jnp.mean(gated * gated, axis=1, keepdims=True) + norm_eps)
        mean_in = jnp.mean(weighted * gated, axis=1, keepdims=True)
        grad_gated = scale * weighted - gated * (scale * scale * scale * mean_in)
        dgate_o[span, :] = (grad_gated * y_now * sig * (1.0 + z * (1.0 - sig))).astype(low)
        dy = grad_gated * silu
        dy_o[span, :] = dy.astype(low)
        cum_now = cum[span, :]
        carry = widen(jnp.exp(cum_now + before), spread_two[...])
        before = before + cum_now[SPAN - 1 : SPAN, :]
        grad = grad + tn(act[span, inner + LANES : inner + 2 * LANES], (carry * dy).astype(low))
    put_message(own_o, grad, before, spread_two[...])


def intra_back_kernel(inner, head_width, act, xdt, dy, cum, flat, u_o, db_o, dc_o):
    length = act.shape[0]
    keep = triangle("upper")
    left = lax.broadcasted_iota(jnp.int32, (SPAN, LANES), 1) < head_width

    def block(k, carry):
        begin = pl.multiple_of(k * SPAN, SPAN)
        span = pl.ds(begin, SPAN)
        b_map = act[span, inner : inner + LANES]
        c_map = act[span, inner + LANES : inner + 2 * LANES]
        scores = nt(b_map, c_map)
        cum_now = cum[span, :]
        dscores = jnp.zeros((SPAN, SPAN), full)
        for pair in range(inner // LANES):
            columns = slice(pair * LANES, (pair + 1) * LANES)
            dy_pair = dy[span, columns]
            nothing = jnp.zeros_like(dy_pair)
            dy_two = jnp.concatenate([jnp.where(left, dy_pair, nothing), jnp.where(left, nothing, dy_pair)], axis=0)
            products = nt(xdt[span, columns], dy_two)
            mixing = []
            for i, head in enumerate((2 * pair, 2 * pair + 1)):
                gap = flat[head : head + 1, span] - cum_now[:, head : head + 1]
                decay = jnp.exp(jnp.where(keep, gap, -1e30))
                mixing.append((scores * decay).astype(low))
                dscores = dscores + products[:, i * SPAN : (i + 1) * SPAN] * decay
            u_o[span, columns] = nn(jnp.concatenate(mixing, axis=1), dy_two).astype(low)
        dlow = dscores.astype(low)
        db_o[span, :] = nn(dlow, c_map)
        dc_o[span, :] = tn(dlow, b_map)
        return carry

    lax.fori_loop(0, length // SPAN, block, 0)


def scan_back_kernel(
    inner, count, layer, rows, halo, tables, front, act, xdt, dy, y, u, db_in, dc_in, dt, cum, dt_raw,
    begin_state, coming, spread_two, *rest,
):
    parts = rest[:count]
    dconv_o, ddt_o, ext, grad, dact = rest[-5:]
    length = act.shape[0]
    channels = rows.shape[1]
    blocks = length // SPAN
    table = tables.at[layer]
    skip = table[SKIP : SKIP + 1, :inner]
    fill_extended(ext, halo, rows)
    grad[...] = combine(parts)
    ends = [cum[(k + 1) * SPAN - 1 : (k + 1) * SPAN, :] for k in range(blocks)]
    for k in reversed(range(blocks)):
        span = slice(k * SPAN, (k + 1) * SPAN)
        cum_now = cum[span, :]
        total = ends[k]
        before = sum(ends[:k], jnp.zeros((1, LANES), full))
        b_map = act[span, inner : inner + LANES]
        c_map = act[span, inner + LANES : inner + 2 * LANES]
        grad_low = grad[...].astype(low)
        tail = widen(jnp.exp(total - cum_now), spread_two[...])
        entry = widen(jnp.exp(cum_now), spread_two[...])
        rows_wide = widen(jnp.exp(jnp.concatenate([total, before] * 4, axis=0)), spread_two[...])
        keep, carry = rows_wide[0:1], rows_wide[1:2]
        x = act[span, 0:inner].astype(full)
        x_dt = xdt[span, :].astype(full)
        from_later = tail * nn(b_map, grad_low)
        v = u[span, :].astype(full) + from_later
        state = begin_state[k].astype(full) + carry * coming[...].astype(full)
        dy_now = dy[span, :].astype(full)
        db = db_in[span, :] + nt((x_dt * tail).astype(low), grad_low)
        entry_dy = (entry * dy_now).astype(low)
        dc = dc_in[span, :] + nt(entry_dy, state.astype(low))
        kept = keep * grad[...]
        end_rows = jnp.sum(x_dt * from_later, axis=0, keepdims=True) + jnp.sum(kept * state, axis=0, keepdims=True)
        grad[...] = kept + tn(c_map, entry_dy)
        y_scan = y[span, :].astype(full) - skip * x
        dcum = per_head(dy_now * y_scan - x_dt * v, spread_two[...])
        at_end = per_head(jnp.broadcast_to(end_rows, (8, inner)), spread_two[...])[0:1]
        ddecay = cumulate(dcum, "upper") + at_end
        raw = dt_raw[span, :] + table[STEP_BIAS : STEP_BIAS + 1, :LANES]
        ddt = per_head(x * v, spread_two[...]) - ddecay * jnp.exp(table[DECAY : DECAY + 1, :LANES])
        ddt_o[span, :] = (ddt * sigmoid(raw)).astype(low)
        dact[span, 0:inner] = widen(dt[span, :], spread_two[...]) * v + skip * dy_now
        dact[span, inner : inner + LANES] = db
        dact[span, inner + LANES : inner + 2 * LANES] = dc
        same = same_documents(front, span)
        for c in range(0, channels, LANES):
            columns = slice(c, c + LANES)
            summed = conv_chunk(ext, same, table, k * SPAN, columns)
            sig = sigmoid(summed)
            dconv_o[span, columns] = (dact[span, columns] * sig * (1.0 + summed * (1.0 - sig))).astype(low)


def gate_back_kernel(packs, core, dgate, spread, wide, dn_o, dl_o, grad_o):
    half = packs.half
    dn = dl = 0.0
    for i, index in enumerate((core[0], 1 - core[0])):
        piece = dgate[:, i * half : (i + 1) * half]
        dn = dn + nt(piece, core_sections(wide, index, *packs.width))
        dl = dl + nt(piece, core_sections(wide, index, *packs.adapt))
        grad_o[i] = tn(spread[...], piece).astype(grad_o.dtype)
    dn_o[...] = dn
    dl_o[...] = dl


def project_back_kernel(
    packs, local, layer, core, upstream, h, tables, mask, dconv, after, leads, ddt, dn_in, dl_in, spread, normed, own, other,
    *rest,
):
    found, rest = rest[:-6], rest[-6:]
    dh_o, *grads_o, ext, drows, dn_s = rest
    gate_grad, found = found[0], found[1:3]
    length = h.shape[0]
    channels = dconv.shape[1]
    half, part = packs.half, packs.part
    ext[0:length, :] = dconv[...].astype(full)
    ext[length : length + PAD, :] = after[...].astype(full)

    def block(k, carry):
        begin = pl.multiple_of(k * SPAN, SPAN)
        span = pl.ds(begin, SPAN)
        same = same_documents(leads, span)
        for c in range(0, channels, LANES):
            columns = slice(c, c + LANES)
            window = ext[pl.ds(begin, SPAN + PAD), columns]
            total = tables[layer, 0:1, columns] * window[:SPAN]
            for lag in range(1, CONV):
                total = total + tables[layer, lag : lag + 1, columns] * window[lag : lag + SPAN] * same[lag - 1]
            drows[span, columns] = total.astype(low)
        return carry

    lax.fori_loop(0, length // SPAN, block, 0)
    step = ddt[...]
    dn = dn_in[...] + nt(step, step_weights(own, other, *packs.width, packs.steps, local))
    dl = dl_in[...] + nt(step, step_weights(own, other, *packs.adapt, packs.steps, local))
    step_grad = tn(spread[...], step)
    places = ((own, core[0]), (other, 1 - core[0]))
    for i, (ref, index) in enumerate(places):
        maps = drows[:, pl.ds(pl.multiple_of(2 * half + index * LANES, LANES), LANES)]
        piece = jnp.concatenate([drows[:, i * half : (i + 1) * half], maps], axis=1)
        dn = dn + nt(piece, sections(ref, *packs.width, packs.mixed))
        dl = dl + nt(piece, sections(ref, *packs.adapt, packs.mixed))
        grad_o = grads_o[i]
        grad_o[:, :half] = gate_grad[i]
        grad_o[:, half : 2 * half + LANES] = tn(spread[...], piece).astype(low)
        turned = step_grad if i == 0 else pltpu.roll(step_grad, LANES - local, 1)
        grad_o[:, 2 * half + LANES : 2 * half + 2 * LANES] = turned.astype(low)
    back = dl.astype(low) * mask[...]
    dn_s[...] = dn
    for i, (ref, index) in enumerate(places):
        columns = pl.ds(pl.multiple_of(index * part, LANES), part)
        begin = 2 * half + 2 * LANES
        grads_o[i][:, begin : begin + part] = tn(back, normed[:, columns]).astype(low)
        if found:
            grads_o[i][:, begin + part :] = found[i][...]
        dn_s[:, columns] = dn_s[:, columns] + nn(back, sections(ref, *packs.ends, packs.down))
    dn = dn_s[...]
    values = h[...].astype(full)
    scale = lax.rsqrt(jnp.mean(values * values, axis=1, keepdims=True) + norm_eps)
    weighted = dn * tables[layer, GAIN : GAIN + 1, : h.shape[1]]
    mean_in = jnp.mean(weighted * values, axis=1, keepdims=True)
    dh = upstream[...].astype(full) + scale * weighted - values * (scale * scale * scale * mean_in)
    dh_o[...] = dh.astype(dh_o.dtype)


def moved(block, axis, distance, wrap=False):
    count = lax.axis_size(axis)
    route = [(i, (i + distance) % count) for i in range(count) if wrap or 0 <= i + distance < count]
    return lax.ppermute(block, axis, route)


def swapped(block):
    count = lax.axis_size("mp")
    return lax.ppermute(block, "mp", [(i, count - 1 - i) for i in range(count)])


def over_mp(own, other):
    return (own.astype(full) + swapped(other).astype(full)).astype(low)


def over_dp(both):
    owners, place = lax.axis_size("dp"), lax.axis_index("dp")
    count = both.shape[0] // owners
    total = lax.dynamic_slice_in_dim(both, place * count, count, 0).astype(full)
    for distance in range(1, owners):
        share = lax.dynamic_slice_in_dim(both, (place + distance) % owners * count, count, 0)
        total = total + moved(share, "dp", distance, True).astype(full)
    return total.astype(low)


def over_seq(total):
    result = total.astype(full)
    for distance in range(1, lax.axis_size("seq")):
        result = result + moved(total, "seq", distance, True).astype(full)
    return result


def adamw_update(param_now, gradient, moment_now, square_now, scale_factor):
    gradient = gradient * scale_factor
    first_mom = beta_one * moment_now + (1.0 - beta_one) * gradient
    second_mom = beta_two * square_now + (1.0 - beta_two) * gradient * gradient
    update = (
        first_mom
        / (1.0 - beta_one**STEP)
        / (jnp.sqrt(second_mom / (1.0 - beta_two**STEP)) + adam_eps)
    )
    param_new = param_now - learn_rate * (update + weight_decay * param_now)
    return (param_new, first_mom, second_mom)


def rows_of(values, count=PAD):
    return jnp.concatenate([values, jnp.zeros((count - values.shape[0],) + values.shape[1:], values.dtype)], axis=0)


def per_device(
    tokens,
    output_cotangent,
    document_numbers,
    document_adapter,
    input_norm_gain,
    gate_head_projection,
    map_projection,
    step_projection,
    output_projection,
    head_conv_taps,
    map_conv_taps,
    head_settings,
    gated_norm_gain,
    adapter_broad,
    adapter_step,
    adapter_shared,
    broad_first_moment,
    step_first_moment,
    shared_first_moment,
    broad_second_moment,
    step_second_moment,
    shared_second_moment,
):
    halves = lax.axis_size("mp")
    pieces = lax.axis_size("seq")
    owners = lax.axis_size("dp")
    core = lax.axis_index("mp")
    place = lax.axis_index("seq")
    length, width = tokens.shape[2:]
    layers, _, _, half = gate_head_projection.shape
    inner = halves * half
    heads_local = head_settings.shape[2]
    heads = halves * heads_local
    head_width = inner // heads
    own_adapters, rank = adapter_broad.shape[1:3]
    own_rows = own_adapters * rank
    adapters = own_adapters * owners
    ranks = adapters * rank
    part = width // halves
    states = map_projection.shape[2] // 2
    channels = inner + 2 * states

    def mine(values):
        return lax.dynamic_index_in_dim(values, core, 0, False)

    h_first = mine(tokens)[0]
    documents = mine(document_numbers)[0]
    chosen = mine(document_adapter)[0]

    low_broad = adapter_broad.astype(low)
    low_step = adapter_step.astype(low)
    low_shared = adapter_shared.astype(low)
    rows_own = gate_head_projection.shape[1]
    packs = Packs(rows_own, own_rows, half, part)
    spots = jnp.stack([lax.axis_index("dp"), place]).astype(jnp.int32)
    core_in = jnp.full((1,), core, jnp.int32)

    def twice(values):
        room = jnp.zeros(values.shape[:-1] + (LANES - 2 * values.shape[-1],), values.dtype)
        return jnp.concatenate([values, values, room], axis=-1)

    def packed(layer):
        zx = gate_head_projection[layer]
        broad = low_broad[layer].reshape(own_rows, 3, half)
        shared = low_shared[layer].reshape(own_rows, -1)
        maps = lax.dynamic_slice_in_dim(map_projection[layer], core * states, states, 1)
        maps_up = lax.dynamic_slice_in_dim(shared, width + core * states, states, 1)
        down = lax.dynamic_slice_in_dim(shared, core * part, part, 1)
        up = lax.dynamic_slice_in_dim(shared, width + 2 * states + core * part, part, 1)
        first = jnp.concatenate(
            [
                jnp.concatenate([zx[:, 1], maps, twice(step_projection[layer])], axis=1),
                jnp.concatenate([broad[:, 1], maps_up, twice(low_step[layer].reshape(own_rows, heads_local))], axis=1),
                jnp.concatenate([down, up, jnp.zeros((own_rows, half + 2 * LANES - 2 * part), low)], axis=1),
            ],
            axis=0,
        )
        second = jnp.concatenate([zx[:, 0], broad[:, 0], output_projection[layer].T, broad[:, 2]], axis=0)
        return first, second

    def ordered(values, after):
        return values if after is None else lax.optimization_barrier((values, after))[0]

    def zero_after(value):
        return value.reshape(-1)[0].astype(full) * 0.0

    def sent(pack, quartered, after):
        quarter = pack.shape[0] // pieces
        if quarter % 16 or pack.shape[0] % pieces or owners == 1 or pieces == 1:
            return ordered(pack, after), None
        if quartered:
            mine_now = lax.dynamic_slice_in_dim(pack, place * quarter, quarter, 0)
        else:
            mine_now = pack
        mine_now = ordered(mine_now, after)
        return pack, [moved(mine_now, "dp", d, True) for d in range(1, owners)]

    def passed_on(near, after):
        if near is None:
            return []
        stack = ordered(jnp.stack(near), after)
        return [moved(stack, "seq", d, True) for d in range(1, pieces)]

    def gathered(pack, near, far, after):
        if near is None:
            own = lax.all_gather(pack, "dp")
        else:
            own = kernel_call(
                functools.partial(assemble_kernel, owners, pieces),
                [shape((owners,) + pack.shape, low)],
                [spots, pack, *near, *far, *after],
                scalars=1,
                name="assemble",
                limit=20,
            )[0]
        return own, swapped(own)

    def last_of(messages, instead):
        return messages[-1] if messages else instead

    packs_of = [packed(layer) for layer in range(layers)]
    flights = {2 * layer: sent(packs_of[layer][0], True, None) for layer in range(layers)}
    first_far = passed_on(flights[0][1], None)
    over = [flights[2 * layer][1][-1][:16, :LANES] for layer in range(1, layers) if flights[2 * layer][1]]
    weights = {0: gathered(*flights[0], first_far, over)}
    next_fars = {}
    for layer in range(1, layers):
        near = flights[2 * layer][1]
        if near:
            near = [near[0] + zero_after(weights[0][0][0, :1, :1]).astype(low), *near[1:]]
        next_fars[layer] = passed_on(near, None)

    def gathered_both(pack, after):
        return lax.all_gather(ordered(pack, after), ("mp", "dp")).reshape((halves, owners) + pack.shape)

    weights[1] = gathered_both(packs_of[0][1], flights[0][1])
    wait = zero_after((first_far[0] if first_far else weights[0][0])[:1, :1, :1])

    def over_cores(values):
        return jnp.concatenate([values, swapped(values)], axis=values.ndim - 1)

    widths = over_cores(jnp.concatenate([head_conv_taps, gated_norm_gain[:, None]], axis=1)).astype(full)
    settings = over_cores(head_settings)
    widths, settings, documents = widths + wait, settings + wait, documents + wait.astype(jnp.int32)
    maps_taps = jnp.pad(map_conv_taps.astype(full), ((0, 0), (0, 1), (0, 0)))
    skips = jnp.broadcast_to(settings[:, 2:3, :, None], (layers, 1, heads, head_width)).reshape(layers, 1, inner)

    def wide_rows(values):
        return jnp.pad(values, ((0, 0), (0, 0), (0, channels - values.shape[2])))

    tables = jnp.concatenate(
        [
            jnp.concatenate([widths, maps_taps], axis=2),
            wide_rows(skips),
            wide_rows(input_norm_gain.astype(full)[:, None]),
            wide_rows(settings[:, :2]),
            jnp.zeros((layers, TABLE_ROWS - DECAY - 1, channels), full),
        ],
        axis=1,
    )
    head_of = np.arange(inner)[None, :] // head_width
    spread_one = (np.arange(LANES)[:, None] == head_of).astype(np.float32)
    spread_two = jnp.asarray(np.concatenate([spread_one, spread_one], axis=0), low)

    begin = place * length
    ends = jnp.concatenate([jnp.full((PAD,), -1, jnp.int32), documents, jnp.full((PAD,), -2, jnp.int32)])
    near = lax.dynamic_slice_in_dim(ends, begin, length + 2 * PAD)
    own = near[PAD : PAD + length]
    lane = jnp.arange(CONV * LANES)[None, :] // LANES

    def same_as(lag):
        return (own == near[PAD + lag : PAD + lag + length])[:, None]

    front = jnp.where(same_as(-1), 0.0, RESET)
    leads = same_as(CONV - 1)
    for lag in range(1, CONV):
        front = jnp.where(lane == lag - 1, jnp.where(same_as(-lag), 1.0, 0.0), front)
    for lag in range(1, CONV - 1):
        leads = jnp.where(lane[:, : -LANES] == lag - 1, same_as(lag), leads)
    front, leads = front.astype(low), leads.astype(low)
    which = jnp.arange(ranks)[None, :] // rank
    mask = jnp.zeros((length, ranks), jnp.bool_)
    for document in range(chosen.shape[0]):
        mask = mask | ((own == document)[:, None] & (which == chosen[document]))
    mask = mask.astype(low)

    flops_in = 2 * length * width * (2 * inner + 3 * LANES)
    flops_out = 2 * length * width * inner
    flops_scan = 4 * length * SPAN * inner

    h = h_first
    kept = []
    for layer in range(layers):
        first_own, first_other = weights[2 * layer]
        normed, spread, rows, dt_raw = kernel_call(
            functools.partial(project_rows_kernel, packs, heads_local, layer),
            [
                shape((length, width), low),
                shape((length, ranks), low),
                shape((length, channels), low),
                shape((length, LANES), full),
            ],
            [core_in, h, tables, mask, first_own, first_other],
            scalars=1,
            flops=flops_in // 2,
            name="project_rows",
        )
        halo = moved(rows[length - PAD :], "seq", 1)
        reached = []
        if layer + 1 < layers:
            weights[2 * layer + 2] = gathered(*flights[2 * layer + 2], next_fars[layer + 1], [rows[:16, :LANES]])
            reached = [weights[2 * layer + 2][0][0, :16, :LANES]]
        act, xdt, dt, cum, flat, begin_state, end_state = kernel_call(
            functools.partial(states_kernel, inner, layer),
            [
                shape((length, channels), low),
                shape((length, inner), low),
                shape((length, LANES), full),
                shape((length, LANES), full),
                shape((LANES, length), full),
                shape((length // SPAN, states, inner), low),
                shape((states + 16, inner), low),
            ],
            [rows, halo, tables, front, dt_raw, spread_two, *reached],
            scratch=[pltpu.VMEM((length + PAD, channels), full), pltpu.VMEM((states, inner), full)],
            flops=flops_scan,
            name="states",
        )
        arrived = [moved(end_state, "seq", d) for d in range(1, pieces)]
        y_local = kernel_call(
            functools.partial(intra_kernel, inner, head_width, layer),
            [shape((length, inner), low)],
            [act, xdt, cum, flat, begin_state, tables, spread_two],
            flops=flops_scan,
            name="intra",
        )[0]
        wide = weights[2 * layer + 1]
        if layer + 1 < layers:
            weights[2 * layer + 3] = gathered_both(packs_of[layer + 1][1], act)
        gate = kernel_call(
            functools.partial(project_gate_kernel, packs),
            [shape((length, inner), full)],
            [core_in, normed, spread, wide],
            scalars=1,
            flops=flops_in // 2,
            name="project_gate",
        )[0]
        h_next, y, normal, spread_out, coming = kernel_call(
            functools.partial(output_kernel, packs, len(arrived), layer),
            [
                shape((length, width), full),
                shape((length, inner), low),
                shape((length, inner), low),
                shape((length, ranks), low),
                shape((states, inner), low),
            ],
            [core_in, h, y_local, gate, act, cum, tables, mask, first_own, first_other, wide, spread_two, *arrived],
            scalars=1,
            flops=flops_out,
            name="output",
        )
        kept.append(
            (h, normed, spread, gate, rows, halo, dt_raw, act, xdt, dt, cum, flat,
             begin_state, y, normal, spread_out, coming)
        )
        h = h_next
    mixed_own = h.astype(low)

    late = zero_after(kept[-1][5][:1, :1]).astype(jnp.int32)
    upstream = lax.dynamic_index_in_dim(output_cotangent, core + late, 0, False)[0]
    shares = []
    for layer in reversed(range(layers)):
        first_own, first_other = weights[2 * layer]
        wide = weights[2 * layer + 1]
        (h, normed, spread, gate, rows, halo, dt_raw, act, xdt, dt, cum, flat,
         begin_state, y, normal, spread_out, coming) = kept[layer]
        dgate, dy, own_grad, *early = kernel_call(
            functools.partial(output_back_kernel, packs, layer),
            [
                shape((length, inner), low),
                shape((length, inner), low),
                shape((states + 16, inner), low),
                *[shape((ranks, half + part), low)] * 2,
            ],
            [core_in, upstream, y, gate, normal, spread_out, act, cum, tables, mask, first_own, first_other, wide,
             spread_two],
            scratch=[pltpu.VMEM((length, ranks), low), pltpu.VMEM((length, width), low)],
            scalars=1,
            flops=flops_out,
            name="output_back",
        )
        arrived = [moved(own_grad, "seq", -d) for d in range(1, pieces)]
        u, db, dc = kernel_call(
            functools.partial(intra_back_kernel, inner, head_width),
            [shape((length, inner), low), shape((length, LANES), full), shape((length, LANES), full)],
            [act, xdt, dy, cum, flat],
            flops=2 * flops_scan,
            name="intra_back",
        )
        dn, dl, g_gate = kernel_call(
            functools.partial(gate_back_kernel, packs),
            [shape((length, width), full), shape((length, ranks), full), shape((halves, ranks, half), low)],
            [core_in, dgate, spread, wide],
            scalars=1,
            flops=flops_in // 2,
            name="gate_back",
        )
        reached = [share[:PAD, :LANES] for share in shares]
        dconv, ddt = kernel_call(
            functools.partial(scan_back_kernel, inner, len(arrived), layer),
            [shape((length, channels), low), shape((length, LANES), low)],
            [rows, halo, tables, front, act, xdt, dy, y, u, db, dc, dt, cum, dt_raw, begin_state, coming,
             spread_two, *arrived, *reached],
            scratch=[
                pltpu.VMEM((length + PAD, channels), full),
                pltpu.VMEM((states, inner), full),
                pltpu.VMEM((length, channels), full),
            ],
            flops=2 * flops_scan,
            name="scan_back",
        )
        after = moved(dconv[:PAD], "seq", -1)
        shares = [over_dp(share) for share in shares]
        reached = [share[:PAD, :LANES] for share in shares]
        dh, *grads = kernel_call(
            functools.partial(project_back_kernel, packs, heads_local, layer),
            [
                shape((length, width), full if layer > 0 else low),
                *[shape((ranks, 2 * half + 2 * LANES + part + sum(e.shape[1] for e in early[:1])), low)] * 2,
            ],
            [core_in, upstream, h, tables, mask, dconv, after, leads, ddt, dn, dl, spread, normed, first_own,
             first_other, g_gate, *early, *reached],
            scratch=[
                pltpu.VMEM((length + PAD, channels), full),
                pltpu.VMEM((length, channels), low),
                pltpu.VMEM((length, width), full),
            ],
            scalars=1,
            flops=flops_in // 2,
            name="project_back",
        )
        upstream = dh
        shares.append(over_mp(*grads))

    behind = [over_seq(share) for share in shares[:-1]]
    whole = jnp.stack([over_seq(ordered(over_dp(shares[-1]), behind)), *reversed(behind)])
    zx, maps, steps, down_in, down_out, up_out = jnp.split(
        whole,
        [2 * half, 2 * half + LANES, 2 * half + 2 * LANES, 2 * half + 2 * LANES + part, 3 * half + 2 * LANES + part],
        axis=2,
    )
    own_shared = jnp.concatenate([maps, down_in, up_out], axis=2)
    other_shared = swapped(own_shared)
    in_order = [jnp.where(core == m, own_shared, other_shared) for m in range(halves)]
    maps, down_in, up_out = (
        [entry[:, :, first:last] for entry in in_order]
        for first, last in ((0, LANES), (LANES, LANES + part), (LANES + part, LANES + 2 * part))
    )
    shared_gradient = jnp.concatenate([*down_in, *maps, *up_out], axis=2).reshape(adapter_shared.shape)
    broad_gradient = jnp.concatenate([zx, down_out], axis=2).reshape(adapter_broad.shape)
    step_gradient = steps[:, :, :heads_local].reshape(adapter_step.shape)
    local_sq = (
        jnp.sum(broad_gradient * broad_gradient)
        + jnp.sum(step_gradient * step_gradient)
        + jnp.sum(own_shared * own_shared)
    )
    squares = jnp.broadcast_to(local_sq, (8, LANES))
    squares = squares + swapped(squares)
    total_sq = squares
    for distance in range(1, owners):
        total_sq = total_sq + moved(squares, "dp", distance, True)
    grad_norm = jnp.sqrt(total_sq[0, 0])
    scale_factor = clip_max / jnp.maximum(grad_norm, clip_max)
    revised_broad, fresh_first_broad, fresh_square_broad = adamw_update(
        adapter_broad, broad_gradient, broad_first_moment, broad_second_moment, scale_factor
    )
    revised_step, fresh_first_step, fresh_square_step = adamw_update(
        adapter_step, step_gradient, step_first_moment, step_second_moment, scale_factor
    )
    revised_shared, fresh_first_shared, fresh_square_shared = adamw_update(
        adapter_shared, shared_gradient, shared_first_moment, shared_second_moment, scale_factor
    )

    def both(values):
        other = swapped(values)
        return jnp.stack([jnp.where(core == m, values, other) for m in range(halves)])[:, None]

    return (
        both(mixed_own),
        both(upstream),
        grad_norm,
        revised_broad,
        revised_step,
        revised_shared,
        fresh_first_broad,
        fresh_first_step,
        fresh_first_shared,
        fresh_square_broad,
        fresh_square_step,
        fresh_square_shared,
        revised_broad.astype(low),
        revised_step.astype(low),
        revised_shared.astype(low),
    )


def solution(mesh):
    placed = (
        P(None, "dp", "seq", None),
        P(None, "dp", "seq", None),
        P(None, "dp", None),
        P(None, "dp", None),
        P(),
        P(None, "dp", None, "mp"),
        P(None, "dp", None),
        P(None, "dp", "mp"),
        P(None, "mp", "dp"),
        P(None, None, "mp"),
        P(),
        P(None, None, "mp"),
        P(None, "mp"),
        P(None, "dp", None, None, "mp"),
        P(None, "dp", None, "mp"),
        P(None, "dp", None, None),
        P(None, "dp", None, None, "mp"),
        P(None, "dp", None, "mp"),
        P(None, "dp", None, None),
        P(None, "dp", None, None, "mp"),
        P(None, "dp", None, "mp"),
        P(None, "dp", None, None),
    )
    return jax.shard_map(
        per_device,
        mesh=mesh,
        in_specs=placed,
        out_specs=(
            P(None, "dp", "seq", None),
            P(None, "dp", "seq", None),
            P(),
            P(None, "dp", None, None, "mp"),
            P(None, "dp", None, "mp"),
            P(None, "dp", None, None),
            P(None, "dp", None, None, "mp"),
            P(None, "dp", None, "mp"),
            P(None, "dp", None, None),
            P(None, "dp", None, None, "mp"),
            P(None, "dp", None, "mp"),
            P(None, "dp", None, None),
            P(None, "dp", None, None, "mp"),
            P(None, "dp", None, "mp"),
            P(None, "dp", None, None),
        ),
        check_vma=False,
    )
```

```python
import functools

import jax
import jax.numpy as jnp
import numpy as np
from jax import lax
from jax.experimental import pallas as pl
from jax.experimental.pallas import tpu as pltpu
from jax.sharding import PartitionSpec as P

CONV = 4
STEP = 10
LANES = 128
SPAN = 128
PAD = 8
RESET = -128.0
GAIN_TWO, SKIP, GAIN, STEP_BIAS, DECAY, TABLE_ROWS = 5, 6, 7, 8, 9, 16

norm_eps = 1e-05
learn_rate = 0.04
beta_one = 0.5
beta_two = 0.5
weight_decay = 0.01
adam_eps = 1e-08
clip_max = 1.0
low = jnp.bfloat16
full = jnp.float32


def nn(a, b):
    return lax.dot_general(a, b, (((1,), (0,)), ((), ())), preferred_element_type=full)


def nt(a, b):
    return lax.dot_general(a, b, (((1,), (1,)), ((), ())), preferred_element_type=full)


def tn(a, b):
    return lax.dot_general(a, b, (((0,), (0,)), ((), ())), preferred_element_type=full)


def two_parts(values, axis):
    high = values.astype(low)
    rest = (values - high.astype(full)).astype(low)
    return jnp.concatenate([high, rest], axis=axis)


def three_parts(values, axis):
    high = values.astype(low)
    rest = values - high.astype(full)
    middle = rest.astype(low)
    last = (rest - middle.astype(full)).astype(low)
    return jnp.concatenate([high, middle, last], axis=axis)


def widen(values, spread_two):
    return nn(two_parts(values, 1), spread_two)


def per_head(values, spread_two):
    heads = spread_two[:LANES]
    high = values.astype(low)
    rest = (values - high.astype(full)).astype(low)
    return nt(high, heads) + nt(rest, heads)


def triangle(kind):
    rows = lax.broadcasted_iota(jnp.int32, (SPAN, SPAN), 0)
    columns = lax.broadcasted_iota(jnp.int32, (SPAN, SPAN), 1)
    return rows >= columns if kind == "lower" else rows <= columns


def cumulate(values, kind):
    keep = triangle(kind).astype(full).astype(low)
    return nn(jnp.concatenate([keep, keep, keep], axis=1), three_parts(values, 0))


def sigmoid(values):
    return 1.0 / (1.0 + jnp.exp(-values))


def kernel_call(body, outs, ins, scratch=(), flops=0, name=None, limit=20, scalars=0):
    moved = sum(a.size * a.dtype.itemsize for a in list(ins) + list(outs))
    whole = pl.BlockSpec(memory_space=pltpu.VMEM)
    return pl.pallas_call(
        body,
        out_shape=tuple(outs),
        in_specs=[pl.BlockSpec(memory_space=pltpu.SMEM)] * scalars + [whole] * (len(ins) - scalars),
        out_specs=tuple([whole] * len(outs)),
        scratch_shapes=list(scratch),
        compiler_params=pltpu.CompilerParams(vmem_limit_bytes=limit * 2**20),
        cost_estimate=pl.CostEstimate(flops=flops, bytes_accessed=moved, transcendentals=0),
        name=name,
    )(*ins)


def shape(dims, kind):
    return jax.ShapeDtypeStruct(dims, kind)


def assemble_kernel(owners, pieces, place, pack, *rest):
    near, far, out = rest[: owners - 1], rest[owners - 1 : owners + pieces - 2], rest[-1]
    quarter = pack.shape[0] // pieces
    owner, piece = place[0], place[1]
    out[owner] = pack[...]
    for i in range(owners - 1):
        source = lax.rem(owner + (owners - 1 - i), owners)
        out[source, pl.ds(pl.multiple_of(piece * quarter, 16), quarter)] = near[i][...]
        for j in range(pieces - 1):
            sender = lax.rem(piece + (pieces - 1 - j), pieces)
            out[source, pl.ds(pl.multiple_of(sender * quarter, 16), quarter)] = far[j][i]


def sections(ref, first, last, columns=slice(None), core=None):
    if core is not None:
        return jnp.concatenate([ref[core, d, first:last, columns] for d in range(ref.shape[1])], axis=0)
    return jnp.concatenate([ref[d, first:last, columns] for d in range(ref.shape[0])], axis=0)


def core_sections(ref, core, first, last):
    return sections(ref, first, last, slice(None), core)


class Packs:
    def __init__(self, rows, adapter_rows, half, part):
        self.width, self.adapt = (0, rows), (rows, rows + adapter_rows)
        self.ends = (rows + adapter_rows, rows + 2 * adapter_rows)
        self.x, self.maps = slice(0, half), slice(half, half + LANES)
        self.steps = slice(half + LANES, half + 2 * LANES)
        self.mixed = slice(0, half + LANES)
        self.down, self.up = slice(0, part), slice(part, 2 * part)
        base = rows + adapter_rows
        self.out, self.out_down = (base, base + rows), (base + rows, base + rows + adapter_rows)
        self.half, self.part, self.rows = half, part, rows


def step_weights(own, other, first, last, columns, local):
    lane = lax.broadcasted_iota(jnp.int32, (1, LANES), 1)
    mine = sections(own, first, last, columns).astype(full)
    theirs = sections(other, first, last, columns).astype(full)
    return jnp.where(lane < local, mine, jnp.where(lane < 2 * local, theirs, 0.0)).astype(low)


def project_rows_kernel(packs, local, layer, core, h, tables, mask, own, other, normed_o, spread_o, rows_o, dt_o):
    values = h[...].astype(full)
    half, part = packs.half, packs.part
    scale = lax.rsqrt(jnp.mean(values * values, axis=1, keepdims=True) + norm_eps)
    normed_o[...] = (values * scale * tables[layer, GAIN : GAIN + 1, : h.shape[1]]).astype(low)
    normed = normed_o[...]
    places = ((own, core[0], 0), (other, 1 - core[0], half))
    down = jnp.zeros((h.shape[0], mask.shape[1]), full)
    for ref, index, _ in places:
        columns = pl.ds(pl.multiple_of(index * part, LANES), part)
        down = down + nt(normed_o[:, columns], sections(ref, *packs.ends, packs.down))
    spread = down.astype(low) * mask[...]
    spread_o[...] = spread
    for ref, index, place in places:
        made = nn(normed, sections(ref, *packs.width, packs.mixed)) + nn(spread, sections(ref, *packs.adapt, packs.mixed))
        rows_o[:, place : place + half] = made[:, :half].astype(low)
        rows_o[:, pl.ds(pl.multiple_of(2 * half + index * LANES, LANES), LANES)] = made[:, half:].astype(low)
    w_dt = step_weights(own, other, *packs.width, packs.steps, local)
    b_dt = step_weights(own, other, *packs.adapt, packs.steps, local)
    dt_o[...] = nn(normed, w_dt) + nn(spread, b_dt)


def project_gate_kernel(packs, core, normed, spread, wide, gate_o):
    half = packs.half
    for index, place in ((core[0], 0), (1 - core[0], half)):
        gate_o[:, place : place + half] = nn(normed[...], core_sections(wide, index, *packs.width)) + nn(
            spread[...], core_sections(wide, index, *packs.adapt)
        )


def conv_chunk(ext, same, taps, begin, columns):
    window = ext[pl.ds(begin, SPAN + PAD), columns]
    summed = taps[CONV : CONV + 1, columns] + taps[0:1, columns] * window[PAD:]
    for lag in range(1, CONV):
        summed = summed + taps[lag : lag + 1, columns] * window[PAD - lag : PAD - lag + SPAN] * same[lag - 1]
    return summed


def same_documents(front, span):
    return [front[span, i * LANES : (i + 1) * LANES].astype(full) for i in range(CONV - 1)]


def fill_extended(ext, halo, rows):
    ext[0:PAD, :] = halo[...].astype(full)
    ext[PAD : PAD + rows.shape[0], :] = rows[...].astype(full)


def states_kernel(
    inner, layer, rows, halo, tables, front, dt_raw, spread_two, *rest,
):
    act_o, slope_o, xdt_o, dt_o, cum_o, flat_o, begin_o, end_o, ext, state = rest[-10:]
    length = rows.shape[0]
    channels = rows.shape[1]
    table = tables.at[layer]
    fill_extended(ext, halo, rows)
    state[...] = jnp.zeros_like(state)

    def block(k, so_far):
        begin = pl.multiple_of(k * SPAN, SPAN)
        span = pl.ds(begin, SPAN)
        same = same_documents(front, span)
        for c in range(0, channels, LANES):
            columns = slice(c, c + LANES)
            summed = conv_chunk(ext, same, table, begin, columns)
            sig = sigmoid(summed)
            act_o[span, columns] = (summed * sig).astype(low)
            slope_o[span, columns] = (sig * (1.0 + summed * (1.0 - sig))).astype(low)
        raw = dt_raw[span, :] + table[STEP_BIAS : STEP_BIAS + 1, :LANES]
        dt = jnp.maximum(raw, 0.0) + jnp.log1p(jnp.exp(-jnp.abs(raw)))
        jump = front[span, (CONV - 1) * LANES :].astype(full)
        cum = cumulate(jump - jnp.exp(table[DECAY : DECAY + 1, :LANES]) * dt, "lower")
        dt_o[span, :] = dt
        cum_o[span, :] = cum
        flat_o[:, span] = cum.T
        total = cum[SPAN - 1 : SPAN, :]
        xdt = (act_o[span, 0:inner].astype(full) * widen(dt, spread_two[...])).astype(low)
        xdt_o[span, :] = xdt
        tail = widen(jnp.exp(total - cum), spread_two[...])
        b_map = act_o[span, inner : inner + LANES]
        begin_o[k] = state[...].astype(low)
        keep = widen(jnp.broadcast_to(jnp.exp(total), (8, LANES)), spread_two[...])[0:1]
        state[...] = state[...] * keep + tn(b_map, (xdt.astype(full) * tail).astype(low))
        return so_far + total

    total = lax.fori_loop(0, length // SPAN, block, jnp.zeros((1, LANES), full))
    put_message(end_o, state[...], total, spread_two[...])


def intra_kernel(inner, head_width, layer, act, xdt, cum, flat, begin_state, tables, spread_two, y_o):
    length = act.shape[0]
    keep = triangle("lower")
    left = lax.broadcasted_iota(jnp.int32, (SPAN, LANES), 1) < head_width

    def block(k, carry):
        begin = pl.multiple_of(k * SPAN, SPAN)
        span = pl.ds(begin, SPAN)
        b_map = act[span, inner : inner + LANES]
        c_map = act[span, inner + LANES : inner + 2 * LANES]
        scores = nt(c_map, b_map)
        cum_now = cum[span, :]
        entry = widen(jnp.exp(cum_now), spread_two[...])
        before = nn(c_map, begin_state[k])
        for pair in range(inner // LANES):
            columns = slice(pair * LANES, (pair + 1) * LANES)
            mixing = []
            for head in (2 * pair, 2 * pair + 1):
                gap = cum_now[:, head : head + 1] - flat[head : head + 1, span]
                mixing.append((scores * jnp.exp(jnp.where(keep, gap, -1e30))).astype(low))
            x_pair = xdt[span, columns]
            nothing = jnp.zeros_like(x_pair)
            x_two = jnp.concatenate([jnp.where(left, x_pair, nothing), jnp.where(left, nothing, x_pair)], axis=0)
            intra = nn(jnp.concatenate(mixing, axis=1), x_two)
            y_o[span, columns] = (
                intra
                + entry[:, columns] * before[:, columns]
                + tables[layer, SKIP : SKIP + 1, columns] * act[span, columns].astype(full)
            ).astype(low)
        return carry

    lax.fori_loop(0, length // SPAN, block, 0)


def put_message(out, values, total, spread_two):
    out[:LANES] = values.astype(low)
    high = total.astype(low).astype(full)
    middle = (total - high).astype(low).astype(full)
    parts = jnp.concatenate([high, middle, total - high - middle, jnp.zeros((13, LANES), full)], axis=0)
    out[LANES:] = nn(parts.astype(low), spread_two[:LANES]).astype(low)


def combine(messages):
    total = messages[0][:LANES].astype(full)
    decay = 0.0
    for i in range(1, len(messages)):
        decay = decay + jnp.sum(messages[i - 1][LANES : LANES + 16].astype(full), axis=0, keepdims=True)
        total = total + messages[i][:LANES].astype(full) * jnp.exp(decay)
    return total


def output_kernel(
    packs, count, layer, core, h, y_local, gate, act, cum, tables, mask, first_own, first_other, wide, spread_two, *rest
):
    parts, rest = rest[:count], rest[count:]
    h_o, y_o, spread_o, coming_o, normal_o = rest
    length = h.shape[0]
    half, part = packs.half, packs.part
    inner = 2 * half
    coming = combine(parts).astype(low)
    coming_o[...] = coming
    before = jnp.zeros((1, LANES), full)
    for k in range(length // SPAN):
        span = slice(k * SPAN, (k + 1) * SPAN)
        cum_now = cum[span, :]
        carry = widen(jnp.exp(cum_now + before), spread_two[...])
        before = before + cum_now[SPAN - 1 : SPAN, :]
        c_map = act[span, inner + LANES : inner + 2 * LANES]
        y = y_local[span, :].astype(full) + carry * nn(c_map, coming)
        y_o[span, :] = y.astype(low)
        z = gate[span, :]
        gated = y * z * sigmoid(z)
        scale = lax.rsqrt(jnp.mean(gated * gated, axis=1, keepdims=True) + norm_eps)
        normal_o[span, :] = (gated * scale * tables[layer, GAIN_TWO : GAIN_TWO + 1, :inner]).astype(low)
    second = jnp.zeros((length, LANES), full)
    branch = h[...].astype(full)
    for index, place in ((core[0], 0), (1 - core[0], half)):
        normal = normal_o[:, place : place + half]
        second = second + nt(normal, core_sections(wide, index, *packs.out_down))
        branch = branch + nt(normal, core_sections(wide, index, *packs.out))
    h_o[...] = branch.astype(h_o.dtype)
    spread = second.astype(low) * mask[...]
    spread_o[...] = spread
    for ref, index in ((first_own, core[0]), (first_other, 1 - core[0])):
        columns = pl.ds(pl.multiple_of(index * part, LANES), part)
        h_o[:, columns] = (h_o[:, columns] + nn(spread, sections(ref, *packs.ends, packs.up))).astype(h_o.dtype)


def output_back_kernel(
    packs, layer, core, upstream, y, gate, spread_out, act, cum, tables, mask, first_own, first_other, wide, spread_two,
    *rest,
):
    found, rest = rest[:-7], rest[-7:]
    dgate_o, dy_o, own_o, *grads_o, seconds, lows = rest
    length = y.shape[0]
    half, part = packs.half, packs.part
    inner = 2 * half
    first = grads_o[0].shape[1] - half - part
    for i in range(len(found)):
        grads_o[i][:, :first] = found[i][...]
    lows[...] = upstream[...].astype(low)
    down = jnp.zeros(seconds.shape, full)
    for i, (ref, index) in enumerate(((first_own, core[0]), (first_other, 1 - core[0]))):
        now = lows[:, pl.ds(pl.multiple_of(index * part, LANES), part)]
        down = down + nt(now, sections(ref, *packs.ends, packs.up))
        grads_o[i][:, first + half :] = tn(spread_out[...], now).astype(low)
    second = down.astype(low) * mask[...]
    seconds[...] = second
    grad = jnp.zeros((LANES, inner), full)
    down_grad = jnp.zeros((LANES, inner), full)
    before = jnp.zeros((1, LANES), full)
    for k in range(length // SPAN):
        span = slice(k * SPAN, (k + 1) * SPAN)
        up_now = lows[span, :]
        grads = []
        for index in (core[0], 1 - core[0]):
            grads.append(
                nn(up_now, core_sections(wide, index, *packs.out))
                + nn(seconds[span, :], core_sections(wide, index, *packs.out_down))
            )
        weighted = jnp.concatenate(grads, axis=1) * tables[layer, GAIN_TWO : GAIN_TWO + 1, :inner]
        y_now = y[span, :].astype(full)
        z = gate[span, :]
        sig = sigmoid(z)
        silu = z * sig
        gated = y_now * silu
        scale = lax.rsqrt(jnp.mean(gated * gated, axis=1, keepdims=True) + norm_eps)
        normal = (gated * scale * tables[layer, GAIN_TWO : GAIN_TWO + 1, :inner]).astype(low)
        down_grad = down_grad + tn(seconds[span, :], normal)
        mean_in = jnp.mean(weighted * gated, axis=1, keepdims=True)
        grad_gated = scale * weighted - gated * (scale * scale * scale * mean_in)
        dgate_o[span, :] = (grad_gated * y_now * sig * (1.0 + z * (1.0 - sig))).astype(low)
        dy = grad_gated * silu
        dy_o[span, :] = dy.astype(low)
        cum_now = cum[span, :]
        carry = widen(jnp.exp(cum_now + before), spread_two[...])
        before = before + cum_now[SPAN - 1 : SPAN, :]
        grad = grad + tn(act[span, inner + LANES : inner + 2 * LANES], (carry * dy).astype(low))
    for i in range(2):
        grads_o[i][:, first : first + half] = down_grad[:, i * half : (i + 1) * half].astype(low)
    put_message(own_o, grad, before, spread_two[...])


def intra_back_kernel(inner, head_width, act, xdt, dy, cum, flat, u_o, db_o, dc_o):
    length = act.shape[0]
    keep = triangle("upper")
    left = lax.broadcasted_iota(jnp.int32, (SPAN, LANES), 1) < head_width

    def block(k, carry):
        begin = pl.multiple_of(k * SPAN, SPAN)
        span = pl.ds(begin, SPAN)
        b_map = act[span, inner : inner + LANES]
        c_map = act[span, inner + LANES : inner + 2 * LANES]
        scores = nt(b_map, c_map)
        cum_now = cum[span, :]
        dscores = jnp.zeros((SPAN, SPAN), full)
        for pair in range(inner // LANES):
            columns = slice(pair * LANES, (pair + 1) * LANES)
            dy_pair = dy[span, columns]
            nothing = jnp.zeros_like(dy_pair)
            dy_two = jnp.concatenate([jnp.where(left, dy_pair, nothing), jnp.where(left, nothing, dy_pair)], axis=0)
            products = nt(xdt[span, columns], dy_two)
            mixing = []
            for i, head in enumerate((2 * pair, 2 * pair + 1)):
                gap = flat[head : head + 1, span] - cum_now[:, head : head + 1]
                decay = jnp.exp(jnp.where(keep, gap, -1e30))
                mixing.append((scores * decay).astype(low))
                dscores = dscores + products[:, i * SPAN : (i + 1) * SPAN] * decay
            u_o[span, columns] = nn(jnp.concatenate(mixing, axis=1), dy_two).astype(low)
        dlow = dscores.astype(low)
        db_o[span, :] = nn(dlow, c_map)
        dc_o[span, :] = tn(dlow, b_map)
        return carry

    lax.fori_loop(0, length // SPAN, block, 0)


def scan_back_kernel(
    inner, count, layer, slope, tables, act, xdt, dy, y, u, db_in, dc_in, dt, cum, dt_raw,
    begin_state, coming, spread_two, *rest,
):
    parts = rest[:count]
    dconv_o, ddt_o, grad = rest[-3:]
    length = act.shape[0]
    blocks = length // SPAN
    table = tables.at[layer]
    skip = table[SKIP : SKIP + 1, :inner]
    grad[...] = combine(parts)
    ends = [cum[(k + 1) * SPAN - 1 : (k + 1) * SPAN, :] for k in range(blocks)]
    for k in reversed(range(blocks)):
        span = slice(k * SPAN, (k + 1) * SPAN)
        cum_now = cum[span, :]
        total = ends[k]
        before = sum(ends[:k], jnp.zeros((1, LANES), full))
        b_map = act[span, inner : inner + LANES]
        c_map = act[span, inner + LANES : inner + 2 * LANES]
        grad_low = grad[...].astype(low)
        tail = widen(jnp.exp(total - cum_now), spread_two[...])
        entry = widen(jnp.exp(cum_now), spread_two[...])
        rows_wide = widen(jnp.exp(jnp.concatenate([total, before] * 4, axis=0)), spread_two[...])
        keep, carry = rows_wide[0:1], rows_wide[1:2]
        x = act[span, 0:inner].astype(full)
        x_dt = xdt[span, :].astype(full)
        from_later = tail * nn(b_map, grad_low)
        v = u[span, :].astype(full) + from_later
        state = begin_state[k].astype(full) + carry * coming[...].astype(full)
        dy_now = dy[span, :].astype(full)
        db = db_in[span, :] + nt((x_dt * tail).astype(low), grad_low)
        entry_dy = (entry * dy_now).astype(low)
        dc = dc_in[span, :] + nt(entry_dy, state.astype(low))
        kept = keep * grad[...]
        end_rows = jnp.sum(x_dt * from_later, axis=0, keepdims=True) + jnp.sum(kept * state, axis=0, keepdims=True)
        grad[...] = kept + tn(c_map, entry_dy)
        y_scan = y[span, :].astype(full) - skip * x
        dcum = per_head(dy_now * y_scan - x_dt * v, spread_two[...])
        at_end = per_head(jnp.broadcast_to(end_rows, (8, inner)), spread_two[...])[0:1]
        ddecay = cumulate(dcum, "upper") + at_end
        raw = dt_raw[span, :] + table[STEP_BIAS : STEP_BIAS + 1, :LANES]
        ddt = per_head(x * v, spread_two[...]) - ddecay * jnp.exp(table[DECAY : DECAY + 1, :LANES])
        ddt_o[span, :] = (ddt * sigmoid(raw)).astype(low)
        dx = widen(dt[span, :], spread_two[...]) * v + skip * dy_now
        dconv_o[span, 0:inner] = (dx * slope[span, 0:inner].astype(full)).astype(low)
        for place, part in ((inner, db), (inner + LANES, dc)):
            columns = slice(place, place + LANES)
            dconv_o[span, columns] = (part * slope[span, columns].astype(full)).astype(low)


def gate_back_kernel(packs, core, dgate, spread, wide, dn_o, dl_o, grad_o):
    half = packs.half
    dn = dl = 0.0
    for i, index in enumerate((core[0], 1 - core[0])):
        piece = dgate[:, i * half : (i + 1) * half]
        dn = dn + nt(piece, core_sections(wide, index, *packs.width))
        dl = dl + nt(piece, core_sections(wide, index, *packs.adapt))
        grad_o[i] = tn(spread[...], piece).astype(grad_o.dtype)
    dn_o[...] = dn
    dl_o[...] = dl


def project_back_kernel(
    packs, local, layer, core, upstream, h, tables, mask, dconv, after, leads, ddt, dn_in, dl_in, spread, normed, own, other,
    *rest,
):
    found, rest = rest[:-6], rest[-6:]
    dh_o, *grads_o, ext, drows, dn_s = rest
    gate_grad, found = found[0], found[1:3]
    length = h.shape[0]
    channels = dconv.shape[1]
    half, part = packs.half, packs.part
    ext[0:length, :] = dconv[...].astype(full)
    ext[length : length + PAD, :] = after[...].astype(full)

    def block(k, carry):
        begin = pl.multiple_of(k * SPAN, SPAN)
        span = pl.ds(begin, SPAN)
        same = same_documents(leads, span)
        for c in range(0, channels, LANES):
            columns = slice(c, c + LANES)
            window = ext[pl.ds(begin, SPAN + PAD), columns]
            total = tables[layer, 0:1, columns] * window[:SPAN]
            for lag in range(1, CONV):
                total = total + tables[layer, lag : lag + 1, columns] * window[lag : lag + SPAN] * same[lag - 1]
            drows[span, columns] = total.astype(low)
        return carry

    lax.fori_loop(0, length // SPAN, block, 0)
    step = ddt[...]
    dn = dn_in[...] + nt(step, step_weights(own, other, *packs.width, packs.steps, local))
    dl = dl_in[...] + nt(step, step_weights(own, other, *packs.adapt, packs.steps, local))
    step_grad = tn(spread[...], step)
    places = ((own, core[0]), (other, 1 - core[0]))
    for i, (ref, index) in enumerate(places):
        maps = drows[:, pl.ds(pl.multiple_of(2 * half + index * LANES, LANES), LANES)]
        piece = jnp.concatenate([drows[:, i * half : (i + 1) * half], maps], axis=1)
        dn = dn + nt(piece, sections(ref, *packs.width, packs.mixed))
        dl = dl + nt(piece, sections(ref, *packs.adapt, packs.mixed))
        grad_o = grads_o[i]
        grad_o[:, :half] = gate_grad[i]
        grad_o[:, half : 2 * half + LANES] = tn(spread[...], piece).astype(low)
        turned = step_grad if i == 0 else pltpu.roll(step_grad, LANES - local, 1)
        grad_o[:, 2 * half + LANES : 2 * half + 2 * LANES] = turned.astype(low)
    back = dl.astype(low) * mask[...]
    dn_s[...] = dn
    for i, (ref, index) in enumerate(places):
        columns = pl.ds(pl.multiple_of(index * part, LANES), part)
        begin = 2 * half + 2 * LANES
        grads_o[i][:, begin : begin + part] = tn(back, normed[:, columns]).astype(low)
        if found:
            grads_o[i][:, begin + part :] = found[i][...]
        dn_s[:, columns] = dn_s[:, columns] + nn(back, sections(ref, *packs.ends, packs.down))
    dn = dn_s[...]
    values = h[...].astype(full)
    scale = lax.rsqrt(jnp.mean(values * values, axis=1, keepdims=True) + norm_eps)
    weighted = dn * tables[layer, GAIN : GAIN + 1, : h.shape[1]]
    mean_in = jnp.mean(weighted * values, axis=1, keepdims=True)
    dh = upstream[...].astype(full) + scale * weighted - values * (scale * scale * scale * mean_in)
    dh_o[...] = dh.astype(dh_o.dtype)


def moved(block, axis, distance, wrap=False):
    count = lax.axis_size(axis)
    route = [(i, (i + distance) % count) for i in range(count) if wrap or 0 <= i + distance < count]
    return lax.ppermute(block, axis, route)


def swapped(block):
    count = lax.axis_size("mp")
    return lax.ppermute(block, "mp", [(i, count - 1 - i) for i in range(count)])


def over_mp(own, other):
    return (own.astype(full) + swapped(other).astype(full)).astype(low)


def over_dp(both):
    owners, place = lax.axis_size("dp"), lax.axis_index("dp")
    count = both.shape[0] // owners
    total = lax.dynamic_slice_in_dim(both, place * count, count, 0).astype(full)
    for distance in range(1, owners):
        share = lax.dynamic_slice_in_dim(both, (place + distance) % owners * count, count, 0)
        total = total + moved(share, "dp", distance, True).astype(full)
    return total.astype(low)


def over_seq(total):
    result = total.astype(full)
    for distance in range(1, lax.axis_size("seq")):
        result = result + moved(total, "seq", distance, True).astype(full)
    return result


def adamw_update(param_now, gradient, moment_now, square_now, scale_factor):
    gradient = gradient * scale_factor
    first_mom = beta_one * moment_now + (1.0 - beta_one) * gradient
    second_mom = beta_two * square_now + (1.0 - beta_two) * gradient * gradient
    update = (
        first_mom
        / (1.0 - beta_one**STEP)
        / (jnp.sqrt(second_mom / (1.0 - beta_two**STEP)) + adam_eps)
    )
    param_new = param_now - learn_rate * (update + weight_decay * param_now)
    return (param_new, first_mom, second_mom)


def rows_of(values, count=PAD):
    return jnp.concatenate([values, jnp.zeros((count - values.shape[0],) + values.shape[1:], values.dtype)], axis=0)


def per_device(
    tokens,
    output_cotangent,
    document_numbers,
    document_adapter,
    input_norm_gain,
    gate_head_projection,
    map_projection,
    step_projection,
    output_projection,
    head_conv_taps,
    map_conv_taps,
    head_settings,
    gated_norm_gain,
    adapter_broad,
    adapter_step,
    adapter_shared,
    broad_first_moment,
    step_first_moment,
    shared_first_moment,
    broad_second_moment,
    step_second_moment,
    shared_second_moment,
):
    halves = lax.axis_size("mp")
    pieces = lax.axis_size("seq")
    owners = lax.axis_size("dp")
    core = lax.axis_index("mp")
    place = lax.axis_index("seq")
    length, width = tokens.shape[2:]
    layers, _, _, half = gate_head_projection.shape
    inner = halves * half
    heads_local = head_settings.shape[2]
    heads = halves * heads_local
    head_width = inner // heads
    own_adapters, rank = adapter_broad.shape[1:3]
    own_rows = own_adapters * rank
    adapters = own_adapters * owners
    ranks = adapters * rank
    part = width // halves
    states = map_projection.shape[2] // 2
    channels = inner + 2 * states

    def mine(values):
        return lax.dynamic_index_in_dim(values, core, 0, False)

    h_first = mine(tokens)[0]
    documents = mine(document_numbers)[0]
    chosen = mine(document_adapter)[0]

    low_broad = adapter_broad.astype(low)
    low_step = adapter_step.astype(low)
    low_shared = adapter_shared.astype(low)
    rows_own = gate_head_projection.shape[1]
    packs = Packs(rows_own, own_rows, half, part)
    spots = jnp.stack([lax.axis_index("dp"), place]).astype(jnp.int32)
    core_in = jnp.full((1,), core, jnp.int32)

    def twice(values):
        room = jnp.zeros(values.shape[:-1] + (LANES - 2 * values.shape[-1],), values.dtype)
        return jnp.concatenate([values, values, room], axis=-1)

    def packed(layer):
        zx = gate_head_projection[layer]
        broad = low_broad[layer].reshape(own_rows, 3, half)
        shared = low_shared[layer].reshape(own_rows, -1)
        maps = lax.dynamic_slice_in_dim(map_projection[layer], core * states, states, 1)
        maps_up = lax.dynamic_slice_in_dim(shared, width + core * states, states, 1)
        down = lax.dynamic_slice_in_dim(shared, core * part, part, 1)
        up = lax.dynamic_slice_in_dim(shared, width + 2 * states + core * part, part, 1)
        first = jnp.concatenate(
            [
                jnp.concatenate([zx[:, 1], maps, twice(step_projection[layer])], axis=1),
                jnp.concatenate([broad[:, 1], maps_up, twice(low_step[layer].reshape(own_rows, heads_local))], axis=1),
                jnp.concatenate([down, up, jnp.zeros((own_rows, half + 2 * LANES - 2 * part), low)], axis=1),
            ],
            axis=0,
        )
        second = jnp.concatenate([zx[:, 0], broad[:, 0], output_projection[layer].T, broad[:, 2]], axis=0)
        return first, second

    def ordered(values, after):
        return values if after is None else lax.optimization_barrier((values, after))[0]

    def zero_after(value):
        return value.reshape(-1)[0].astype(full) * 0.0

    def sent(pack, quartered, after):
        quarter = pack.shape[0] // pieces
        if quarter % 16 or pack.shape[0] % pieces or owners == 1 or pieces == 1:
            return ordered(pack, after), None
        if quartered:
            mine_now = lax.dynamic_slice_in_dim(pack, place * quarter, quarter, 0)
        else:
            mine_now = pack
        mine_now = ordered(mine_now, after)
        return pack, [moved(mine_now, "dp", d, True) for d in range(1, owners)]

    def passed_on(near, after):
        if near is None:
            return []
        stack = ordered(jnp.stack(near), after)
        return [moved(stack, "seq", d, True) for d in range(1, pieces)]

    def gathered(pack, near, far, after):
        if near is None:
            own = lax.all_gather(pack, "dp")
        else:
            own = kernel_call(
                functools.partial(assemble_kernel, owners, pieces),
                [shape((owners,) + pack.shape, low)],
                [spots, pack, *near, *far, *after],
                scalars=1,
                name="assemble",
                limit=20,
            )[0]
        return own, swapped(own)

    def last_of(messages, instead):
        return messages[-1] if messages else instead

    packs_of = [packed(layer) for layer in range(layers)]
    flights = {2 * layer: sent(packs_of[layer][0], True, None) for layer in range(layers)}
    first_far = passed_on(flights[0][1], None)
    over = [flights[2 * layer][1][-1][:16, :LANES] for layer in range(1, layers) if flights[2 * layer][1]]
    weights = {0: gathered(*flights[0], first_far, over)}
    next_fars = {}
    for layer in range(1, layers):
        near = flights[2 * layer][1]
        if near:
            near = [near[0] + zero_after(weights[0][0][0, :1, :1]).astype(low), *near[1:]]
        next_fars[layer] = passed_on(near, None)

    def gathered_both(pack, after):
        return lax.all_gather(ordered(pack, after), ("mp", "dp")).reshape((halves, owners) + pack.shape)

    weights[1] = gathered_both(packs_of[0][1], flights[0][1])
    wait = zero_after((first_far[0] if first_far else weights[0][0])[:1, :1, :1])

    def over_cores(values):
        return jnp.concatenate([values, swapped(values)], axis=values.ndim - 1)

    widths = over_cores(jnp.concatenate([head_conv_taps, gated_norm_gain[:, None]], axis=1)).astype(full)
    settings = over_cores(head_settings)
    widths, settings, documents = widths + wait, settings + wait, documents + wait.astype(jnp.int32)
    maps_taps = jnp.pad(map_conv_taps.astype(full), ((0, 0), (0, 1), (0, 0)))
    skips = jnp.broadcast_to(settings[:, 2:3, :, None], (layers, 1, heads, head_width)).reshape(layers, 1, inner)

    def wide_rows(values):
        return jnp.pad(values, ((0, 0), (0, 0), (0, channels - values.shape[2])))

    tables = jnp.concatenate(
        [
            jnp.concatenate([widths, maps_taps], axis=2),
            wide_rows(skips),
            wide_rows(input_norm_gain.astype(full)[:, None]),
            wide_rows(settings[:, :2]),
            jnp.zeros((layers, TABLE_ROWS - DECAY - 1, channels), full),
        ],
        axis=1,
    )
    head_of = np.arange(inner)[None, :] // head_width
    spread_one = (np.arange(LANES)[:, None] == head_of).astype(np.float32)
    spread_two = jnp.asarray(np.concatenate([spread_one, spread_one], axis=0), low)

    begin = place * length
    ends = jnp.concatenate([jnp.full((PAD,), -1, jnp.int32), documents, jnp.full((PAD,), -2, jnp.int32)])
    near = lax.dynamic_slice_in_dim(ends, begin, length + 2 * PAD)
    own = near[PAD : PAD + length]
    lane = jnp.arange(CONV * LANES)[None, :] // LANES

    def same_as(lag):
        return (own == near[PAD + lag : PAD + lag + length])[:, None]

    front = jnp.where(same_as(-1), 0.0, RESET)
    leads = same_as(CONV - 1)
    for lag in range(1, CONV):
        front = jnp.where(lane == lag - 1, jnp.where(same_as(-lag), 1.0, 0.0), front)
    for lag in range(1, CONV - 1):
        leads = jnp.where(lane[:, : -LANES] == lag - 1, same_as(lag), leads)
    front, leads = front.astype(low), leads.astype(low)
    which = jnp.arange(ranks)[None, :] // rank
    mask = jnp.zeros((length, ranks), jnp.bool_)
    for document in range(chosen.shape[0]):
        mask = mask | ((own == document)[:, None] & (which == chosen[document]))
    mask = mask.astype(low)

    flops_in = 2 * length * width * (2 * inner + 3 * LANES)
    flops_out = 2 * length * width * inner
    flops_scan = 4 * length * SPAN * inner

    h = h_first
    kept = []
    for layer in range(layers):
        first_own, first_other = weights[2 * layer]
        normed, spread, rows, dt_raw = kernel_call(
            functools.partial(project_rows_kernel, packs, heads_local, layer),
            [
                shape((length, width), low),
                shape((length, ranks), low),
                shape((length, channels), low),
                shape((length, LANES), full),
            ],
            [core_in, h, tables, mask, first_own, first_other],
            scalars=1,
            flops=flops_in // 2,
            name="project_rows",
        )
        halo = moved(rows[length - PAD :], "seq", 1)
        reached = []
        if layer + 1 < layers:
            weights[2 * layer + 2] = gathered(*flights[2 * layer + 2], next_fars[layer + 1], [rows[:16, :LANES]])
            reached = [weights[2 * layer + 2][0][0, :16, :LANES]]
        act, slope, xdt, dt, cum, flat, begin_state, end_state = kernel_call(
            functools.partial(states_kernel, inner, layer),
            [
                shape((length, channels), low),
                shape((length, channels), low),
                shape((length, inner), low),
                shape((length, LANES), full),
                shape((length, LANES), full),
                shape((LANES, length), full),
                shape((length // SPAN, states, inner), low),
                shape((states + 16, inner), low),
            ],
            [rows, halo, tables, front, dt_raw, spread_two, *reached],
            scratch=[pltpu.VMEM((length + PAD, channels), full), pltpu.VMEM((states, inner), full)],
            flops=flops_scan,
            name="states",
        )
        arrived = [moved(end_state, "seq", d) for d in range(1, pieces)]
        y_local = kernel_call(
            functools.partial(intra_kernel, inner, head_width, layer),
            [shape((length, inner), low)],
            [act, xdt, cum, flat, begin_state, tables, spread_two],
            flops=flops_scan,
            name="intra",
        )[0]
        wide = weights[2 * layer + 1]
        if layer + 1 < layers:
            weights[2 * layer + 3] = gathered_both(packs_of[layer + 1][1], act)
        gate = kernel_call(
            functools.partial(project_gate_kernel, packs),
            [shape((length, inner), full)],
            [core_in, normed, spread, wide],
            scalars=1,
            flops=flops_in // 2,
            name="project_gate",
        )[0]
        h_next, y, spread_out, coming = kernel_call(
            functools.partial(output_kernel, packs, len(arrived), layer),
            [
                shape((length, width), full),
                shape((length, inner), low),
                shape((length, ranks), low),
                shape((states, inner), low),
            ],
            [core_in, h, y_local, gate, act, cum, tables, mask, first_own, first_other, wide, spread_two, *arrived],
            scratch=[pltpu.VMEM((length, inner), low)],
            scalars=1,
            flops=flops_out,
            name="output",
        )
        kept.append(
            (h, normed, spread, gate, slope, halo, dt_raw, act, xdt, dt, cum, flat,
             begin_state, y, spread_out, coming)
        )
        h = h_next
    mixed_own = h.astype(low)

    late = zero_after(kept[-1][5][:1, :1]).astype(jnp.int32)
    upstream = lax.dynamic_index_in_dim(output_cotangent, core + late, 0, False)[0]
    shares = []
    for layer in reversed(range(layers)):
        first_own, first_other = weights[2 * layer]
        wide = weights[2 * layer + 1]
        (h, normed, spread, gate, slope, halo, dt_raw, act, xdt, dt, cum, flat,
         begin_state, y, spread_out, coming) = kept[layer]
        dgate, dy, own_grad, *early = kernel_call(
            functools.partial(output_back_kernel, packs, layer),
            [
                shape((length, inner), low),
                shape((length, inner), low),
                shape((states + 16, inner), low),
                *[shape((ranks, half + part), low)] * 2,
            ],
            [core_in, upstream, y, gate, spread_out, act, cum, tables, mask, first_own, first_other, wide,
             spread_two],
            scratch=[pltpu.VMEM((length, ranks), low), pltpu.VMEM((length, width), low)],
            scalars=1,
            flops=flops_out,
            name="output_back",
        )
        arrived = [moved(own_grad, "seq", -d) for d in range(1, pieces)]
        u, db, dc = kernel_call(
            functools.partial(intra_back_kernel, inner, head_width),
            [shape((length, inner), low), shape((length, LANES), full), shape((length, LANES), full)],
            [act, xdt, dy, cum, flat],
            flops=2 * flops_scan,
            name="intra_back",
        )
        dn, dl, g_gate = kernel_call(
            functools.partial(gate_back_kernel, packs),
            [shape((length, width), full), shape((length, ranks), full), shape((halves, ranks, half), low)],
            [core_in, dgate, spread, wide],
            scalars=1,
            flops=flops_in // 2,
            name="gate_back",
        )
        reached = [share[:PAD, :LANES] for share in shares]
        dconv, ddt = kernel_call(
            functools.partial(scan_back_kernel, inner, len(arrived), layer),
            [shape((length, channels), low), shape((length, LANES), low)],
            [slope, tables, act, xdt, dy, y, u, db, dc, dt, cum, dt_raw, begin_state, coming,
             spread_two, *arrived, *reached],
            scratch=[pltpu.VMEM((states, inner), full)],
            flops=2 * flops_scan,
            name="scan_back",
        )
        after = moved(dconv[:PAD], "seq", -1)
        shares = [over_dp(share) for share in shares]
        reached = [share[:PAD, :LANES] for share in shares]
        dh, *grads = kernel_call(
            functools.partial(project_back_kernel, packs, heads_local, layer),
            [
                shape((length, width), full if layer > 0 else low),
                *[shape((ranks, 2 * half + 2 * LANES + part + sum(e.shape[1] for e in early[:1])), low)] * 2,
            ],
            [core_in, upstream, h, tables, mask, dconv, after, leads, ddt, dn, dl, spread, normed, first_own,
             first_other, g_gate, *early, *reached],
            scratch=[
                pltpu.VMEM((length + PAD, channels), full),
                pltpu.VMEM((length, channels), low),
                pltpu.VMEM((length, width), full),
            ],
            scalars=1,
            flops=flops_in // 2,
            name="project_back",
        )
        upstream = dh
        shares.append(over_mp(*grads))

    behind = [over_seq(share) for share in shares[:-1]]
    whole = jnp.stack([over_seq(ordered(over_dp(shares[-1]), behind)), *reversed(behind)])
    zx, maps, steps, down_in, down_out, up_out = jnp.split(
        whole,
        [2 * half, 2 * half + LANES, 2 * half + 2 * LANES, 2 * half + 2 * LANES + part, 3 * half + 2 * LANES + part],
        axis=2,
    )
    own_shared = jnp.concatenate([maps, down_in, up_out], axis=2)
    other_shared = swapped(own_shared)
    in_order = [jnp.where(core == m, own_shared, other_shared) for m in range(halves)]
    maps, down_in, up_out = (
        [entry[:, :, first:last] for entry in in_order]
        for first, last in ((0, LANES), (LANES, LANES + part), (LANES + part, LANES + 2 * part))
    )
    shared_gradient = jnp.concatenate([*down_in, *maps, *up_out], axis=2).reshape(adapter_shared.shape)
    broad_gradient = jnp.concatenate([zx, down_out], axis=2).reshape(adapter_broad.shape)
    step_gradient = steps[:, :, :heads_local].reshape(adapter_step.shape)
    local_sq = (
        jnp.sum(broad_gradient * broad_gradient)
        + jnp.sum(step_gradient * step_gradient)
        + jnp.sum(own_shared * own_shared)
    )
    squares = jnp.broadcast_to(local_sq, (8, LANES))
    squares = squares + swapped(squares)
    total_sq = squares
    for distance in range(1, owners):
        total_sq = total_sq + moved(squares, "dp", distance, True)
    grad_norm = jnp.sqrt(total_sq[0, 0])
    scale_factor = clip_max / jnp.maximum(grad_norm, clip_max)
    revised_broad, fresh_first_broad, fresh_square_broad = adamw_update(
        adapter_broad, broad_gradient, broad_first_moment, broad_second_moment, scale_factor
    )
    revised_step, fresh_first_step, fresh_square_step = adamw_update(
        adapter_step, step_gradient, step_first_moment, step_second_moment, scale_factor
    )
    revised_shared, fresh_first_shared, fresh_square_shared = adamw_update(
        adapter_shared, shared_gradient, shared_first_moment, shared_second_moment, scale_factor
    )

    def both(values):
        other = swapped(values)
        return jnp.stack([jnp.where(core == m, values, other) for m in range(halves)])[:, None]

    return (
        both(mixed_own),
        both(upstream),
        grad_norm,
        revised_broad,
        revised_step,
        revised_shared,
        fresh_first_broad,
        fresh_first_step,
        fresh_first_shared,
        fresh_square_broad,
        fresh_square_step,
        fresh_square_shared,
        revised_broad.astype(low),
        revised_step.astype(low),
        revised_shared.astype(low),
    )


def solution(mesh):
    placed = (
        P(None, "dp", "seq", None),
        P(None, "dp", "seq", None),
        P(None, "dp", None),
        P(None, "dp", None),
        P(),
        P(None, "dp", None, "mp"),
        P(None, "dp", None),
        P(None, "dp", "mp"),
        P(None, "mp", "dp"),
        P(None, None, "mp"),
        P(),
        P(None, None, "mp"),
        P(None, "mp"),
        P(None, "dp", None, None, "mp"),
        P(None, "dp", None, "mp"),
        P(None, "dp", None, None),
        P(None, "dp", None, None, "mp"),
        P(None, "dp", None, "mp"),
        P(None, "dp", None, None),
        P(None, "dp", None, None, "mp"),
        P(None, "dp", None, "mp"),
        P(None, "dp", None, None),
    )
    return jax.shard_map(
        per_device,
        mesh=mesh,
        in_specs=placed,
        out_specs=(
            P(None, "dp", "seq", None),
            P(None, "dp", "seq", None),
            P(),
            P(None, "dp", None, None, "mp"),
            P(None, "dp", None, "mp"),
            P(None, "dp", None, None),
            P(None, "dp", None, None, "mp"),
            P(None, "dp", None, "mp"),
            P(None, "dp", None, None),
            P(None, "dp", None, None, "mp"),
            P(None, "dp", None, "mp"),
            P(None, "dp", None, None),
            P(None, "dp", None, None, "mp"),
            P(None, "dp", None, "mp"),
            P(None, "dp", None, None),
        ),
        check_vma=False,
    )
```
